128 devices in a mesh: freq: 4 (over x), bl: 32 (over z, y, core).
Axes of the slice: x: 4, y: 4, z: 4, core: 2. Of those that a mesh axis runs over, the one named last changes fastest.
Arguments:
- visibilities: float32 [2, 2, 256, 16384], P(None, None, 'freq', 'bl'), may hold values from -6 to 6
- model: bfloat16 [2, 16, 2, 256, 16384], P(None, None, None, 'freq', 'bl'), may hold values from -1.5 to 1.5
- pairs: int32 [2, 16384, 2], P(None, 'bl'), may hold values from 0 to 511, as said below
- uv: float32 [2, 2, 16384], P(None, None, 'bl'), may hold values from -8 to 8
- held_gains: float32 [32, 2, 2, 16, 512], P('bl'), may hold values from -0.5 to 1.5
- solver_owner: int32 [2], replicated, may hold values from 0 to 31
- facet_owner: int32 [2, 4, 4096, 1], P(None, 'freq', 'bl'), may hold values from 0 to 127; in each aligned block of 128 rows (0 to 127, 128 to 255, ..., all dimensions but the last counted through in order) at most 2 rows name the same one
- subgrid_pos: int32 [2, 4, 4096, 2], P(None, 'freq', 'bl'), may hold values from 0 to 32
Outputs:
- solved_gains: float32 [2, 2, 16, 512], replicated
- residual_facets: float32 [4, 32, 2, 64, 64], P('freq', 'bl')
The draws below stay inside these ranges and needn't reach their ends.
Inputs may be any that keep to these rules, and one draw needn't show every extreme that they name: `pairs`: every station is the first station of some row in each interval. `facet_owner`: in each interval, at most 2 of the 128 subgrids of one device name the same facet owner.
All inputs are finite; a program needn't handle non-finite values.
Results may differ from the reference program's by a relative error of at most 0.0003.
Values sent between devices are 32-bit elements; how exact they have to be, the bound alone decides.
A program may use at most 192 MiB of HBM per device.

```python
import math
import jax
import jax.numpy as jnp
import numpy as np
from jax import lax

STATIONS = 512
DIRS = 16
CH_DEV = 64
CHANNELS = 256
SG = 32
FACET = 64
RPS = 4
ROWS = 512
ROWS_ALL = 16384
NSUB = 128
CAP = 2
ITERS = 4
INTERVALS = 2
N_FREQ = 4
N_BL = 32
DEVICES = 128


def draw_pairs(key, part):
    key = jax.random.fold_in(key, 7)
    rows_total = N_BL * ROWS
    row_axis = jnp.arange(rows_total, dtype=jnp.int32)
    layers = []
    for interval in range(INTERVALS):
        key_perm, key_first, key_second = jax.random.split(jax.random.fold_in(key, interval), 3)
        shuffled = jax.random.permutation(key_perm, STATIONS).astype(jnp.int32)
        random_first = jax.random.randint(key_first, (rows_total,), 0, STATIONS, dtype=jnp.int32)
        covered = shuffled[jnp.minimum(row_axis, STATIONS - 1)]
        first_station = jnp.where(row_axis < STATIONS, covered, random_first)
        second_station = jax.random.randint(key_second, (rows_total,), 0, STATIONS, dtype=jnp.int32)
        layers.append(jnp.stack([first_station, second_station], axis=1))
    return jnp.stack(layers)


def draw_held_gains(key, part):
    key = jax.random.fold_in(key, 11)
    key_real, key_imag = jax.random.split(key)
    shape = (N_BL, INTERVALS, DIRS, STATIONS)
    real_part = 1.0 + jnp.clip(0.15 * jax.random.normal(key_real, shape, jnp.float32), -0.5, 0.5)
    imag_part = jnp.clip(0.15 * jax.random.normal(key_imag, shape, jnp.float32), -0.5, 0.5)
    return jnp.stack([real_part, imag_part], axis=2)


def plant(drawn, stream_key, low, top_value):
    longest = drawn.shape.index(max(drawn.shape))
    spots = []
    for shift in (0, 1):
        where = [jax.random.randint(jax.random.fold_in(stream_key, axis), (), 0, length) for axis, length in enumerate(drawn.shape)]
        where[longest] = (where[longest] + shift) % drawn.shape[longest]
        spots.append(tuple(where))
    return drawn.at[spots[0]].set(low).at[spots[1]].set(top_value)


def shard_levels(key, shape, cuts, least, high):
    factor_of, own = 1.0, jax.random.fold_in(key, 6)
    for axis_at, shards_of in cuts:
        heights = jnp.exp(jax.random.uniform(jax.random.fold_in(own, axis_at), (shards_of,), jnp.float32, least / len(cuts), high / len(cuts)))
        factor_of = factor_of * jnp.repeat(heights, shape[axis_at] // shards_of).reshape([-1 if axis == axis_at else 1 for axis in range(len(shape))])
    return factor_of


def routed_block(stream_key, own, number, rows, count, top, bound, skew):
    sequence = jax.random.permutation(stream_key, count)
    crowded, ordinary = shares(count, rows * top, bound, skew, True), shares(count, rows * top, bound, skew, False)
    places = jnp.arange(count)

    def named(lengths, offset_by):
        used = int((lengths > 0).sum())
        fixed = max(1, used // 4)
        moved = fixed + (places - fixed + offset_by * (used - fixed)) % max(1, count - fixed)
        return jnp.zeros((count,), jnp.int32).at[sequence[jnp.where(places < fixed, places, moved)]].set(jnp.asarray(lengths, jnp.int32))

    lengths = jnp.where(number % 4 == 0, named(crowded, number // 4), named(ordinary, number - number // 4 - 1))
    mixed = jax.random.permutation(jax.random.fold_in(own, 3), count)
    giver, receiver = mixed[0:count // 2 * 2:2], mixed[1:count // 2 * 2:2]
    room = jnp.minimum(lengths[giver] - 1, bound - lengths[receiver]) // 2
    room = jnp.where((giver == sequence[0]) | (receiver == sequence[0]) | (lengths[receiver] == 0), 0, jnp.maximum(room, 0))
    moved = jax.random.randint(jax.random.fold_in(own, 4), (count // 2,), 0, 1 << 20) % (room + 1)
    lengths = lengths.at[giver].add(-moved).at[receiver].add(moved)
    items = jnp.searchsorted(jnp.cumsum(lengths), jnp.arange(rows * top), side="right").astype(jnp.int32)
    grid = items.reshape(top, rows).T
    grid = grid[jax.random.permutation(jax.random.fold_in(own, 1), rows)]
    offset_by = jax.random.randint(jax.random.fold_in(own, 2), (rows, 1), 0, top)
    return jnp.take_along_axis(grid, (jnp.arange(top)[None, :] + offset_by) % top, axis=1)


def shares(count, total, limit, skew, full):
    portions = [(1 << 20) // math.isqrt(grade ** skew) + 1 for grade in range(1, count + 1)]
    largest = limit if full else min(limit, max(-(-total // count), total * portions[0] // sum(portions)))
    least = 1 if total - largest >= count - 1 else 0
    given, rest = [largest] + [least] * (count - 1), total - largest - least * (count - 1)
    while rest > 0:
        candidates = [i for i in range(1, count) if given[i] < largest] or [i for i in range(1, count) if given[i] < limit]
        whole, remaining = sum([portions[i] for i in candidates]), rest
        for i in candidates:
            extra = min(limit - given[i], max(1, remaining * portions[i] // whole), rest)
            given[i] = given[i] + extra
            rest = rest - extra
    return np.array(given)


def scatter_about(key, shape, deviation, limit, cuts=(), kind=jnp.bfloat16):
    level = shard_levels(key, shape, cuts, -0.22, 0.18) if cuts else 1.0
    drawn = jax.random.normal(key, shape, jnp.float32) * deviation * level
    return jnp.minimum(jnp.maximum(drawn, -limit), limit).astype(kind)


def setup_inputs(seed: int = 0) -> dict:
    splits = jax.random.split(jax.random.key(seed), 9)
    visibilities = scatter_about(splits[0], (INTERVALS, 2, CHANNELS, ROWS_ALL), 1.0, 6.0, ((2, 4), (3, 32)), jnp.float32)
    model = scatter_about(splits[1], (INTERVALS, DIRS, 2, CHANNELS, ROWS_ALL), 0.25, 1.5, ((3, 4), (4, 32)))
    pairs = draw_pairs(jax.random.fold_in(splits[8], 71), 0)
    uv = jnp.clip(jax.random.uniform(splits[3], (INTERVALS, 2, ROWS_ALL), jnp.float32, -8.0, 8.0) * shard_levels(splits[3], (INTERVALS, 2, ROWS_ALL), ((2, 32),), -0.4, 0.0), -8.0, 8.0)
    held_gains = draw_held_gains(jax.random.fold_in(splits[8], 71), 0)
    solver_owner = jax.random.randint(splits[5], (INTERVALS,), 0, N_BL).astype(jnp.int32)
    facet_owner_keys = jax.random.split(jax.random.fold_in(splits[6], 1), INTERVALS * N_FREQ * (N_BL * NSUB) // NSUB)
    facet_owner_turns = jax.random.permutation(jax.random.fold_in(splits[6], 3), INTERVALS * N_FREQ * (N_BL * NSUB) // NSUB)
    facet_owner = jax.vmap(lambda own, number: routed_block(jax.random.fold_in(splits[6], 2), own, number, NSUB, DEVICES, 1, CAP, 2))(facet_owner_keys, facet_owner_turns).reshape((INTERVALS, N_FREQ, N_BL * NSUB, 1))
    subgrid_pos = plant(jax.random.randint(splits[7], (INTERVALS, N_FREQ, N_BL * NSUB, 2), 0, FACET - SG + 1), jax.random.fold_in(splits[7], 1), 0, FACET - SG).astype(jnp.int32)
    return dict(visibilities=visibilities, model=model, pairs=pairs, uv=uv, held_gains=held_gains, solver_owner=solver_owner, facet_owner=facet_owner, subgrid_pos=subgrid_pos)


damping = 0.5
highest = lax.Precision.HIGHEST

def predict(model_re, model_im, vis_re, vis_im, first_re, first_im, second_re, second_im):
    zeta_re = model_re * second_re + model_im * second_im
    zeta_im = model_im * second_re - model_re * second_im
    resid_re = vis_re - lax.optimization_barrier(jnp.sum(first_re * zeta_re - first_im * zeta_im, axis=0))
    resid_im = vis_im - lax.optimization_barrier(jnp.sum(first_re * zeta_im + first_im * zeta_re, axis=0))
    return (resid_re, resid_im, zeta_re, zeta_im)

def normal_terms(model_re, model_im, resid_re, resid_im, zeta_re, zeta_im, first_re, first_im, second_re, second_im, model_power):
    left_re = lax.optimization_barrier(jnp.sum(resid_re * zeta_re + resid_im * zeta_im, axis=1))
    left_im = lax.optimization_barrier(jnp.sum(resid_im * zeta_re - resid_re * zeta_im, axis=1))
    chi_re = model_re * first_re - model_im * first_im
    chi_im = -(model_im * first_re + model_re * first_im)
    right_re = lax.optimization_barrier(jnp.sum(resid_re * chi_re - resid_im * chi_im, axis=1))
    right_im = -lax.optimization_barrier(jnp.sum(resid_re * chi_im + resid_im * chi_re, axis=1))
    left_den = model_power * (second_re[:, 0] ** 2 + second_im[:, 0] ** 2)
    right_den = model_power * (first_re[:, 0] ** 2 + first_im[:, 0] ** 2)
    return (left_re, left_im, right_re, right_im, left_den, right_den)

def subgrid_image(resid_re, resid_im, coords, chan_start, total_channels):
    chan_count = resid_re.shape[0]
    count_sub = resid_re.shape[1] // RPS
    channel = (chan_start + jnp.arange(chan_count, dtype=jnp.int32)).astype(jnp.float32)
    scale_freq = 1.0 + 0.5 * channel / total_channels

    def regroup(values):
        return values.reshape(chan_count, count_sub, RPS).transpose(1, 0, 2).reshape(count_sub, chan_count * RPS)
    coord_u = regroup(coords[0][None, :] * scale_freq[:, None])
    coord_v = regroup(coords[1][None, :] * scale_freq[:, None])
    res_re = regroup(resid_re)
    res_im = regroup(resid_im)
    pixel_pos = (jnp.arange(SG, dtype=jnp.float32) - SG // 2) / SG
    phase_u = 2.0 * math.pi * pixel_pos[None, :, None] * coord_u[:, None, :]
    phase_v = 2.0 * math.pi * pixel_pos[None, :, None] * coord_v[:, None, :]
    ucos, usin = (jnp.cos(phase_u), jnp.sin(phase_u))
    vcos, vsin = (jnp.cos(phase_v), jnp.sin(phase_v))
    weight_re = res_re[:, None, :] * ucos - res_im[:, None, :] * usin
    weight_im = res_re[:, None, :] * usin + res_im[:, None, :] * ucos
    sub_re = jnp.einsum('jak,jbk->jab', weight_re, vcos, precision=highest) - jnp.einsum('jak,jbk->jab', weight_im, vsin, precision=highest)
    sub_im = jnp.einsum('jak,jbk->jab', weight_re, vsin, precision=highest) + jnp.einsum('jak,jbk->jab', weight_im, vcos, precision=highest)
    return jnp.stack([sub_re, sub_im], axis=1) / math.sqrt(chan_count * RPS)

def placed_each(subgrid_set, positions):
    facet_axis = jnp.arange(FACET, dtype=jnp.int32)
    offsets = jnp.arange(SG, dtype=jnp.int32)
    row_hot = (facet_axis[None, :, None] == positions[:, 0][:, None, None] + offsets[None, None, :]).astype(jnp.float32)
    col_hot = (facet_axis[None, :, None] == positions[:, 1][:, None, None] + offsets[None, None, :]).astype(jnp.float32)
    half_placed = jnp.einsum('jzab,jcb->jzac', subgrid_set, col_hot, precision=highest)
    return jnp.einsum('jxa,jzac->jzxc', row_hot, half_placed, precision=highest)

def reference(visibilities, model, pairs, uv, held_gains, solver_owner, facet_owner, subgrid_pos):
    count_sub = ROWS // RPS
    zero_index = jnp.zeros((), jnp.int32)
    facets = jnp.zeros((N_FREQ * N_BL, 2, FACET, FACET), jnp.float32)
    results = []
    for interval in range(INTERVALS):
        gain_now = held_gains[solver_owner[interval], interval].astype(jnp.float32)
        first_all = pairs[interval, :, 0]
        second_all = pairs[interval, :, 1]
        vis_now = visibilities[interval]
        model_now = model[interval]
        coords_now = uv[interval]

        def block_data(gain_used, chan_start, row_start, chan_count):
            model_blk = lax.dynamic_slice(model_now, (zero_index, zero_index, chan_start, row_start), (DIRS, 2, chan_count, ROWS)).astype(jnp.float32)
            vis_blk = lax.dynamic_slice(vis_now, (zero_index, chan_start, row_start), (2, chan_count, ROWS))
            first_idx = lax.dynamic_slice_in_dim(first_all, row_start, ROWS)
            second_idx = lax.dynamic_slice_in_dim(second_all, row_start, ROWS)
            first_gain = jnp.take(gain_used, first_idx, axis=2)
            second_gain = jnp.take(gain_used, second_idx, axis=2)
            model_re, model_im = (model_blk[:, 0], model_blk[:, 1])
            first_re, first_im = (first_gain[0][:, None, :], first_gain[1][:, None, :])
            second_re, second_im = (second_gain[0][:, None, :], second_gain[1][:, None, :])
            resid_re, resid_im, zeta_re, zeta_im = predict(model_re, model_im, vis_blk[0], vis_blk[1], first_re, first_im, second_re, second_im)
            return (model_re, model_im, resid_re, resid_im, zeta_re, zeta_im, first_re, first_im, second_re, second_im, first_idx, second_idx)
        for sweep_index in range(ITERS):

            def sums_block(block_index, totals, gain_used=gain_now):
                row_start = (block_index * ROWS).astype(jnp.int32)
                data = block_data(gain_used, zero_index, row_start, CHANNELS)
                model_re, model_im, resid_re, resid_im, zeta_re, zeta_im, first_re, first_im, second_re, second_im, first_idx, second_idx = data
                model_power = lax.optimization_barrier(jnp.sum(model_re * model_re + model_im * model_im, axis=1))
                terms = normal_terms(model_re, model_im, resid_re, resid_im, zeta_re, zeta_im, first_re, first_im, second_re, second_im, model_power)
                left_re, left_im, right_re, right_im, left_den, right_den = terms

                def gather_sum(left_val, right_val):
                    first_sum = jax.ops.segment_sum(left_val.T, first_idx, num_segments=STATIONS).T
                    second_sum = jax.ops.segment_sum(right_val.T, second_idx, num_segments=STATIONS).T
                    return first_sum + second_sum
                return (totals[0] + gather_sum(left_re, right_re), totals[1] + gather_sum(left_im, right_im), totals[2] + gather_sum(left_den, right_den))
            zero_table = jnp.zeros((DIRS, STATIONS), jnp.float32)
            num_re, num_im, den_all = lax.fori_loop(0, N_BL, sums_block, (zero_table, zero_table, zero_table))
            gain_now = gain_now + damping * jnp.stack([num_re, num_im]) / den_all
        results.append(gain_now)

        def image_block(block_index, facet_sum, gain_used=gain_now, interval_now=interval):
            group = (block_index // N_BL).astype(jnp.int32)
            local = (block_index % N_BL).astype(jnp.int32)
            chan_start = (group * CH_DEV).astype(jnp.int32)
            row_start = (local * ROWS).astype(jnp.int32)
            data = block_data(gain_used, chan_start, row_start, CH_DEV)
            coords = lax.dynamic_slice(coords_now, (zero_index, row_start), (2, ROWS))
            subgrid_set = subgrid_image(data[2], data[3], coords, chan_start, CHANNELS)
            sub_start = (local * count_sub).astype(jnp.int32)
            owners = lax.dynamic_slice(facet_owner[interval_now], (group, sub_start, zero_index), (1, count_sub, 1))[0, :, 0]
            positions = lax.dynamic_slice(subgrid_pos[interval_now], (group, sub_start, zero_index), (1, count_sub, 2))[0]
            return facet_sum.at[owners].add(placed_each(subgrid_set, positions))
        facets = lax.fori_loop(0, N_FREQ * N_BL, image_block, facets)
    facets = facets * (2.0 / math.sqrt(INTERVALS * count_sub))
    return (jnp.stack(results), facets.reshape(N_FREQ, N_BL, 2, FACET, FACET))
```

```python
import functools
import math

import jax
import jax.numpy as jnp
from jax import lax
from jax.experimental import pallas as pl
from jax.experimental.pallas import tpu as pltpu
from jax.sharding import PartitionSpec as P

SG = 32
FACET = 64
RPS = 4
ITERS = 4
INTERVALS = 2
DIRS = 16
STATIONS = 512
ROWS = 512
CH = 64
PLANE = 16
COLUMN = 8
SBLOCKS = STATIONS // 128
MESH = pl.DeviceIdType.MESH
F32 = jnp.float32
BF16 = jnp.bfloat16

damping = 0.5


def split3(x):
    hi = x.astype(BF16)
    rest = x - hi.astype(F32)
    mid = rest.astype(BF16)
    low = (rest - mid.astype(F32)).astype(BF16)
    return hi, mid, low


def solve_kernel(
    model,
    vis,
    prow,
    pcol,
    start,
    gains_out,
    mix_out,
    hot_sr,
    hot_rs,
    power,
    pairgain,
    mix,
    kterm,
    sums,
    arrived,
    partial,
    chunk,
    rs_send,
    rs_recv,
    ex_send,
    ex_recv,
    ag_send,
    ag_recv,
):
    freq = lax.axis_index("freq")
    bl = lax.axis_index("bl")
    core = lax.rem(bl, 2)
    plane = lax.div(bl, 2)
    column = freq * 2 + core

    def plane_peer(step):
        other = lax.rem(plane + step, PLANE)
        return other, (freq, other * 2 + core)

    def column_peer(step):
        other = lax.rem(column + step, COLUMN)
        return other, (lax.div(other, 2), plane * 2 + lax.rem(other, 2))

    barrier = pltpu.get_barrier_semaphore()
    for step in range(1, PLANE):
        pl.semaphore_signal(barrier, inc=1, device_id=plane_peer(step)[1], device_id_type=MESH)
    for step in range(1, COLUMN):
        pl.semaphore_signal(barrier, inc=1, device_id=column_peer(step)[1], device_id_type=MESH)
    pl.semaphore_wait(barrier, PLANE - 1 + COLUMN - 1)

    def exchange(turn, update):
        def rs_copy(step):
            other, device = plane_peer(step)
            return pltpu.make_async_remote_copy(
                src_ref=sums.at[other],
                dst_ref=arrived.at[plane],
                send_sem=rs_send.at[step],
                recv_sem=rs_recv.at[step],
                device_id=device,
                device_id_type=MESH,
            )

        for step in range(1, PLANE):
            rs_copy(step).start()
        arrived[plane] = sums[plane]
        for step in range(1, PLANE):
            rs_copy(step).wait_recv()
        total = arrived[0]
        for m in range(1, PLANE):
            total = total + arrived[m]
        par = lax.rem(turn, 2)
        partial[par, column] = total

        def ex_copy(step):
            _, device = column_peer(step)
            return pltpu.make_async_remote_copy(
                src_ref=partial.at[par, column],
                dst_ref=partial.at[par, column],
                send_sem=ex_send.at[step],
                recv_sem=ex_recv.at[par, step],
                device_id=device,
                device_id_type=MESH,
            )

        for step in range(1, COLUMN):
            ex_copy(step).start()
        for step in range(1, COLUMN):
            ex_copy(step).wait_recv()
        total = partial[par, 0]
        for m in range(1, COLUMN):
            total = total + partial[par, m]
        chunk[plane] = update(total)

        def ag_copy(step):
            _, device = plane_peer(step)
            return pltpu.make_async_remote_copy(
                src_ref=chunk.at[plane],
                dst_ref=chunk.at[plane],
                send_sem=ag_send.at[step],
                recv_sem=ag_recv.at[step],
                device_id=device,
                device_id_type=MESH,
            )

        for step in range(1, PLANE):
            ag_copy(step).start()
        for step in range(1, PLANE):
            rs_copy(step).wait_send()
        for step in range(1, COLUMN):
            ex_copy(step).wait_send()
        for step in range(1, PLANE):
            ag_copy(step).wait_recv()
        for step in range(1, PLANE):
            ag_copy(step).wait_send()

    def pack(interval, table):
        for sb in range(SBLOCKS):
            for dh in range(2):
                for q in range(3):
                    sums[interval * 8 + sb * 2 + dh, q * 8 : q * 8 + 8, :] = table[
                        q * 16 + dh * 8 : q * 16 + dh * 8 + 8, sb * 128 : sb * 128 + 128
                    ]

    for interval in range(INTERVALS):
        pack(interval, start[interval])

    def first_update(total):
        scale = 1.0 / total[16:24]
        return jnp.concatenate([total[0:8] * scale, total[8:16] * scale], axis=0)

    exchange(0, first_update)

    for interval in range(INTERVALS):
        stations = lax.broadcasted_iota(jnp.int32, (STATIONS, 2 * ROWS), 0)
        hot_sr[interval] = (stations == prow[interval]).astype(F32).astype(BF16)
        stations = lax.broadcasted_iota(jnp.int32, (2 * ROWS, STATIONS), 1)
        hot_rs[interval] = (stations == pcol[interval]).astype(F32).astype(BF16)

    def blocks(body):
        def run(index, carry):
            interval = lax.div(index, 4)
            lanes = pl.ds(pl.multiple_of(lax.rem(index, 4) * 128, 128), 128)
            body(interval, lanes)
            return carry

        lax.fori_loop(0, INTERVALS * 4, run, 0)

    def model_at(interval, d, lanes):
        return (
            model[interval, d, 0, :, lanes].astype(F32),
            model[interval, d, 1, :, lanes].astype(F32),
        )

    def power_block(interval, lanes):
        rows = []
        for d in range(DIRS):
            mre, mim = model_at(interval, d, lanes)
            rows.append(jnp.sum(mre * mre + mim * mim, axis=0, keepdims=True))
        power[interval, :, lanes] = jnp.concatenate(rows, axis=0)

    blocks(power_block)

    def gather(interval):
        rows = []
        for z in range(2):
            for dh in range(2):
                rows.append(
                    jnp.concatenate(
                        [
                            chunk[interval * 8 + sb * 2 + dh, z * 8 : z * 8 + 8, :]
                            for sb in range(SBLOCKS)
                        ],
                        axis=1,
                    )
                )
        table = jnp.concatenate(rows, axis=0)
        found = jnp.dot(
            jnp.concatenate(split3(table), axis=0),
            hot_sr[interval],
            preferred_element_type=F32,
        )
        found = found[0:32] + found[32:64] + found[64:96]
        pairgain[interval] = found
        pre, pim = found[0:16, 0:ROWS], found[16:32, 0:ROWS]
        qre, qim = found[0:16, ROWS:], found[16:32, ROWS:]
        mix[interval, 0:16] = pre * qre + pim * qim
        mix[interval, 16:32] = pim * qre - pre * qim
        return table

    def kterm_block(interval, lanes):
        rre, rim = vis[interval, 0, :, lanes], vis[interval, 1, :, lanes]
        for d in range(DIRS):
            mre, mim = model_at(interval, d, lanes)
            wre = mix[interval, d : d + 1, lanes]
            wim = mix[interval, d + 16 : d + 17, lanes]
            rre = rre - (wre * mre - wim * mim)
            rim = rim - (wre * mim + wim * mre)
        real, imag = [], []
        for d in range(DIRS):
            mre, mim = model_at(interval, d, lanes)
            real.append(jnp.sum(rre * mre + rim * mim, axis=0, keepdims=True))
            imag.append(jnp.sum(rim * mre - rre * mim, axis=0, keepdims=True))
        kterm[interval, :, lanes] = jnp.concatenate(real + imag, axis=0)

    def scatter(interval):
        found = pairgain[interval]
        pre, pim = found[0:16, 0:ROWS], found[16:32, 0:ROWS]
        qre, qim = found[0:16, ROWS:], found[16:32, ROWS:]
        kre, kim = kterm[interval, 0:16], kterm[interval, 16:32]
        power_now = power[interval]
        left = jnp.concatenate(
            [qre * kre - qim * kim, qre * kim + qim * kre, power_now * (qre * qre + qim * qim)],
            axis=0,
        )
        right = jnp.concatenate(
            [pre * kre + pim * kim, pim * kre - pre * kim, power_now * (pre * pre + pim * pim)],
            axis=0,
        )
        terms = jnp.concatenate([left, right], axis=1)
        table = jnp.dot(
            jnp.concatenate(split3(terms), axis=0), hot_rs[interval], preferred_element_type=F32
        )
        pack(interval, table[0:48] + table[48:96] + table[96:144])

    def update(total):
        scale = damping / total[16:24]
        return chunk[plane] + jnp.concatenate([total[0:8] * scale, total[8:16] * scale], axis=0)

    def iterate(turn, carry):
        for interval in range(INTERVALS):
            gather(interval)
        blocks(kterm_block)
        for interval in range(INTERVALS):
            scatter(interval)
        exchange(turn, update)
        return carry

    lax.fori_loop(1, ITERS + 1, iterate, 0)
    for interval in range(INTERVALS):
        gains_out[interval] = gather(interval)
        mix_out[interval] = mix[interval]


def solve(model, visibilities, pairs, held, owner):
    bl = lax.axis_index("bl")
    freq = lax.axis_index("freq")
    mine = jnp.logical_and(owner == bl, freq == 0)
    masked = jnp.where(mine[:, None, None, None], held, 0.0).reshape(INTERVALS, 32, STATIONS)
    ones = jnp.broadcast_to(mine.astype(F32)[:, None, None], (INTERVALS, 16, STATIONS))
    start = jnp.concatenate([masked, ones], axis=1)
    prow = pairs.transpose(0, 2, 1).reshape(INTERVALS, 1, 2 * ROWS)
    pcol = prow.reshape(INTERVALS, 2 * ROWS, 1)
    vmem = pl.BlockSpec(memory_space=pltpu.VMEM)
    return pl.pallas_call(
        solve_kernel,
        out_shape=(
            jax.ShapeDtypeStruct((INTERVALS, 32, STATIONS), F32),
            jax.ShapeDtypeStruct((INTERVALS, 32, ROWS), F32),
        ),
        in_specs=[vmem] * 5,
        out_specs=(vmem, vmem),
        scratch_shapes=[
            pltpu.VMEM((INTERVALS, STATIONS, 2 * ROWS), BF16),
            pltpu.VMEM((INTERVALS, 2 * ROWS, STATIONS), BF16),
            pltpu.VMEM((INTERVALS, 16, ROWS), F32),
            pltpu.VMEM((INTERVALS, 32, 2 * ROWS), F32),
            pltpu.VMEM((INTERVALS, 32, ROWS), F32),
            pltpu.VMEM((INTERVALS, 32, ROWS), F32),
            pltpu.VMEM((PLANE, 24, 128), F32),
            pltpu.VMEM((PLANE, 24, 128), F32),
            pltpu.VMEM((2, COLUMN, 24, 128), F32),
            pltpu.VMEM((PLANE, 16, 128), F32),
            pltpu.SemaphoreType.DMA((PLANE,)),
            pltpu.SemaphoreType.DMA((PLANE,)),
            pltpu.SemaphoreType.DMA((COLUMN,)),
            pltpu.SemaphoreType.DMA((2, COLUMN)),
            pltpu.SemaphoreType.DMA((PLANE,)),
            pltpu.SemaphoreType.DMA((PLANE,)),
        ],
        compiler_params=pltpu.CompilerParams(
            collective_id=0, has_side_effects=True, vmem_limit_bytes=48 * 1024 * 1024
        ),
        name="solve",
    )(model, visibilities, prow, pcol, start)


GROUP = 16
HALVES = 2
NSUB = ROWS // RPS


def sincos(x):
    y = x * x
    s = jnp.full_like(x, 1.0 / math.factorial(17))
    c = jnp.full_like(x, 1.0 / math.factorial(16))
    for n in range(7, -1, -1):
        s = s * y + (-1) ** n / math.factorial(2 * n + 1)
        c = c * y + (-1) ** n / math.factorial(2 * n)
    return c, s * x


def powers(c, s):
    table = {1: (c, s)}
    for n in range(2, SG // 2 + 1):
        (ca, sa), (cb, sb) = table[n // 2], table[n - n // 2]
        table[n] = (ca * cb - sa * sb, ca * sb + sa * cb)
    return table


def image_kernel(
    owner, place, model, vis, mix, coords, factor, facets, turned, resid, base, left, right
):
    half = SG // 2

    def clear(index, carry):
        facets[index] = jnp.zeros((FACET, 128), F32)
        return carry

    lax.fori_loop(0, facets.shape[0], clear, 0)
    lane = lax.broadcasted_iota(jnp.int32, (1, 128), 1)
    low = lane < 64

    def residual_block(index, carry):
        interval = lax.div(index, 4)
        start = pl.multiple_of(lax.rem(index, 4) * 128, 128)
        lanes = pl.ds(start, 128)
        rre, rim = vis[interval, 0, :, lanes], vis[interval, 1, :, lanes]
        for d in range(DIRS):
            mre = model[interval, d, 0, :, lanes].astype(F32)
            mim = model[interval, d, 1, :, lanes].astype(F32)
            wre = mix[interval, d : d + 1, lanes]
            wim = mix[interval, d + 16 : d + 17, lanes]
            rre = rre - (wre * mre - wim * mim)
            rim = rim - (wre * mim + wim * mre)
        turned[pl.ds(start, 128), :] = jnp.concatenate([rre, rim], axis=0).T
        return carry

    def group(index, carry):
        interval = lax.div(index, NSUB // GROUP)
        first = pl.multiple_of(lax.rem(index, NSUB // GROUP) * GROUP, GROUP)
        rows = pl.ds(first, GROUP)
        re = jnp.concatenate([resid[0, h, rows, :] for h in range(HALVES)], axis=1)
        im = jnp.concatenate([resid[1, h, rows, :] for h in range(HALVES)], axis=1)

        def angles(which):
            c = jnp.concatenate([base[2 * which, h, rows, :] for h in range(HALVES)], axis=1)
            s = jnp.concatenate([base[2 * which + 1, h, rows, :] for h in range(HALVES)], axis=1)
            return powers(c, s)

        def put(table, part, pixel, value):
            for h in range(HALVES):
                table[h, pl.ds(part * SG + pixel, GROUP, stride=2 * SG), :] = value[
                    :, h * 128 : h * 128 + 128
                ]

        put(left, 0, half, re)
        put(left, 1, half, im)
        for n, (c, s) in angles(0).items():
            rc, rs, ic, js = re * c, re * s, im * c, im * s
            if n < half:
                put(left, 0, half + n, rc - js)
                put(left, 1, half + n, rs + ic)
            put(left, 0, half - n, rc + js)
            put(left, 1, half - n, ic - rs)
        put(right, 0, half, jnp.ones_like(re))
        put(right, 1, half, jnp.zeros_like(re))
        for n, (c, s) in angles(1).items():
            if n < half:
                put(right, 0, half + n, c)
                put(right, 1, half + n, s)
            put(right, 0, half - n, c)
            put(right, 1, half - n, -s)
        sign = jnp.where(low, -1.0, 1.0)
        inside = lax.rem(lane, 64) < SG
        for j in range(GROUP):
            span = slice(j * 2 * SG, (j + 1) * 2 * SG)
            lhs = jnp.concatenate([left[h, span, :] for h in range(HALVES)], axis=1)
            rhs = jnp.concatenate([right[h, span, :] for h in range(HALVES)], axis=1)
            lhs_hi, rhs_hi = lhs.astype(BF16), rhs.astype(BF16)
            lhs_lo = (lhs - lhs_hi.astype(F32)).astype(BF16)
            rhs_lo = (rhs - rhs_hi.astype(F32)).astype(BF16)
            both = lax.dot_general(
                jnp.concatenate([lhs_hi, lhs_lo], axis=0),
                jnp.concatenate([rhs_hi[0:SG], rhs_lo[0:SG], rhs_hi[SG:], rhs_lo[SG:]], axis=0),
                (((1,), (1,)), ((), ())),
                preferred_element_type=F32,
            )
            real = both[0:SG] + both[2 * SG : 3 * SG]
            imag = both[SG : 2 * SG] + both[3 * SG :]
            image = real + sign * pltpu.roll(imag, 64, axis=1)
            image = image + pltpu.roll(image, 128 - SG, axis=1)
            image = jnp.where(inside, image, 0.0)
            at = owner[interval, first + j]
            across = place[interval, 1, first + j]
            down = place[interval, 0, first + j]
            image = pltpu.roll(image, across, axis=1)
            facets[at, pl.ds(down, SG), :] += image
        return carry

    for interval in range(INTERVALS):
        lax.fori_loop(interval * 4, interval * 4 + 4, residual_block, 0)
        scale = 2.0 / (math.sqrt(INTERVALS * NSUB) * math.sqrt(CH * RPS))
        for h in range(HALVES):
            one = turned[pl.ds(2 * h, NSUB, stride=RPS), :] * scale
            two = turned[pl.ds(2 * h + 1, NSUB, stride=RPS), :] * scale
            resid[0, h] = jnp.where(low, one, pltpu.roll(two, 64, axis=1))
            resid[1, h] = jnp.where(low, pltpu.roll(one, 64, axis=1), two)
            for which in range(2):
                at = which * RPS + 2 * h
                coord = jnp.where(
                    low, coords[interval, :, at : at + 1], coords[interval, :, at + 1 : at + 2]
                )
                c, s = sincos(coord * factor[...] * (2.0 * math.pi / SG))
                base[2 * which, h] = c
                base[2 * which + 1, h] = s
        per = NSUB // GROUP
        lax.fori_loop(interval * per, interval * per + per, group, 0)


def local_facets(model, visibilities, mix, uv, owner, place):
    devices = lax.axis_size("freq") * lax.axis_size("bl")
    channel = lax.axis_index("freq") * CH + jnp.arange(CH, dtype=jnp.int32)
    factor = 1.0 + 0.5 * channel.astype(F32) / (lax.axis_size("freq") * CH)
    factor = jnp.concatenate([factor, factor])[None, :]
    coords = uv.reshape(INTERVALS, 2, NSUB, RPS).transpose(0, 2, 1, 3).reshape(INTERVALS, NSUB, 8)
    owner = owner[:, 0, :, 0]
    owner = (owner % 2) * (devices // 2) + owner // 2
    place = place[:, 0].transpose(0, 2, 1)
    vmem = pl.BlockSpec(memory_space=pltpu.VMEM)
    smem = pl.BlockSpec(memory_space=pltpu.SMEM)
    return pl.pallas_call(
        image_kernel,
        out_shape=jax.ShapeDtypeStruct((devices, FACET, 128), F32),
        in_specs=[smem, smem, vmem, vmem, vmem, vmem, vmem],
        out_specs=vmem,
        scratch_shapes=[
            pltpu.VMEM((ROWS, 128), F32),
            pltpu.VMEM((2, HALVES, NSUB, 128), F32),
            pltpu.VMEM((4, HALVES, NSUB, 128), F32),
            pltpu.VMEM((HALVES, GROUP * 2 * SG, 128), F32),
            pltpu.VMEM((HALVES, GROUP * 2 * SG, 128), F32),
        ],
        compiler_params=pltpu.CompilerParams(vmem_limit_bytes=48 * 1024 * 1024),
        name="image",
    )(owner, place, model, visibilities, mix, coords, factor)


PARTS = ((0, 24, (0, 1, 2)), (24, 24, (1, 2, 0)), (48, 16, (2, 0, 1)))


def collect_kernel(facets, out, *scratch):
    sibling, one, two, three, s1, s2, s3 = (scratch[3 * n : 3 * n + 3] for n in range(7))
    core_send, core_recv, send, recv = scratch[21:]
    freq = lax.axis_index("freq")
    bl = lax.axis_index("bl")
    core = lax.rem(bl, 2)
    here = (freq, lax.div(bl, 8), lax.rem(lax.div(bl, 2), 4))

    def device(at, core):
        return (at[0], at[1] * 8 + at[2] * 2 + core)

    def peer(axis, step):
        other = lax.rem(here[axis] + step, 4)
        at = list(here)
        at[axis] = other
        return other, device(at, core)

    barrier = pltpu.get_barrier_semaphore()
    pl.semaphore_signal(barrier, inc=1, device_id=device(here, 1 - core), device_id_type=MESH)
    for axis in range(3):
        for step in range(1, 4):
            pl.semaphore_signal(barrier, inc=1, device_id=peer(axis, step)[1], device_id_type=MESH)
    pl.semaphore_wait(barrier, 10)

    def core_copy(p):
        first, rows, _ = PARTS[p]
        return pltpu.make_async_remote_copy(
            src_ref=facets.at[1 - core, :, :, :, pl.ds(first, rows), :],
            dst_ref=sibling[p],
            send_sem=core_send.at[p],
            recv_sem=core_recv.at[p],
            device_id=device(here, 1 - core),
            device_id_type=MESH,
        )

    def stage_copy(stage, p, step):
        axis = PARTS[p][2][stage]
        other, target = peer(axis, step)
        source, into = ((one, s1), (two, s2), (three, s3))[stage]
        return pltpu.make_async_remote_copy(
            src_ref=source[p].at[other],
            dst_ref=into[p].at[step - 1],
            send_sem=send.at[stage, p, step],
            recv_sem=recv.at[stage, p, step],
            device_id=target,
            device_id_type=MESH,
        )

    for p in range(3):
        core_copy(p).start()
    for p in range(3):
        first, rows, order = PARTS[p]
        core_copy(p).wait_recv()

        def add(index, carry, p=p, first=first, rows=rows, order=order):
            at = (lax.div(index, 16), lax.rem(lax.div(index, 4), 4), lax.rem(index, 4))
            i, j, k = (at[axis] for axis in order)
            one[p][i, j, k] = (
                facets[core, at[0], at[1], at[2], pl.ds(first, rows), :]
                + sibling[p][at[0], at[1], at[2]]
            )
            return carry

        lax.fori_loop(0, 64, add, 0, unroll=4)
        for step in range(1, 4):
            stage_copy(0, p, step).start()
    for stage in range(3):
        source, into = ((one, s1), (two, s2), (three, s3))[stage]
        for p in range(3):
            first, rows, order = PARTS[p]
            mine = here[order[stage]]
            for step in range(1, 4):
                stage_copy(stage, p, step).wait_recv()
            total = source[p][mine] + into[p][0] + into[p][1] + into[p][2]
            if stage < 2:
                (two, three)[stage][p][...] = total
                for step in range(1, 4):
                    stage_copy(stage + 1, p, step).start()
            else:
                out[first : first + rows, :] = total
    for p in range(3):
        core_copy(p).wait_send()
        for stage in range(3):
            for step in range(1, 4):
                stage_copy(stage, p, step).wait_send()


def collect(facets):
    vmem = pl.BlockSpec(memory_space=pltpu.VMEM)
    leads = ((4, 4, 4), (4, 4, 4), (4, 4), (4,), (3, 4, 4), (3, 4), (3,))
    return pl.pallas_call(
        collect_kernel,
        out_shape=jax.ShapeDtypeStruct((FACET, 128), F32),
        in_specs=[vmem],
        out_specs=vmem,
        scratch_shapes=[
            pltpu.VMEM(lead + (rows, 128), F32) for lead in leads for _, rows, _ in PARTS
        ]
        + [
            pltpu.SemaphoreType.DMA((3,)),
            pltpu.SemaphoreType.DMA((3,)),
            pltpu.SemaphoreType.DMA((3, 3, 4)),
            pltpu.SemaphoreType.DMA((3, 3, 4)),
        ],
        compiler_params=pltpu.CompilerParams(
            collective_id=1, has_side_effects=True, vmem_limit_bytes=32 * 1024 * 1024
        ),
        name="collect",
    )(facets.reshape(2, 4, 4, 4, FACET, 128))


def body(visibilities, model, pairs, uv, held_gains, solver_owner, facet_owner, subgrid_pos):
    gains, mix = solve(model, visibilities, pairs, held_gains[0], solver_owner)
    facets = local_facets(model, visibilities, mix, uv, facet_owner, subgrid_pos)
    facet = collect(facets)
    facet = facet.reshape(FACET, 2, FACET).transpose(1, 0, 2)
    return (gains.reshape(INTERVALS, 2, DIRS, STATIONS), facet[None, None])


def solution(mesh):
    placed = (
        P(None, None, "freq", "bl"),
        P(None, None, None, "freq", "bl"),
        P(None, "bl", None),
        P(None, None, "bl"),
        P("bl", None, None, None, None),
        P(),
        P(None, "freq", "bl", None),
        P(None, "freq", "bl", None),
    )
    return jax.shard_map(
        body,
        mesh=mesh,
        in_specs=placed,
        out_specs=(P(), P("freq", "bl", None, None, None)),
        check_vma=False,
    )
```

```python
import functools
import math

import jax
import jax.numpy as jnp
from jax import lax
from jax.experimental import pallas as pl
from jax.experimental.pallas import tpu as pltpu
from jax.sharding import PartitionSpec as P

SG = 32
FACET = 64
RPS = 4
ITERS = 4
INTERVALS = 2
DIRS = 16
STATIONS = 512
ROWS = 512
CH = 64
PLANE = 16
COLUMN = 8
SBLOCKS = STATIONS // 128
MESH = pl.DeviceIdType.MESH
F32 = jnp.float32
BF16 = jnp.bfloat16

damping = 0.5


def split3(x):
    hi = x.astype(BF16)
    rest = x - hi.astype(F32)
    mid = rest.astype(BF16)
    low = (rest - mid.astype(F32)).astype(BF16)
    return hi, mid, low


def spread(sizes):
    steps = [(i, j) for i in range(sizes[0]) for j in range(sizes[1]) if i or j]
    return sorted(steps, key=lambda t: -sum(min(k, n - k) for k, n in zip(t, sizes)))


PLANE_STEPS = spread((4, 4))
COLUMN_STEPS = spread((4, 2))


def solve_kernel(
    owner,
    model_far,
    vis_far,
    prow,
    held,
    gains_out,
    mix_out,
    model,
    vis,
    hot,
    power,
    bterm,
    gram,
    kterm,
    pairgain,
    mix,
    sums,
    arrived,
    partial,
    chunk,
    rs_send,
    rs_recv,
    ex_send,
    ex_recv,
    ag_send,
    ag_recv,
    loaded,
):
    def load(interval, which):
        far, into = ((model_far, model), (vis_far, vis))[which]
        return pltpu.make_async_copy(
            far.at[interval], into.at[interval], loaded.at[interval, which]
        )

    for interval in range(INTERVALS):
        for which in range(2):
            load(interval, which).start()
    freq = lax.axis_index("freq")
    bl = lax.axis_index("bl")
    core = lax.rem(bl, 2)
    plane = lax.div(bl, 2)
    column = freq * 2 + core

    def plane_peer(steps):
        first = lax.rem(lax.div(plane, 4) + steps[0], 4)
        second = lax.rem(lax.rem(plane, 4) + steps[1], 4)
        other = first * 4 + second
        return other, (freq, other * 2 + core)

    def column_peer(steps):
        first = lax.rem(freq + steps[0], 4)
        second = lax.rem(core + steps[1], 2)
        return first * 2 + second, (first, plane * 2 + second)

    barrier = pltpu.get_barrier_semaphore()
    for steps in PLANE_STEPS:
        pl.semaphore_signal(barrier, inc=1, device_id=plane_peer(steps)[1], device_id_type=MESH)
    for steps in COLUMN_STEPS:
        pl.semaphore_signal(barrier, inc=1, device_id=column_peer(steps)[1], device_id_type=MESH)
    pl.semaphore_wait(barrier, PLANE - 1 + COLUMN - 1)

    def exchange(turn, update, column_steps, during_sums, during_gains):
        par = lax.rem(turn, 2)
        reach = len(column_steps)

        def remote(source, into, send, recv, device):
            return pltpu.make_async_remote_copy(
                src_ref=source,
                dst_ref=into,
                send_sem=send,
                recv_sem=recv,
                device_id=device,
                device_id_type=MESH,
            )

        near = plane_peer(PLANE_STEPS[0])[1]
        beside = column_peer(column_steps[0])[1]
        rs_all = remote(sums.at[pl.ds(0, PLANE - 1)], arrived, rs_send, rs_recv, near)
        ex_all = remote(
            partial.at[par, pl.ds(0, reach)],
            partial.at[par, pl.ds(0, reach)],
            ex_send,
            ex_recv.at[par],
            beside,
        )
        ag_all = remote(
            chunk.at[pl.ds(0, PLANE - 1)], chunk.at[pl.ds(0, PLANE - 1)], ag_send, ag_recv, near
        )
        for k, steps in enumerate(PLANE_STEPS):
            other, device = plane_peer(steps)
            remote(sums.at[other], arrived.at[k], rs_send, rs_recv, device).start()
        during_sums()
        rs_all.wait_recv()
        total = sums[plane]
        for k in range(PLANE - 1):
            total = total + arrived[k]
        partial[par, column] = total
        for steps in column_steps:
            _, device = column_peer(steps)
            mine = partial.at[par, column]
            remote(mine, mine, ex_send, ex_recv.at[par], device).start()
        rs_all.wait_send()
        ex_all.wait_recv()
        if reach == COLUMN - 1:
            total = partial[par, 0]
            for m in range(1, COLUMN):
                total = total + partial[par, m]
        else:
            total = partial[par, freq * 2] + partial[par, freq * 2 + 1]
        chunk[plane] = update(total)
        for steps in PLANE_STEPS:
            _, device = plane_peer(steps)
            mine = chunk.at[plane]
            remote(mine, mine, ag_send, ag_recv, device).start()
        during_gains()
        ex_all.wait_send()
        ag_all.wait_recv()
        ag_all.wait_send()

    def pack(interval, table):
        for sb in range(SBLOCKS):
            for dh in range(2):
                for q in range(3):
                    sums[interval * 8 + sb * 2 + dh, q * 8 : q * 8 + 8, :] = table[
                        q * 16 + dh * 8 : q * 16 + dh * 8 + 8, sb * 128 : sb * 128 + 128
                    ]

    for interval in range(INTERVALS):
        mine = (owner[interval] == bl).astype(F32)
        pack(
            interval,
            jnp.concatenate([held[interval] * mine, jnp.full((DIRS, STATIONS), mine)], axis=0),
        )

    def first_update(total):
        scale = 1.0 / total[16:24]
        return jnp.concatenate([total[0:8] * scale, total[8:16] * scale], axis=0)

    def model_at(interval, d, lanes):
        return (
            model[interval, d, 0, :, lanes].astype(F32),
            model[interval, d, 1, :, lanes].astype(F32),
        )

    def lookup_table(interval):
        stations = lax.broadcasted_iota(jnp.int32, (STATIONS, 2 * ROWS), 0)
        hot[interval] = (stations == prow[interval]).astype(F32).astype(BF16)

    def prepare(interval, first, last):
        def block(index, carry):
            lanes = pl.ds(pl.multiple_of(index * 128, 128), 128)
            vre, vim = vis[interval, 0, :, lanes], vis[interval, 1, :, lanes]

            def direction(d, carry):
                dre, dim = model_at(interval, d, lanes)
                at = pl.ds(d, 1)
                bterm[interval, 0, index, at, :] = jnp.sum(
                    vre * dre + vim * dim, axis=0, keepdims=True
                )
                bterm[interval, 1, index, at, :] = jnp.sum(
                    vim * dre - vre * dim, axis=0, keepdims=True
                )
                strength = jnp.sum(dre * dre + dim * dim, axis=0, keepdims=True)
                power[interval, index, at, :] = strength
                gram[interval, 0, index, d, at, :] = strength
                gram[interval, 1, index, d, at, :] = jnp.zeros_like(strength)
                for step in range(1, DIRS // 2 + 1):
                    e = lax.rem(d + step, DIRS)
                    ere, eim = model_at(interval, e, lanes)
                    re = jnp.sum(ere * dre + eim * dim, axis=0, keepdims=True)
                    im = jnp.sum(eim * dre - ere * dim, axis=0, keepdims=True)
                    gram[interval, 0, index, e, at, :] = re
                    gram[interval, 1, index, e, at, :] = im
                    gram[interval, 0, index, d, pl.ds(e, 1), :] = re
                    gram[interval, 1, index, d, pl.ds(e, 1), :] = -im
                return carry

            lax.fori_loop(0, DIRS, direction, 0)
            return carry

        lax.fori_loop(first, last, block, 0)

    def during_first_sums():
        for interval in range(INTERVALS):
            lookup_table(interval)
            for which in range(2):
                load(interval, which).wait()
        prepare(0, 0, 2)

    exchange(0, first_update, [(0, 1)], during_first_sums, lambda: prepare(0, 2, 4))

    def direct(interval):
        def block(index, carry):
            lanes = pl.ds(pl.multiple_of(index * 128, 128), 128)

            rre, rim = vis[interval, 0, :, lanes], vis[interval, 1, :, lanes]
            for d in range(DIRS):
                mre, mim = model_at(interval, d, lanes)
                wre = mix[interval, d : d + 1, lanes]
                wim = mix[interval, d + 16 : d + 17, lanes]
                rre = rre - (wre * mre - wim * mim)
                rim = rim - (wre * mim + wim * mre)

            def correlate(d, carry):
                mre, mim = model_at(interval, d, lanes)
                at = pl.ds(d, 1)
                kterm[0, index, at, :] = jnp.sum(rre * mre + rim * mim, axis=0, keepdims=True)
                kterm[1, index, at, :] = jnp.sum(rim * mre - rre * mim, axis=0, keepdims=True)
                power[interval, index, at, :] = jnp.sum(
                    mre * mre + mim * mim, axis=0, keepdims=True
                )
                return carry

            lax.fori_loop(0, DIRS, correlate, 0, unroll=4)
            return carry

        lax.fori_loop(0, ROWS // 128, block, 0)

    def gather(interval):
        rows = []
        for z in range(2):
            for dh in range(2):
                rows.append(
                    jnp.concatenate(
                        [
                            chunk[interval * 8 + sb * 2 + dh, z * 8 : z * 8 + 8, :]
                            for sb in range(SBLOCKS)
                        ],
                        axis=1,
                    )
                )
        table = jnp.concatenate(rows, axis=0)
        found = jnp.dot(
            jnp.concatenate(split3(table), axis=0), hot[interval], preferred_element_type=F32
        )
        found = found[0:32] + found[32:64] + found[64:96]
        pairgain[interval] = found
        pre, pim = found[0:16, 0:ROWS], found[16:32, 0:ROWS]
        qre, qim = found[0:16, ROWS:], found[16:32, ROWS:]
        mix[interval, 0:16] = pre * qre + pim * qim
        mix[interval, 16:32] = pim * qre - pre * qim
        return table

    def scatter(interval, prepared=True):
        left, right = [], []
        for block in range(ROWS // 128):
            lanes = slice(block * 128, block * 128 + 128)
            if prepared:
                kre, kim = bterm[interval, 0, block], bterm[interval, 1, block]
            else:
                kre, kim = kterm[0, block], kterm[1, block]
            for e in range(DIRS if prepared else 0):
                wre, wim = mix[interval, e : e + 1, lanes], mix[interval, e + 16 : e + 17, lanes]
                are, aim = gram[interval, 0, block, e], gram[interval, 1, block, e]
                kre = kre - (wre * are - wim * aim)
                kim = kim - (wre * aim + wim * are)
            pre, pim = pairgain[interval, 0:16, lanes], pairgain[interval, 16:32, lanes]
            lanes = slice(ROWS + block * 128, ROWS + block * 128 + 128)
            qre, qim = pairgain[interval, 0:16, lanes], pairgain[interval, 16:32, lanes]
            strength = power[interval, block]
            left.append(
                jnp.concatenate(
                    [
                        qre * kre - qim * kim,
                        qre * kim + qim * kre,
                        strength * (qre * qre + qim * qim),
                    ],
                    axis=0,
                )
            )
            right.append(
                jnp.concatenate(
                    [
                        pre * kre + pim * kim,
                        pim * kre - pre * kim,
                        strength * (pre * pre + pim * pim),
                    ],
                    axis=0,
                )
            )
        terms = jnp.concatenate(left + right, axis=1)
        table = lax.dot_general(
            jnp.concatenate(split3(terms), axis=0),
            hot[interval],
            (((1,), (1,)), ((), ())),
            preferred_element_type=F32,
        )
        pack(interval, table[0:48] + table[48:96] + table[96:144])

    def update(total):
        scale = damping / total[16:24]
        return chunk[plane] + jnp.concatenate([total[0:8] * scale, total[8:16] * scale], axis=0)

    def nothing():
        pass

    def iterate(turn, carry):
        for interval in range(INTERVALS):
            gather(interval)
            scatter(interval)
        exchange(turn, update, COLUMN_STEPS, nothing, nothing)
        return carry

    for interval in range(INTERVALS):
        gather(interval)
    scatter(0)
    direct(1)
    scatter(1, prepared=False)
    exchange(1, update, COLUMN_STEPS, lambda: prepare(1, 0, 2), lambda: prepare(1, 2, 4))
    lax.fori_loop(2, ITERS + 1, iterate, 0)
    for interval in range(INTERVALS):
        gains_out[interval] = gather(interval)
        mix_out[interval] = mix[interval]


def solve(model, visibilities, pairs, held, owner):
    held = held.reshape(INTERVALS, 32, STATIONS)
    prow = pairs.transpose(0, 2, 1).reshape(INTERVALS, 1, 2 * ROWS)
    vmem = pl.BlockSpec(memory_space=pltpu.VMEM)
    smem = pl.BlockSpec(memory_space=pltpu.SMEM)
    far = pl.BlockSpec(memory_space=pl.ANY)
    return pl.pallas_call(
        solve_kernel,
        out_shape=(
            jax.ShapeDtypeStruct((INTERVALS, 32, STATIONS), F32),
            jax.ShapeDtypeStruct((INTERVALS, 32, ROWS), F32),
        ),
        in_specs=[smem, far, far, vmem, vmem],
        out_specs=(vmem, vmem),
        scratch_shapes=[
            pltpu.VMEM((INTERVALS, DIRS, 2, CH, ROWS), BF16),
            pltpu.VMEM((INTERVALS, 2, CH, ROWS), F32),
            pltpu.VMEM((INTERVALS, STATIONS, 2 * ROWS), BF16),
            pltpu.VMEM((INTERVALS, ROWS // 128, DIRS, 128), F32),
            pltpu.VMEM((INTERVALS, 2, ROWS // 128, DIRS, 128), F32),
            pltpu.VMEM((INTERVALS, 2, ROWS // 128, DIRS, DIRS, 128), F32),
            pltpu.VMEM((2, ROWS // 128, DIRS, 128), F32),
            pltpu.VMEM((INTERVALS, 32, 2 * ROWS), F32),
            pltpu.VMEM((INTERVALS, 32, ROWS), F32),
            pltpu.VMEM((PLANE, 24, 128), F32),
            pltpu.VMEM((PLANE - 1, 24, 128), F32),
            pltpu.VMEM((2, COLUMN, 24, 128), F32),
            pltpu.VMEM((PLANE, 16, 128), F32),
            pltpu.SemaphoreType.DMA,
            pltpu.SemaphoreType.DMA,
            pltpu.SemaphoreType.DMA,
            pltpu.SemaphoreType.DMA((2,)),
            pltpu.SemaphoreType.DMA,
            pltpu.SemaphoreType.DMA,
            pltpu.SemaphoreType.DMA((INTERVALS, 2)),
        ],
        compiler_params=pltpu.CompilerParams(
            collective_id=0, has_side_effects=True, vmem_limit_bytes=48 * 1024 * 1024
        ),
        name="solve",
    )(owner, model, visibilities, prow, held)


GROUP = 16
PITCH = 2 * SG + 1
HALVES = 2
NSUB = ROWS // RPS


def sincos(x):
    y = x * x
    s = jnp.full_like(x, 1.0 / math.factorial(17))
    c = jnp.full_like(x, 1.0 / math.factorial(16))
    for n in range(7, -1, -1):
        s = s * y + (-1) ** n / math.factorial(2 * n + 1)
        c = c * y + (-1) ** n / math.factorial(2 * n)
    return c, s * x


def powers(c, s):
    table = {1: (c, s)}
    for n in range(2, SG // 2 + 1):
        (ca, sa), (cb, sb) = table[n // 2], table[n - n // 2]
        table[n] = (ca * cb - sa * sb, ca * sb + sa * cb)
    return table


def image_kernel(
    owner,
    place,
    model_far,
    vis_far,
    mix,
    coords,
    factor,
    facets,
    model,
    vis,
    turned,
    resid,
    base,
    left,
    right,
    loaded,
):
    half = SG // 2

    def load(interval, which):
        far, into = ((model_far, model), (vis_far, vis))[which]
        return pltpu.make_async_copy(
            far.at[interval], into.at[interval], loaded.at[interval, which]
        )

    for interval in range(INTERVALS):
        for which in range(2):
            load(interval, which).start()

    def clear(index, carry):
        facets[index] = jnp.zeros((FACET, 128), F32)
        return carry

    lax.fori_loop(0, facets.shape[0], clear, 0)
    lane = lax.broadcasted_iota(jnp.int32, (1, 128), 1)
    low = lane < 64

    def residual_block(index, carry):
        interval = lax.div(index, 4)
        start = pl.multiple_of(lax.rem(index, 4) * 128, 128)
        lanes = pl.ds(start, 128)
        rre, rim = vis[interval, 0, :, lanes], vis[interval, 1, :, lanes]
        for d in range(DIRS):
            mre = model[interval, d, 0, :, lanes].astype(F32)
            mim = model[interval, d, 1, :, lanes].astype(F32)
            wre = mix[interval, d : d + 1, lanes]
            wim = mix[interval, d + 16 : d + 17, lanes]
            rre = rre - (wre * mre - wim * mim)
            rim = rim - (wre * mim + wim * mre)
        turned[pl.ds(start, 128), :] = jnp.concatenate([rre, rim], axis=0).T
        return carry

    def group(index, carry):
        interval = lax.div(index, NSUB // GROUP)
        first = pl.multiple_of(lax.rem(index, NSUB // GROUP) * GROUP, GROUP)
        rows = pl.ds(first, GROUP)
        re = jnp.concatenate([resid[0, h, rows, :] for h in range(HALVES)], axis=1)
        im = jnp.concatenate([resid[1, h, rows, :] for h in range(HALVES)], axis=1)

        def angles(which):
            c = jnp.concatenate([base[interval, 2 * which, h, rows, :] for h in range(HALVES)], axis=1)
            s = jnp.concatenate([base[interval, 2 * which + 1, h, rows, :] for h in range(HALVES)], axis=1)
            return powers(c, s)

        def put(table, part, pixel, value):
            for h in range(HALVES):
                table[h, pl.ds(part * SG + pixel, GROUP, stride=PITCH), :] = value[
                    :, h * 128 : h * 128 + 128
                ]

        put(left, 0, half, re)
        put(left, 1, half, im)
        for n, (c, s) in angles(0).items():
            rc, rs, ic, js = re * c, re * s, im * c, im * s
            if n < half:
                put(left, 0, half + n, rc - js)
                put(left, 1, half + n, rs + ic)
            put(left, 0, half - n, rc + js)
            put(left, 1, half - n, ic - rs)
        put(right, 0, half, jnp.ones_like(re))
        put(right, 1, half, jnp.zeros_like(re))
        for n, (c, s) in angles(1).items():
            if n < half:
                put(right, 0, half + n, c)
                put(right, 1, half + n, s)
            put(right, 0, half - n, c)
            put(right, 1, half - n, -s)
        sign = jnp.where(low, -1.0, 1.0)
        inside = lax.rem(lane, 64) < SG
        for j in range(GROUP):
            span = slice(j * PITCH, j * PITCH + 2 * SG)
            lhs = jnp.concatenate([left[h, span, :] for h in range(HALVES)], axis=1)
            rhs = jnp.concatenate([right[h, span, :] for h in range(HALVES)], axis=1)
            lhs_hi, rhs_hi = lhs.astype(BF16), rhs.astype(BF16)
            lhs_lo = (lhs - lhs_hi.astype(F32)).astype(BF16)
            rhs_lo = (rhs - rhs_hi.astype(F32)).astype(BF16)
            both = lax.dot_general(
                jnp.concatenate([lhs_hi, lhs_lo], axis=0),
                jnp.concatenate([rhs_hi[0:SG], rhs_lo[0:SG], rhs_hi[SG:], rhs_lo[SG:]], axis=0),
                (((1,), (1,)), ((), ())),
                preferred_element_type=F32,
            )
            real = both[0:SG] + both[2 * SG : 3 * SG]
            imag = both[SG : 2 * SG] + both[3 * SG :]
            image = real + sign * pltpu.roll(imag, 64, axis=1)
            image = image + pltpu.roll(image, 128 - SG, axis=1)
            image = jnp.where(inside, image, 0.0)
            at = owner[interval, first + j]
            across = place[interval, 1, first + j]
            down = place[interval, 0, first + j]
            image = pltpu.roll(image, across, axis=1)
            facets[at, pl.ds(down, SG), :] += image
        return carry

    for interval in range(INTERVALS):
        for h in range(HALVES):
            for which in range(2):
                at = which * RPS + 2 * h
                coord = jnp.where(
                    low, coords[interval, :, at : at + 1], coords[interval, :, at + 1 : at + 2]
                )
                c, s = sincos(coord * factor[...] * (2.0 * math.pi / SG))
                base[interval, 2 * which, h] = c
                base[interval, 2 * which + 1, h] = s
    for interval in range(INTERVALS):
        for which in range(2):
            load(interval, which).wait()
        lax.fori_loop(interval * 4, interval * 4 + 4, residual_block, 0)
        scale = 2.0 / (math.sqrt(INTERVALS * NSUB) * math.sqrt(CH * RPS))
        for h in range(HALVES):
            one = turned[pl.ds(2 * h, NSUB, stride=RPS), :] * scale
            two = turned[pl.ds(2 * h + 1, NSUB, stride=RPS), :] * scale
            resid[0, h] = jnp.where(low, one, pltpu.roll(two, 64, axis=1))
            resid[1, h] = jnp.where(low, pltpu.roll(one, 64, axis=1), two)
        per = NSUB // GROUP
        lax.fori_loop(interval * per, interval * per + per, group, 0)


def local_facets(model, visibilities, mix, uv, owner, place):
    devices = lax.axis_size("freq") * lax.axis_size("bl")
    channel = lax.axis_index("freq") * CH + jnp.arange(CH, dtype=jnp.int32)
    factor = 1.0 + 0.5 * channel.astype(F32) / (lax.axis_size("freq") * CH)
    factor = jnp.concatenate([factor, factor])[None, :]
    coords = uv.reshape(INTERVALS, 2, NSUB, RPS).transpose(0, 2, 1, 3).reshape(INTERVALS, NSUB, 8)
    owner = owner[:, 0, :, 0]
    owner = (owner % 2) * (devices // 2) + owner // 2
    place = place[:, 0].transpose(0, 2, 1)
    vmem = pl.BlockSpec(memory_space=pltpu.VMEM)
    smem = pl.BlockSpec(memory_space=pltpu.SMEM)
    far = pl.BlockSpec(memory_space=pl.ANY)
    return pl.pallas_call(
        image_kernel,
        out_shape=jax.ShapeDtypeStruct((devices, FACET, 128), F32),
        in_specs=[smem, smem, far, far, vmem, vmem, vmem],
        out_specs=vmem,
        scratch_shapes=[
            pltpu.VMEM((INTERVALS, DIRS, 2, CH, ROWS), BF16),
            pltpu.VMEM((INTERVALS, 2, CH, ROWS), F32),
            pltpu.VMEM((ROWS, 128), F32),
            pltpu.VMEM((2, HALVES, NSUB, 128), F32),
            pltpu.VMEM((INTERVALS, 4, HALVES, NSUB, 128), F32),
            pltpu.VMEM((HALVES, GROUP * PITCH, 128), F32),
            pltpu.VMEM((HALVES, GROUP * PITCH, 128), F32),
            pltpu.SemaphoreType.DMA((INTERVALS, 2)),
        ],
        compiler_params=pltpu.CompilerParams(vmem_limit_bytes=48 * 1024 * 1024),
        name="image",
    )(owner, place, model, visibilities, mix, coords, factor)


PARTS = ((0, 24, (0, 1, 2)), (24, 24, (1, 2, 0)), (48, 16, (2, 0, 1)))


def collect_kernel(facets, out, *scratch):
    sibling, one, two, three, s1, s2, s3 = (scratch[3 * n : 3 * n + 3] for n in range(7))
    core_send, core_recv, send, recv = scratch[21:]
    freq = lax.axis_index("freq")
    bl = lax.axis_index("bl")
    core = lax.rem(bl, 2)
    here = (freq, lax.div(bl, 8), lax.rem(lax.div(bl, 2), 4))

    def device(at, core):
        return (at[0], at[1] * 8 + at[2] * 2 + core)

    def peer(axis, step):
        other = lax.rem(here[axis] + step, 4)
        at = list(here)
        at[axis] = other
        return other, device(at, core)

    barrier = pltpu.get_barrier_semaphore()
    pl.semaphore_signal(barrier, inc=1, device_id=device(here, 1 - core), device_id_type=MESH)
    for axis in range(3):
        for step in range(1, 4):
            pl.semaphore_signal(barrier, inc=1, device_id=peer(axis, step)[1], device_id_type=MESH)
    pl.semaphore_wait(barrier, 10)

    def core_copy(p):
        first, rows, _ = PARTS[p]
        return pltpu.make_async_remote_copy(
            src_ref=facets.at[1 - core, :, :, :, pl.ds(first, rows), :],
            dst_ref=sibling[p],
            send_sem=core_send.at[p],
            recv_sem=core_recv.at[p],
            device_id=device(here, 1 - core),
            device_id_type=MESH,
        )

    def stage_copy(stage, p, step):
        axis = PARTS[p][2][stage]
        other, target = peer(axis, step)
        source, into = ((one, s1), (two, s2), (three, s3))[stage]
        return pltpu.make_async_remote_copy(
            src_ref=source[p].at[other],
            dst_ref=into[p].at[step - 1],
            send_sem=send.at[stage, p, step],
            recv_sem=recv.at[stage, p, step],
            device_id=target,
            device_id_type=MESH,
        )

    for p in range(3):
        core_copy(p).start()
    for p in range(3):
        first, rows, order = PARTS[p]
        core_copy(p).wait_recv()

        def add(index, carry, p=p, first=first, rows=rows, order=order):
            at = (lax.div(index, 16), lax.rem(lax.div(index, 4), 4), lax.rem(index, 4))
            i, j, k = (at[axis] for axis in order)
            one[p][i, j, k] = (
                facets[core, at[0], at[1], at[2], pl.ds(first, rows), :]
                + sibling[p][at[0], at[1], at[2]]
            )
            return carry

        lax.fori_loop(0, 64, add, 0, unroll=4)
        for step in range(1, 4):
            stage_copy(0, p, step).start()
    for stage in range(3):
        source, into = ((one, s1), (two, s2), (three, s3))[stage]
        for p in range(3):
            first, rows, order = PARTS[p]
            mine = here[order[stage]]
            for step in range(1, 4):
                stage_copy(stage, p, step).wait_recv()
            total = source[p][mine] + into[p][0] + into[p][1] + into[p][2]
            if stage < 2:
                (two, three)[stage][p][...] = total
                for step in range(1, 4):
                    stage_copy(stage + 1, p, step).start()
            else:
                out[first : first + rows, :] = total
    for p in range(3):
        core_copy(p).wait_send()
        for stage in range(3):
            for step in range(1, 4):
                stage_copy(stage, p, step).wait_send()


def collect(facets):
    vmem = pl.BlockSpec(memory_space=pltpu.VMEM)
    leads = ((4, 4, 4), (4, 4, 4), (4, 4), (4,), (3, 4, 4), (3, 4), (3,))
    return pl.pallas_call(
        collect_kernel,
        out_shape=jax.ShapeDtypeStruct((FACET, 128), F32),
        in_specs=[vmem],
        out_specs=vmem,
        scratch_shapes=[
            pltpu.VMEM(lead + (rows, 128), F32) for lead in leads for _, rows, _ in PARTS
        ]
        + [
            pltpu.SemaphoreType.DMA((3,)),
            pltpu.SemaphoreType.DMA((3,)),
            pltpu.SemaphoreType.DMA((3, 3, 4)),
            pltpu.SemaphoreType.DMA((3, 3, 4)),
        ],
        compiler_params=pltpu.CompilerParams(
            collective_id=1, has_side_effects=True, vmem_limit_bytes=32 * 1024 * 1024
        ),
        name="collect",
    )(facets.reshape(2, 4, 4, 4, FACET, 128))


def body(visibilities, model, pairs, uv, held_gains, solver_owner, facet_owner, subgrid_pos):
    gains, mix = solve(model, visibilities, pairs, held_gains[0], solver_owner)
    facets = local_facets(model, visibilities, mix, uv, facet_owner, subgrid_pos)
    facet = collect(facets)
    facet = facet.reshape(FACET, 2, FACET).transpose(1, 0, 2)
    return (gains.reshape(INTERVALS, 2, DIRS, STATIONS), facet[None, None])


def solution(mesh):
    placed = (
        P(None, None, "freq", "bl"),
        P(None, None, None, "freq", "bl"),
        P(None, "bl", None),
        P(None, None, "bl"),
        P("bl", None, None, None, None),
        P(),
        P(None, "freq", "bl", None),
        P(None, "freq", "bl", None),
    )
    return jax.shard_map(
        body,
        mesh=mesh,
        in_specs=placed,
        out_specs=(P(), P("freq", "bl", None, None, None)),
        check_vma=False,
    )
```

```python
import functools
import math

import jax
import jax.numpy as jnp
from jax import lax
from jax.experimental import pallas as pl
from jax.experimental.pallas import tpu as pltpu
from jax.sharding import PartitionSpec as P

SG = 32
FACET = 64
RPS = 4
ITERS = 4
INTERVALS = 2
DIRS = 16
STATIONS = 512
ROWS = 512
CH = 64
PLANE = 16
COLUMN = 8
SBLOCKS = STATIONS // 128
MESH = pl.DeviceIdType.MESH
F32 = jnp.float32
BF16 = jnp.bfloat16

damping = 0.5


def split3(x):
    hi = x.astype(BF16)
    rest = x - hi.astype(F32)
    mid = rest.astype(BF16)
    low = (rest - mid.astype(F32)).astype(BF16)
    return hi, mid, low


GROUP = 16
SOLVE_MIB = 18
IMAGE_MIB = 12
PITCH = 2 * SG + 1
HALVES = 2
NSUB = ROWS // RPS


def sincos(x):
    y = x * x
    s = jnp.full_like(x, 1.0 / math.factorial(17))
    c = jnp.full_like(x, 1.0 / math.factorial(16))
    for n in range(7, -1, -1):
        s = s * y + (-1) ** n / math.factorial(2 * n + 1)
        c = c * y + (-1) ** n / math.factorial(2 * n)
    return c, s * x


def powers(c, s):
    table = {1: (c, s)}
    for n in range(2, SG // 2 + 1):
        (ca, sa), (cb, sb) = table[n // 2], table[n - n // 2]
        table[n] = (ca * cb - sa * sb, ca * sb + sa * cb)
    return table


def spread(sizes):
    steps = [(i, j) for i in range(sizes[0]) for j in range(sizes[1]) if i or j]
    return sorted(steps, key=lambda t: -sum(min(k, n - k) for k, n in zip(t, sizes)))


PLANE_STEPS = spread((4, 4))
COLUMN_STEPS = spread((4, 2))


def solve_kernel(
    owner_far,
    model_far,
    vis_far,
    pairs_far,
    held_far,
    uv_far,
    gains_out,
    mix_out,
    across,
    down,
    owner,
    model,
    vis,
    pairs,
    held,
    uv,
    turned,
    coords,
    hot,
    power,
    bterm,
    gram,
    kterm,
    right,
    pairgain,
    mix,
    sums,
    arrived,
    partial,
    chunk,
    rs_send,
    rs_recv,
    ex_send,
    ex_recv,
    ag_send,
    ag_recv,
    loaded,
):
    whole = (
        (owner_far, owner),
        (held_far, held),
        (pairs_far, pairs),
        (uv_far, uv),
        (vis_far, vis),
        (model_far, model),
    )
    loads = [
        pltpu.make_async_copy(far, near, loaded.at[k]) for k, (far, near) in enumerate(whole)
    ]
    for load in loads:
        load.start()
    freq = lax.axis_index("freq")
    bl = lax.axis_index("bl")
    core = lax.rem(bl, 2)
    plane = lax.div(bl, 2)
    column = freq * 2 + core

    def plane_peer(steps):
        first = lax.rem(lax.div(plane, 4) + steps[0], 4)
        second = lax.rem(lax.rem(plane, 4) + steps[1], 4)
        other = first * 4 + second
        return other, (freq, other * 2 + core)

    def column_peer(steps):
        first = lax.rem(freq + steps[0], 4)
        second = lax.rem(core + steps[1], 2)
        return first * 2 + second, (first, plane * 2 + second)

    barrier = pltpu.get_barrier_semaphore()
    for steps in PLANE_STEPS:
        pl.semaphore_signal(barrier, inc=1, device_id=plane_peer(steps)[1], device_id_type=MESH)
    for steps in COLUMN_STEPS:
        pl.semaphore_signal(barrier, inc=1, device_id=column_peer(steps)[1], device_id_type=MESH)
    pl.semaphore_wait(barrier, PLANE - 1 + COLUMN - 1)

    def exchange(turn, update, column_steps, during_sums, during_gains):
        par = lax.rem(turn, 2)
        reach = len(column_steps)

        def remote(source, into, send, recv, device):
            return pltpu.make_async_remote_copy(
                src_ref=source,
                dst_ref=into,
                send_sem=send,
                recv_sem=recv,
                device_id=device,
                device_id_type=MESH,
            )

        near = plane_peer(PLANE_STEPS[0])[1]
        beside = column_peer(column_steps[0])[1]
        rs_all = remote(sums.at[pl.ds(0, PLANE - 1)], arrived, rs_send, rs_recv, near)
        ex_all = remote(
            partial.at[par, pl.ds(0, reach)],
            partial.at[par, pl.ds(0, reach)],
            ex_send,
            ex_recv.at[par],
            beside,
        )
        ag_all = remote(
            chunk.at[pl.ds(0, PLANE - 1)], chunk.at[pl.ds(0, PLANE - 1)], ag_send, ag_recv, near
        )
        for k, steps in enumerate(PLANE_STEPS):
            other, device = plane_peer(steps)
            remote(sums.at[other], arrived.at[k], rs_send, rs_recv, device).start()
        during_sums()
        rs_all.wait_recv()
        total = sums[plane]
        for k in range(PLANE - 1):
            total = total + arrived[k]
        partial[par, column] = total
        for steps in column_steps:
            _, device = column_peer(steps)
            mine = partial.at[par, column]
            remote(mine, mine, ex_send, ex_recv.at[par], device).start()
        rs_all.wait_send()
        ex_all.wait_recv()
        if reach == COLUMN - 1:
            total = partial[par, 0]
            for m in range(1, COLUMN):
                total = total + partial[par, m]
        else:
            total = partial[par, freq * 2] + partial[par, freq * 2 + 1]
        chunk[plane] = update(total)
        for steps in PLANE_STEPS:
            _, device = plane_peer(steps)
            mine = chunk.at[plane]
            remote(mine, mine, ag_send, ag_recv, device).start()
        during_gains()
        ex_all.wait_send()
        ag_all.wait_recv()
        ag_all.wait_send()

    def pack(interval, table):
        for sb in range(SBLOCKS):
            for dh in range(2):
                for q in range(3):
                    sums[interval * 8 + sb * 2 + dh, q * 8 : q * 8 + 8, :] = table[
                        q * 16 + dh * 8 : q * 16 + dh * 8 + 8, sb * 128 : sb * 128 + 128
                    ]

    for load in loads[:2]:
        load.wait()
    for interval in range(INTERVALS):
        mine = (owner[interval] == bl).astype(F32)
        pack(
            interval,
            jnp.concatenate([held[interval] * mine, jnp.full((DIRS, STATIONS), mine)], axis=0),
        )

    def first_update(total):
        scale = 1.0 / total[16:24]
        return jnp.concatenate([total[0:8] * scale, total[8:16] * scale], axis=0)

    def model_at(interval, d, lanes):
        return (
            model[interval, d, 0, :, lanes].astype(F32),
            model[interval, d, 1, :, lanes].astype(F32),
        )

    def lookup_table(interval):
        stations = lax.broadcasted_iota(jnp.int32, (STATIONS, ROWS), 0)
        for end in range(2):
            found = stations == pairs[interval, end : end + 1, :]
            hot[interval, :, end * ROWS : end * ROWS + ROWS] = found.astype(F32).astype(BF16)

    def prepare(interval, first, last):
        def block(index, carry):
            lanes = pl.ds(pl.multiple_of(index * 128, 128), 128)
            vre, vim = vis[interval, 0, :, lanes], vis[interval, 1, :, lanes]

            def direction(d, carry):
                dre, dim = model_at(interval, d, lanes)
                at = pl.ds(d, 1)
                bterm[interval, 0, index, at, :] = jnp.sum(
                    vre * dre + vim * dim, axis=0, keepdims=True
                )
                bterm[interval, 1, index, at, :] = jnp.sum(
                    vim * dre - vre * dim, axis=0, keepdims=True
                )
                strength = jnp.sum(dre * dre + dim * dim, axis=0, keepdims=True)
                power[interval, index, at, :] = strength
                gram[interval, 0, index, d, at, :] = strength
                gram[interval, 1, index, d, at, :] = jnp.zeros_like(strength)
                for step in range(1, DIRS // 2 + 1):
                    e = lax.rem(d + step, DIRS)
                    ere, eim = model_at(interval, e, lanes)
                    re = jnp.sum(ere * dre + eim * dim, axis=0, keepdims=True)
                    im = jnp.sum(eim * dre - ere * dim, axis=0, keepdims=True)
                    gram[interval, 0, index, e, at, :] = re
                    gram[interval, 1, index, e, at, :] = im
                    gram[interval, 0, index, d, pl.ds(e, 1), :] = re
                    gram[interval, 1, index, d, pl.ds(e, 1), :] = -im
                return carry

            lax.fori_loop(0, DIRS, direction, 0)
            return carry

        lax.fori_loop(first, last, block, 0)

    def sample_coords(interval):
        for block in range(ROWS // 128):
            lanes = slice(block * 128, block * 128 + 128)
            padded = jnp.concatenate([uv[interval, :, lanes], jnp.zeros((126, 128), F32)], axis=0)
            turned[lanes, :] = padded.T
        for row in range(RPS):
            coords[interval, row] = turned[pl.ds(row, NSUB, stride=RPS), :]

    def during_first_sums():
        for load in loads[2:]:
            load.wait()
        for interval in range(INTERVALS):
            lookup_table(interval)
            sample_coords(interval)
        prepare(0, 0, 2)

    exchange(0, first_update, [(0, 1)], during_first_sums, lambda: prepare(0, 2, 4))

    def direct(interval):
        def block(index, carry):
            lanes = pl.ds(pl.multiple_of(index * 128, 128), 128)

            rre, rim = vis[interval, 0, :, lanes], vis[interval, 1, :, lanes]
            for d in range(DIRS):
                mre, mim = model_at(interval, d, lanes)
                wre = mix[interval, d : d + 1, lanes]
                wim = mix[interval, d + 16 : d + 17, lanes]
                rre = rre - (wre * mre - wim * mim)
                rim = rim - (wre * mim + wim * mre)

            def correlate(d, carry):
                mre, mim = model_at(interval, d, lanes)
                at = pl.ds(d, 1)
                kterm[0, index, at, :] = jnp.sum(rre * mre + rim * mim, axis=0, keepdims=True)
                kterm[1, index, at, :] = jnp.sum(rim * mre - rre * mim, axis=0, keepdims=True)
                power[interval, index, at, :] = jnp.sum(
                    mre * mre + mim * mim, axis=0, keepdims=True
                )
                return carry

            lax.fori_loop(0, DIRS, correlate, 0, unroll=4)
            return carry

        lax.fori_loop(0, ROWS // 128, block, 0)

    def gather(interval):
        rows = []
        for z in range(2):
            for dh in range(2):
                rows.append(
                    jnp.concatenate(
                        [
                            chunk[interval * 8 + sb * 2 + dh, z * 8 : z * 8 + 8, :]
                            for sb in range(SBLOCKS)
                        ],
                        axis=1,
                    )
                )
        table = jnp.concatenate(rows, axis=0)
        found = jnp.dot(
            jnp.concatenate(split3(table), axis=0), hot[interval], preferred_element_type=F32
        )
        found = found[0:32] + found[32:64] + found[64:96]
        pairgain[interval] = found
        pre, pim = found[0:16, 0:ROWS], found[16:32, 0:ROWS]
        qre, qim = found[0:16, ROWS:], found[16:32, ROWS:]
        mix[interval, 0:16] = pre * qre + pim * qim
        mix[interval, 16:32] = pim * qre - pre * qim
        return table

    def scatter(interval, prepared=True):
        left, right = [], []
        for block in range(ROWS // 128):
            lanes = slice(block * 128, block * 128 + 128)
            if prepared:
                kre, kim = bterm[interval, 0, block], bterm[interval, 1, block]
            else:
                kre, kim = kterm[0, block], kterm[1, block]
            for e in range(DIRS if prepared else 0):
                wre, wim = mix[interval, e : e + 1, lanes], mix[interval, e + 16 : e + 17, lanes]
                are, aim = gram[interval, 0, block, e], gram[interval, 1, block, e]
                kre = kre - (wre * are - wim * aim)
                kim = kim - (wre * aim + wim * are)
            pre, pim = pairgain[interval, 0:16, lanes], pairgain[interval, 16:32, lanes]
            lanes = slice(ROWS + block * 128, ROWS + block * 128 + 128)
            qre, qim = pairgain[interval, 0:16, lanes], pairgain[interval, 16:32, lanes]
            strength = power[interval, block]
            left.append(
                jnp.concatenate(
                    [
                        qre * kre - qim * kim,
                        qre * kim + qim * kre,
                        strength * (qre * qre + qim * qim),
                    ],
                    axis=0,
                )
            )
            right.append(
                jnp.concatenate(
                    [
                        pre * kre + pim * kim,
                        pim * kre - pre * kim,
                        strength * (pre * pre + pim * pim),
                    ],
                    axis=0,
                )
            )
        terms = jnp.concatenate(left + right, axis=1)
        table = lax.dot_general(
            jnp.concatenate(split3(terms), axis=0),
            hot[interval],
            (((1,), (1,)), ((), ())),
            preferred_element_type=F32,
        )
        pack(interval, table[0:48] + table[48:96] + table[96:144])

    def update(total):
        scale = damping / total[16:24]
        return chunk[plane] + jnp.concatenate([total[0:8] * scale, total[8:16] * scale], axis=0)

    lane = lax.broadcasted_iota(jnp.int32, (1, 128), 1)
    low = lane < CH
    channel = (freq * CH + lax.rem(lane, CH)).astype(F32)
    factor = 1.0 + 0.5 * channel / (4 * CH)

    def put(pixel, value):
        for h in range(HALVES):
            right[h, pl.ds(pixel, GROUP, stride=PITCH), :] = value[:, h * 128 : h * 128 + 128]

    def phases(index, carry):
        interval = lax.div(index, NSUB // GROUP)
        first = pl.multiple_of(lax.rem(index, NSUB // GROUP) * GROUP, GROUP)
        rows = pl.ds(first, GROUP)

        def angles(which):
            coord = []
            for h in range(HALVES):
                one = coords[interval, 2 * h, rows, which : which + 1]
                two = coords[interval, 2 * h + 1, rows, which : which + 1]
                coord.append(jnp.where(low, one, two) * factor)
            return powers(*sincos(jnp.concatenate(coord, axis=1) * (2.0 * math.pi / SG)))

        for n, pair in angles(0).items():
            for z in range(2):
                for h in range(HALVES):
                    down[interval, n - 1, z, h, rows, :] = pair[z][:, h * 128 : h * 128 + 128]
        half = SG // 2
        one = jnp.ones((GROUP, HALVES * 128), F32)
        put(half, one)
        put(SG + half, one * 0.0)
        for n, (c, s) in angles(1).items():
            if n < half:
                put(half + n, c)
                put(SG + half + n, s)
            put(half - n, c)
            put(SG + half - n, -s)
        for j in range(GROUP):
            for part in range(2):
                span = slice(j * PITCH + part * SG, j * PITCH + part * SG + SG)
                for h in range(HALVES):
                    lanes = slice(h * 128, h * 128 + 128)
                    value = right[h, span, :]
                    high = value.astype(BF16)
                    across[interval, first + j, 2 * part * SG : 2 * part * SG + SG, lanes] = high
                    across[interval, first + j, 2 * part * SG + SG : 2 * part * SG + 2 * SG, lanes] = (
                        value - high.astype(F32)
                    ).astype(BF16)
        return carry

    groups = INTERVALS * NSUB // GROUP
    each = -(-groups // (2 * (ITERS - 1)))

    def some_phases(slot):
        first = slot * each
        lax.fori_loop(first, jnp.minimum(first + each, groups), phases, 0)

    def iterate(turn, carry):
        for interval in range(INTERVALS):
            gather(interval)
            scatter(interval)
        slot = (turn - 2) * 2
        exchange(
            turn,
            update,
            COLUMN_STEPS,
            lambda: some_phases(slot),
            lambda: some_phases(slot + 1),
        )
        return carry

    for interval in range(INTERVALS):
        gather(interval)
    scatter(0)
    direct(1)
    scatter(1, prepared=False)
    exchange(1, update, COLUMN_STEPS, lambda: prepare(1, 0, 2), lambda: prepare(1, 2, 4))
    lax.fori_loop(2, ITERS + 1, iterate, 0)
    for interval in range(INTERVALS):
        gains_out[interval] = gather(interval)
        mix_out[interval] = mix[interval]


def in_hbm(*arrays):
    return [pltpu.with_memory_space_constraint(array, pltpu.HBM) for array in arrays]


def solve(model, visibilities, pairs, held, owner, uv):
    held = held.reshape(INTERVALS, 32, STATIONS)
    pairs = pairs.transpose(0, 2, 1)
    vmem = pl.BlockSpec(memory_space=pltpu.VMEM)
    far = pl.BlockSpec(memory_space=pltpu.HBM)
    return pl.pallas_call(
        solve_kernel,
        out_shape=(
            jax.ShapeDtypeStruct((INTERVALS, 32, STATIONS), F32),
            jax.ShapeDtypeStruct((INTERVALS, 32, ROWS), F32),
            jax.ShapeDtypeStruct((INTERVALS, NSUB, 4 * SG, HALVES * 128), BF16),
            jax.ShapeDtypeStruct((INTERVALS, SG // 2, 2, HALVES, NSUB, 128), F32),
        ),
        in_specs=[far] * 6,
        out_specs=(vmem, vmem, vmem, vmem),
        scratch_shapes=[
            pltpu.SMEM((INTERVALS,), jnp.int32),
            pltpu.VMEM((INTERVALS, DIRS, 2, CH, ROWS), BF16),
            pltpu.VMEM((INTERVALS, 2, CH, ROWS), F32),
            pltpu.VMEM((INTERVALS, 2, ROWS), jnp.int32),
            pltpu.VMEM((INTERVALS, 32, STATIONS), F32),
            pltpu.VMEM((INTERVALS, 2, ROWS), F32),
            pltpu.VMEM((ROWS, 128), F32),
            pltpu.VMEM((INTERVALS, RPS, NSUB, 128), F32),
            pltpu.VMEM((INTERVALS, STATIONS, 2 * ROWS), BF16),
            pltpu.VMEM((INTERVALS, ROWS // 128, DIRS, 128), F32),
            pltpu.VMEM((INTERVALS, 2, ROWS // 128, DIRS, 128), F32),
            pltpu.VMEM((INTERVALS, 2, ROWS // 128, DIRS, DIRS, 128), F32),
            pltpu.VMEM((2, ROWS // 128, DIRS, 128), F32),
            pltpu.VMEM((HALVES, GROUP * PITCH, 128), F32),
            pltpu.VMEM((INTERVALS, 32, 2 * ROWS), F32),
            pltpu.VMEM((INTERVALS, 32, ROWS), F32),
            pltpu.VMEM((PLANE, 24, 128), F32),
            pltpu.VMEM((PLANE - 1, 24, 128), F32),
            pltpu.VMEM((2, COLUMN, 24, 128), F32),
            pltpu.VMEM((PLANE, 16, 128), F32),
            pltpu.SemaphoreType.DMA,
            pltpu.SemaphoreType.DMA,
            pltpu.SemaphoreType.DMA,
            pltpu.SemaphoreType.DMA((2,)),
            pltpu.SemaphoreType.DMA,
            pltpu.SemaphoreType.DMA,
            pltpu.SemaphoreType.DMA((6,)),
        ],
        compiler_params=pltpu.CompilerParams(
            collective_id=0, has_side_effects=True, vmem_limit_bytes=SOLVE_MIB * 1024 * 1024
        ),
        name="solve",
    )(*in_hbm(owner, model, visibilities, pairs, held, uv))


def image_kernel(
    owner_far,
    place_far,
    model_far,
    vis_far,
    gains,
    mix,
    phase_across,
    phase_down,
    facets,
    gains_out,
    owner,
    place,
    model,
    vis,
    turned,
    resid,
    left_even,
    left_odd,
    loaded,
):
    half = SG // 2
    whole = (
        (vis_far, vis),
        (model_far, model),
        (owner_far, owner),
        (place_far, place),
        (gains, gains_out),
    )
    loads = [
        pltpu.make_async_copy(far, near, loaded.at[k]) for k, (far, near) in enumerate(whole)
    ]
    for load in loads:
        load.start()

    def clear(index, carry):
        facets[index] = jnp.zeros((FACET, 128), F32)
        return carry

    lax.fori_loop(0, facets.shape[0], clear, 0)
    lane = lax.broadcasted_iota(jnp.int32, (1, 128), 1)
    low = lane < 64

    def residual_block(index, carry):
        interval = lax.div(index, 4)
        start = pl.multiple_of(lax.rem(index, 4) * 128, 128)
        lanes = pl.ds(start, 128)
        rre, rim = vis[interval, 0, :, lanes], vis[interval, 1, :, lanes]
        for d in range(DIRS):
            mre = model[interval, d, 0, :, lanes].astype(F32)
            mim = model[interval, d, 1, :, lanes].astype(F32)
            wre = mix[interval, d : d + 1, lanes]
            wim = mix[interval, d + 16 : d + 17, lanes]
            rre = rre - (wre * mre - wim * mim)
            rim = rim - (wre * mim + wim * mre)
        turned[interval, pl.ds(start, 128), :] = jnp.concatenate([rre, rim], axis=0).T
        return carry

    def where(index):
        interval = lax.div(index, NSUB // GROUP)
        return interval, pl.multiple_of(lax.rem(index, NSUB // GROUP) * GROUP, GROUP)

    def operands(index, left):
        interval, first = where(index)
        rows = pl.ds(first, GROUP)
        re = jnp.concatenate([resid[interval, 0, h, rows, :] for h in range(HALVES)], axis=1)
        im = jnp.concatenate([resid[interval, 1, h, rows, :] for h in range(HALVES)], axis=1)

        def put(part, pixel, value):
            for h in range(HALVES):
                left[h, pl.ds(part * SG + pixel, GROUP, stride=PITCH), :] = value[
                    :, h * 128 : h * 128 + 128
                ]

        put(0, half, re)
        put(1, half, im)
        for n in range(1, half + 1):
            c, s = (
                jnp.concatenate(
                    [phase_down[interval, n - 1, z, h, rows, :] for h in range(HALVES)], axis=1
                )
                for z in range(2)
            )
            rc, rs, ic, js = re * c, re * s, im * c, im * s
            if n < half:
                put(0, half + n, rc - js)
                put(1, half + n, rs + ic)
            put(0, half - n, rc + js)
            put(1, half - n, ic - rs)

    def images(index, left):
        interval, first = where(index)
        sign = jnp.where(low, -1.0, 1.0)
        inside = lax.rem(lane, 64) < SG
        for j in range(GROUP):
            span = slice(j * PITCH, j * PITCH + 2 * SG)
            lhs = jnp.concatenate([left[h, span, :] for h in range(HALVES)], axis=1)
            high = lhs.astype(BF16)
            rest = (lhs - high.astype(F32)).astype(BF16)
            both = lax.dot_general(
                jnp.concatenate([high, rest], axis=0),
                phase_across[interval, first + j],
                (((1,), (1,)), ((), ())),
                preferred_element_type=F32,
            )
            real = both[0:SG] + both[2 * SG : 3 * SG]
            imag = both[SG : 2 * SG] + both[3 * SG :]
            image = real + sign * pltpu.roll(imag, 64, axis=1)
            image = image + pltpu.roll(image, 128 - SG, axis=1)
            image = jnp.where(inside, image, 0.0)
            at = owner[interval, first + j]
            at = lax.rem(at, 2) * (facets.shape[0] // 2) + lax.div(at, 2)
            across = place[interval, 1, first + j]
            down = place[interval, 0, first + j]
            image = pltpu.roll(image, across, axis=1)
            facets[at, pl.ds(down, SG), :] += image

    for load in loads[:2]:
        load.wait()
    lax.fori_loop(0, INTERVALS * 4, residual_block, 0)
    scale = 2.0 / (math.sqrt(INTERVALS * NSUB) * math.sqrt(CH * RPS))
    for interval in range(INTERVALS):
        for h in range(HALVES):
            one = turned[interval, pl.ds(2 * h, NSUB, stride=RPS), :] * scale
            two = turned[interval, pl.ds(2 * h + 1, NSUB, stride=RPS), :] * scale
            resid[interval, 0, h] = jnp.where(low, one, pltpu.roll(two, 64, axis=1))
            resid[interval, 1, h] = jnp.where(low, pltpu.roll(one, 64, axis=1), two)
    for load in loads[2:]:
        load.wait()
    groups = INTERVALS * NSUB // GROUP
    operands(0, left_even)

    def two_groups(index, carry):
        operands(2 * index + 1, left_odd)
        images(2 * index, left_even)
        operands(jnp.minimum(2 * index + 2, groups - 1), left_even)
        images(2 * index + 1, left_odd)
        return carry

    lax.fori_loop(0, groups // 2, two_groups, 0)


def local_facets(model, visibilities, gains, mix, phase_across, phase_down, owner, place):
    devices = lax.axis_size("freq") * lax.axis_size("bl")
    owner = owner[:, 0, :, 0]
    place = place[:, 0].transpose(0, 2, 1)
    vmem = pl.BlockSpec(memory_space=pltpu.VMEM)
    far = pl.BlockSpec(memory_space=pltpu.HBM)
    return pl.pallas_call(
        image_kernel,
        out_shape=(
            jax.ShapeDtypeStruct((devices, FACET, 128), F32),
            jax.ShapeDtypeStruct(gains.shape, F32),
        ),
        in_specs=[far] * 4 + [vmem] * 4,
        out_specs=(vmem, far),
        scratch_shapes=[
            pltpu.SMEM((INTERVALS, NSUB), jnp.int32),
            pltpu.SMEM((INTERVALS, 2, NSUB), jnp.int32),
            pltpu.VMEM((INTERVALS, DIRS, 2, CH, ROWS), BF16),
            pltpu.VMEM((INTERVALS, 2, CH, ROWS), F32),
            pltpu.VMEM((INTERVALS, ROWS, 128), F32),
            pltpu.VMEM((INTERVALS, 2, HALVES, NSUB, 128), F32),
            pltpu.VMEM((HALVES, GROUP * PITCH, 128), F32),
            pltpu.VMEM((HALVES, GROUP * PITCH, 128), F32),
            pltpu.SemaphoreType.DMA((5,)),
        ],
        compiler_params=pltpu.CompilerParams(vmem_limit_bytes=IMAGE_MIB * 1024 * 1024),
        name="image",
    )(*in_hbm(owner, place, model, visibilities), gains, mix, phase_across, phase_down)


PARTS = ((0, 24, (0, 1, 2)), (24, 24, (1, 2, 0)), (48, 16, (2, 0, 1)))


def collect_kernel(facets, out, *scratch):
    sibling, one, two, three, s1, s2, s3 = (scratch[3 * n : 3 * n + 3] for n in range(7))
    core_send, core_recv, send, recv = scratch[21:]
    freq = lax.axis_index("freq")
    bl = lax.axis_index("bl")
    core = lax.rem(bl, 2)
    here = (freq, lax.div(bl, 8), lax.rem(lax.div(bl, 2), 4))

    def device(at, core):
        return (at[0], at[1] * 8 + at[2] * 2 + core)

    def peer(axis, step):
        other = lax.rem(here[axis] + step, 4)
        at = list(here)
        at[axis] = other
        return other, device(at, core)

    barrier = pltpu.get_barrier_semaphore()
    pl.semaphore_signal(barrier, inc=1, device_id=device(here, 1 - core), device_id_type=MESH)
    for axis in range(3):
        for step in range(1, 4):
            pl.semaphore_signal(barrier, inc=1, device_id=peer(axis, step)[1], device_id_type=MESH)
    pl.semaphore_wait(barrier, 10)

    def core_copy(p):
        first, rows, _ = PARTS[p]
        return pltpu.make_async_remote_copy(
            src_ref=facets.at[1 - core, :, :, :, pl.ds(first, rows), :],
            dst_ref=sibling[p],
            send_sem=core_send.at[p],
            recv_sem=core_recv.at[p],
            device_id=device(here, 1 - core),
            device_id_type=MESH,
        )

    def stage_copy(stage, p, step):
        axis = PARTS[p][2][stage]
        other, target = peer(axis, step)
        source, into = ((one, s1), (two, s2), (three, s3))[stage]
        return pltpu.make_async_remote_copy(
            src_ref=source[p].at[other],
            dst_ref=into[p].at[step - 1],
            send_sem=send.at[stage, p, step],
            recv_sem=recv.at[stage, p, step],
            device_id=target,
            device_id_type=MESH,
        )

    for p in range(3):
        core_copy(p).start()
    for p in range(3):
        first, rows, order = PARTS[p]
        core_copy(p).wait_recv()

        def add(index, carry, p=p, first=first, rows=rows, order=order):
            at = (lax.div(index, 16), lax.rem(lax.div(index, 4), 4), lax.rem(index, 4))
            i, j, k = (at[axis] for axis in order)
            one[p][i, j, k] = (
                facets[core, at[0], at[1], at[2], pl.ds(first, rows), :]
                + sibling[p][at[0], at[1], at[2]]
            )
            return carry

        lax.fori_loop(0, 64, add, 0, unroll=4)
        for step in range(1, 4):
            stage_copy(0, p, step).start()
    for stage in range(3):
        source, into = ((one, s1), (two, s2), (three, s3))[stage]
        for p in range(3):
            first, rows, order = PARTS[p]
            mine = here[order[stage]]
            for step in range(1, 4):
                stage_copy(stage, p, step).wait_recv()
            total = source[p][mine] + into[p][0] + into[p][1] + into[p][2]
            if stage < 2:
                (two, three)[stage][p][...] = total
                for step in range(1, 4):
                    stage_copy(stage + 1, p, step).start()
            else:
                out[first : first + rows, :] = total
    for p in range(3):
        core_copy(p).wait_send()
        for stage in range(3):
            for step in range(1, 4):
                stage_copy(stage, p, step).wait_send()


def collect(facets):
    vmem = pl.BlockSpec(memory_space=pltpu.VMEM)
    leads = ((4, 4, 4), (4, 4, 4), (4, 4), (4,), (3, 4, 4), (3, 4), (3,))
    return pl.pallas_call(
        collect_kernel,
        out_shape=jax.ShapeDtypeStruct((FACET, 128), F32),
        in_specs=[vmem],
        out_specs=vmem,
        scratch_shapes=[
            pltpu.VMEM(lead + (rows, 128), F32) for lead in leads for _, rows, _ in PARTS
        ]
        + [
            pltpu.SemaphoreType.DMA((3,)),
            pltpu.SemaphoreType.DMA((3,)),
            pltpu.SemaphoreType.DMA((3, 3, 4)),
            pltpu.SemaphoreType.DMA((3, 3, 4)),
        ],
        compiler_params=pltpu.CompilerParams(
            collective_id=1, has_side_effects=True, vmem_limit_bytes=32 * 1024 * 1024
        ),
        name="collect",
    )(facets.reshape(2, 4, 4, 4, FACET, 128))


def body(visibilities, model, pairs, uv, held_gains, solver_owner, facet_owner, subgrid_pos):
    gains, mix, phase_across, phase_down = solve(
        model, visibilities, pairs, held_gains[0], solver_owner, uv
    )
    facets, gains = local_facets(
        model, visibilities, gains, mix, phase_across, phase_down, facet_owner, subgrid_pos
    )
    facet = collect(facets)
    facet = facet.reshape(FACET, 2, FACET).transpose(1, 0, 2)
    return (gains.reshape(INTERVALS, 2, DIRS, STATIONS), facet[None, None])


def solution(mesh):
    placed = (
        P(None, None, "freq", "bl"),
        P(None, None, None, "freq", "bl"),
        P(None, "bl", None),
        P(None, None, "bl"),
        P("bl", None, None, None, None),
        P(),
        P(None, "freq", "bl", None),
        P(None, "freq", "bl", None),
    )
    return jax.shard_map(
        body,
        mesh=mesh,
        in_specs=placed,
        out_specs=(P(), P("freq", "bl", None, None, None)),
        check_vma=False,
    )
```

```python
import functools
import math

import jax
import jax.numpy as jnp
from jax import lax
from jax.experimental import pallas as pl
from jax.experimental.pallas import tpu as pltpu
from jax.sharding import PartitionSpec as P

SG = 32
FACET = 64
RPS = 4
ITERS = 4
INTERVALS = 2
DIRS = 16
STATIONS = 512
ROWS = 512
CH = 64
PLANE = 16
COLUMN = 8
SBLOCKS = STATIONS // 128
MESH = pl.DeviceIdType.MESH
F32 = jnp.float32
BF16 = jnp.bfloat16

damping = 0.5


def split3(x):
    hi = x.astype(BF16)
    rest = x - hi.astype(F32)
    mid = rest.astype(BF16)
    low = (rest - mid.astype(F32)).astype(BF16)
    return hi, mid, low


GROUP = 32
SOLVE_MIB = 20
IMAGE_MIB = 12
PITCH = 2 * SG + 1
HALVES = 2
NSUB = ROWS // RPS


def sincos(x):
    y = x * x
    s = jnp.full_like(x, 1.0 / math.factorial(17))
    c = jnp.full_like(x, 1.0 / math.factorial(16))
    for n in range(7, -1, -1):
        s = s * y + (-1) ** n / math.factorial(2 * n + 1)
        c = c * y + (-1) ** n / math.factorial(2 * n)
    return c, s * x


def powers(c, s):
    table = {1: (c, s)}
    for n in range(2, SG // 2 + 1):
        (ca, sa), (cb, sb) = table[n // 2], table[n - n // 2]
        table[n] = (ca * cb - sa * sb, ca * sb + sa * cb)
    return table


def spread(sizes):
    steps = [(i, j) for i in range(sizes[0]) for j in range(sizes[1]) if i or j]
    return sorted(steps, key=lambda t: -sum(min(k, n - k) for k, n in zip(t, sizes)))


PLANE_STEPS = spread((4, 4))
COLUMN_STEPS = spread((4, 2))


def solve_kernel(
    owner_far,
    model_far,
    vis_far,
    pairs_far,
    held_far,
    uv_far,
    gains_out,
    resid,
    across,
    down,
    owner,
    model,
    vis,
    pairs,
    held,
    uv,
    turned,
    coords,
    hot,
    power,
    bterm,
    gram,
    kterm,
    flipped,
    right,
    pairgain,
    mix,
    sums,
    arrived,
    partial,
    chunk,
    rs_send,
    rs_recv,
    ex_send,
    ex_recv,
    ag_send,
    ag_recv,
    loaded,
):
    whole = (
        (owner_far, owner),
        (held_far, held),
        (pairs_far, pairs),
        (uv_far, uv),
        (vis_far, vis),
        (model_far, model),
    )
    loads = [
        pltpu.make_async_copy(far, near, loaded.at[k]) for k, (far, near) in enumerate(whole)
    ]
    for load in loads:
        load.start()
    freq = lax.axis_index("freq")
    bl = lax.axis_index("bl")
    core = lax.rem(bl, 2)
    plane = lax.div(bl, 2)
    column = freq * 2 + core

    def plane_peer(steps):
        first = lax.rem(lax.div(plane, 4) + steps[0], 4)
        second = lax.rem(lax.rem(plane, 4) + steps[1], 4)
        other = first * 4 + second
        return other, (freq, other * 2 + core)

    def column_peer(steps):
        first = lax.rem(freq + steps[0], 4)
        second = lax.rem(core + steps[1], 2)
        return first * 2 + second, (first, plane * 2 + second)

    barrier = pltpu.get_barrier_semaphore()
    for steps in PLANE_STEPS:
        pl.semaphore_signal(barrier, inc=1, device_id=plane_peer(steps)[1], device_id_type=MESH)
    for steps in COLUMN_STEPS:
        pl.semaphore_signal(barrier, inc=1, device_id=column_peer(steps)[1], device_id_type=MESH)

    def exchange(turn, update, column_steps, during_sums, during_gains):
        par = lax.rem(turn, 2)
        reach = len(column_steps)

        def remote(source, into, send, recv, device):
            return pltpu.make_async_remote_copy(
                src_ref=source,
                dst_ref=into,
                send_sem=send,
                recv_sem=recv,
                device_id=device,
                device_id_type=MESH,
            )

        near = plane_peer(PLANE_STEPS[0])[1]
        beside = column_peer(column_steps[0])[1]
        rs_all = remote(sums.at[pl.ds(0, PLANE - 1)], arrived, rs_send, rs_recv, near)
        ex_all = remote(
            partial.at[par, pl.ds(0, reach)],
            partial.at[par, pl.ds(0, reach)],
            ex_send,
            ex_recv.at[par],
            beside,
        )
        ag_all = remote(
            chunk.at[pl.ds(0, PLANE - 1)], chunk.at[pl.ds(0, PLANE - 1)], ag_send, ag_recv, near
        )
        for k, steps in enumerate(PLANE_STEPS):
            other, device = plane_peer(steps)
            remote(sums.at[other], arrived.at[k], rs_send, rs_recv, device).start()
        during_sums()
        rs_all.wait_recv()
        total = sums[plane]
        for k in range(PLANE - 1):
            total = total + arrived[k]
        partial[par, column] = total
        for steps in column_steps:
            _, device = column_peer(steps)
            mine = partial.at[par, column]
            remote(mine, mine, ex_send, ex_recv.at[par], device).start()
        rs_all.wait_send()
        ex_all.wait_recv()
        if reach == COLUMN - 1:
            total = partial[par, 0]
            for m in range(1, COLUMN):
                total = total + partial[par, m]
        else:
            total = partial[par, freq * 2] + partial[par, freq * 2 + 1]
        chunk[plane] = update(total)
        for steps in PLANE_STEPS:
            _, device = plane_peer(steps)
            mine = chunk.at[plane]
            remote(mine, mine, ag_send, ag_recv, device).start()
        during_gains()
        ex_all.wait_send()
        ag_all.wait_recv()
        ag_all.wait_send()

    def pack(interval, table):
        for sb in range(SBLOCKS):
            for dh in range(2):
                for q in range(3):
                    sums[interval * 8 + sb * 2 + dh, q * 8 : q * 8 + 8, :] = table[
                        q * 16 + dh * 8 : q * 16 + dh * 8 + 8, sb * 128 : sb * 128 + 128
                    ]

    def first_update(total):
        scale = 1.0 / total[16:24]
        return jnp.concatenate([total[0:8] * scale, total[8:16] * scale], axis=0)

    def model_at(interval, d, lanes):
        return (
            model[interval, d, 0, :, lanes].astype(F32),
            model[interval, d, 1, :, lanes].astype(F32),
        )

    def lookup_table(interval):
        stations = lax.broadcasted_iota(jnp.int32, (STATIONS, ROWS), 0)
        for end in range(2):
            found = stations == pairs[interval, end : end + 1, :]
            hot[interval, :, end * ROWS : end * ROWS + ROWS] = found.astype(F32).astype(BF16)

    def prepare(interval, first, last):
        def block(index, carry):
            lanes = pl.ds(pl.multiple_of(index * 128, 128), 128)
            vre, vim = vis[interval, 0, :, lanes], vis[interval, 1, :, lanes]

            def direction(d, carry):
                dre, dim = model_at(interval, d, lanes)
                at = pl.ds(d, 1)
                bterm[interval, 0, index, at, :] = jnp.sum(
                    vre * dre + vim * dim, axis=0, keepdims=True
                )
                bterm[interval, 1, index, at, :] = jnp.sum(
                    vim * dre - vre * dim, axis=0, keepdims=True
                )
                strength = jnp.sum(dre * dre + dim * dim, axis=0, keepdims=True)
                power[interval, index, at, :] = strength
                gram[interval, 0, index, d, at, :] = strength
                gram[interval, 1, index, d, at, :] = jnp.zeros_like(strength)
                for step in range(1, DIRS // 2 + 1):
                    e = lax.rem(d + step, DIRS)
                    ere, eim = model_at(interval, e, lanes)
                    re = jnp.sum(ere * dre + eim * dim, axis=0, keepdims=True)
                    im = jnp.sum(eim * dre - ere * dim, axis=0, keepdims=True)
                    gram[interval, 0, index, e, at, :] = re
                    gram[interval, 1, index, e, at, :] = im
                    gram[interval, 0, index, d, pl.ds(e, 1), :] = re
                    gram[interval, 1, index, d, pl.ds(e, 1), :] = -im
                return carry

            lax.fori_loop(0, DIRS, direction, 0)
            return carry

        lax.fori_loop(first, last, block, 0)

    def sample_coords(interval):
        for block in range(ROWS // 128):
            lanes = slice(block * 128, block * 128 + 128)
            padded = jnp.concatenate([uv[interval, :, lanes], jnp.zeros((126, 128), F32)], axis=0)
            turned[lanes, :] = padded.T
        for row in range(RPS):
            coords[interval, row] = turned[pl.ds(row, NSUB, stride=RPS), :]

    for load in loads[:4]:
        load.wait()
    for interval in range(INTERVALS):
        lookup_table(interval)
        sample_coords(interval)
    for interval in range(INTERVALS):
        mine = (owner[interval] == bl).astype(F32)
        pack(
            interval,
            jnp.concatenate([held[interval] * mine, jnp.full((DIRS, STATIONS), mine)], axis=0),
        )

    pl.semaphore_wait(barrier, PLANE - 1 + COLUMN - 1)

    def during_first_sums():
        for load in loads[4:]:
            load.wait()
        prepare(0, 0, 2)

    exchange(0, first_update, [(0, 1)], during_first_sums, lambda: prepare(0, 2, 4))

    def direct(interval):
        def block(index, carry):
            lanes = pl.ds(pl.multiple_of(index * 128, 128), 128)

            rre, rim = vis[interval, 0, :, lanes], vis[interval, 1, :, lanes]
            for d in range(DIRS):
                mre, mim = model_at(interval, d, lanes)
                wre = mix[interval, d : d + 1, lanes]
                wim = mix[interval, d + 16 : d + 17, lanes]
                rre = rre - (wre * mre - wim * mim)
                rim = rim - (wre * mim + wim * mre)

            def correlate(d, carry):
                mre, mim = model_at(interval, d, lanes)
                at = pl.ds(d, 1)
                kterm[0, index, at, :] = jnp.sum(rre * mre + rim * mim, axis=0, keepdims=True)
                kterm[1, index, at, :] = jnp.sum(rim * mre - rre * mim, axis=0, keepdims=True)
                power[interval, index, at, :] = jnp.sum(
                    mre * mre + mim * mim, axis=0, keepdims=True
                )
                return carry

            lax.fori_loop(0, DIRS, correlate, 0, unroll=4)
            return carry

        lax.fori_loop(0, ROWS // 128, block, 0)

    def gather(interval):
        rows = []
        for z in range(2):
            for dh in range(2):
                rows.append(
                    jnp.concatenate(
                        [
                            chunk[interval * 8 + sb * 2 + dh, z * 8 : z * 8 + 8, :]
                            for sb in range(SBLOCKS)
                        ],
                        axis=1,
                    )
                )
        table = jnp.concatenate(rows, axis=0)
        found = jnp.dot(
            jnp.concatenate(split3(table), axis=0), hot[interval], preferred_element_type=F32
        )
        found = found[0:32] + found[32:64] + found[64:96]
        pairgain[interval] = found
        pre, pim = found[0:16, 0:ROWS], found[16:32, 0:ROWS]
        qre, qim = found[0:16, ROWS:], found[16:32, ROWS:]
        mix[interval, 0:16] = pre * qre + pim * qim
        mix[interval, 16:32] = pim * qre - pre * qim
        return table

    def scatter(interval, prepared=True):
        left, right = [], []
        for block in range(ROWS // 128):
            lanes = slice(block * 128, block * 128 + 128)
            if prepared:
                kre, kim = bterm[interval, 0, block], bterm[interval, 1, block]
            else:
                kre, kim = kterm[0, block], kterm[1, block]
            for e in range(DIRS if prepared else 0):
                wre, wim = mix[interval, e : e + 1, lanes], mix[interval, e + 16 : e + 17, lanes]
                are, aim = gram[interval, 0, block, e], gram[interval, 1, block, e]
                kre = kre - (wre * are - wim * aim)
                kim = kim - (wre * aim + wim * are)
            pre, pim = pairgain[interval, 0:16, lanes], pairgain[interval, 16:32, lanes]
            lanes = slice(ROWS + block * 128, ROWS + block * 128 + 128)
            qre, qim = pairgain[interval, 0:16, lanes], pairgain[interval, 16:32, lanes]
            strength = power[interval, block]
            left.append(
                jnp.concatenate(
                    [
                        qre * kre - qim * kim,
                        qre * kim + qim * kre,
                        strength * (qre * qre + qim * qim),
                    ],
                    axis=0,
                )
            )
            right.append(
                jnp.concatenate(
                    [
                        pre * kre + pim * kim,
                        pim * kre - pre * kim,
                        strength * (pre * pre + pim * pim),
                    ],
                    axis=0,
                )
            )
        terms = jnp.concatenate(left + right, axis=1)
        table = lax.dot_general(
            jnp.concatenate(split3(terms), axis=0),
            hot[interval],
            (((1,), (1,)), ((), ())),
            preferred_element_type=F32,
        )
        pack(interval, table[0:48] + table[48:96] + table[96:144])

    def update(total):
        scale = damping / total[16:24]
        return chunk[plane] + jnp.concatenate([total[0:8] * scale, total[8:16] * scale], axis=0)

    lane = lax.broadcasted_iota(jnp.int32, (1, 128), 1)
    low = lane < CH
    channel = (freq * CH + lax.rem(lane, CH)).astype(F32)
    factor = 1.0 + 0.5 * channel / (4 * CH)

    def put(pixel, value):
        for h in range(HALVES):
            right[h, pl.ds(pixel, GROUP, stride=PITCH), :] = value[:, h * 128 : h * 128 + 128]

    def phases(index, carry):
        interval = lax.div(index, NSUB // GROUP)
        first = pl.multiple_of(lax.rem(index, NSUB // GROUP) * GROUP, GROUP)
        rows = pl.ds(first, GROUP)

        def angles(which):
            coord = []
            for h in range(HALVES):
                one = coords[interval, 2 * h, rows, which : which + 1]
                two = coords[interval, 2 * h + 1, rows, which : which + 1]
                coord.append(jnp.where(low, one, two) * factor)
            return powers(*sincos(jnp.concatenate(coord, axis=1) * (2.0 * math.pi / SG)))

        for n, pair in angles(0).items():
            for z in range(2):
                for h in range(HALVES):
                    down[interval, n - 1, z, h, rows, :] = pair[z][:, h * 128 : h * 128 + 128]
        half = SG // 2
        one = jnp.ones((GROUP, HALVES * 128), F32)
        put(half, one)
        put(SG + half, one * 0.0)
        for n, (c, s) in angles(1).items():
            if n < half:
                put(half + n, c)
                put(SG + half + n, s)
            put(half - n, c)
            put(SG + half - n, -s)
        for j in range(GROUP):
            for part in range(2):
                span = slice(j * PITCH + part * SG, j * PITCH + part * SG + SG)
                for h in range(HALVES):
                    lanes = slice(h * 128, h * 128 + 128)
                    value = right[h, span, :]
                    high = value.astype(BF16)
                    across[interval, first + j, 2 * part * SG : 2 * part * SG + SG, lanes] = high
                    across[interval, first + j, 2 * part * SG + SG : 2 * part * SG + 2 * SG, lanes] = (
                        value - high.astype(F32)
                    ).astype(BF16)
        return carry

    groups = INTERVALS * NSUB // GROUP
    each = -(-groups // (2 * (ITERS - 1)))

    def some_phases(slot):
        first = slot * each
        lax.fori_loop(first, jnp.minimum(first + each, groups), phases, 0)

    def iterate(turn, carry):
        for interval in range(INTERVALS):
            gather(interval)
            scatter(interval)
        slot = (turn - 2) * 2
        exchange(
            turn,
            update,
            COLUMN_STEPS,
            lambda: some_phases(slot),
            lambda: some_phases(slot + 1),
        )
        return carry

    for interval in range(INTERVALS):
        gather(interval)
    scatter(0)
    direct(1)
    scatter(1, prepared=False)
    exchange(1, update, COLUMN_STEPS, lambda: prepare(1, 0, 2), lambda: prepare(1, 2, 4))
    lax.fori_loop(2, ITERS + 1, iterate, 0)
    for interval in range(INTERVALS):
        gains_out[interval] = gather(interval)

    def residual(index, carry):
        interval = lax.div(index, 4)
        start = pl.multiple_of(lax.rem(index, 4) * 128, 128)
        lanes = pl.ds(start, 128)
        rre, rim = vis[interval, 0, :, lanes], vis[interval, 1, :, lanes]
        for d in range(DIRS):
            mre, mim = model_at(interval, d, lanes)
            wre = mix[interval, d : d + 1, lanes]
            wim = mix[interval, d + 16 : d + 17, lanes]
            rre = rre - (wre * mre - wim * mim)
            rim = rim - (wre * mim + wim * mre)
        flipped[interval, lanes, :] = jnp.concatenate([rre, rim], axis=0).T
        return carry

    lax.fori_loop(0, INTERVALS * 4, residual, 0)
    scale = 2.0 / (math.sqrt(INTERVALS * NSUB) * math.sqrt(CH * RPS))
    for interval in range(INTERVALS):
        for h in range(HALVES):
            one = flipped[interval, pl.ds(2 * h, NSUB, stride=RPS), :] * scale
            two = flipped[interval, pl.ds(2 * h + 1, NSUB, stride=RPS), :] * scale
            resid[interval, 0, h] = jnp.where(low, one, pltpu.roll(two, 64, axis=1))
            resid[interval, 1, h] = jnp.where(low, pltpu.roll(one, 64, axis=1), two)


def in_hbm(*arrays):
    return [pltpu.with_memory_space_constraint(array, pltpu.HBM) for array in arrays]


def solve(model, visibilities, pairs, held, owner, uv):
    held = held.reshape(INTERVALS, 32, STATIONS)
    pairs = pairs.transpose(0, 2, 1)
    vmem = pl.BlockSpec(memory_space=pltpu.VMEM)
    far = pl.BlockSpec(memory_space=pltpu.HBM)
    return pl.pallas_call(
        solve_kernel,
        out_shape=(
            jax.ShapeDtypeStruct((INTERVALS, 32, STATIONS), F32),
            jax.ShapeDtypeStruct((INTERVALS, 2, HALVES, NSUB, 128), F32),
            jax.ShapeDtypeStruct((INTERVALS, NSUB, 4 * SG, HALVES * 128), BF16),
            jax.ShapeDtypeStruct((INTERVALS, SG // 2, 2, HALVES, NSUB, 128), F32),
        ),
        in_specs=[far] * 6,
        out_specs=(vmem, vmem, vmem, vmem),
        scratch_shapes=[
            pltpu.SMEM((INTERVALS,), jnp.int32),
            pltpu.VMEM((INTERVALS, DIRS, 2, CH, ROWS), BF16),
            pltpu.VMEM((INTERVALS, 2, CH, ROWS), F32),
            pltpu.VMEM((INTERVALS, 2, ROWS), jnp.int32),
            pltpu.VMEM((INTERVALS, 32, STATIONS), F32),
            pltpu.VMEM((INTERVALS, 2, ROWS), F32),
            pltpu.VMEM((ROWS, 128), F32),
            pltpu.VMEM((INTERVALS, RPS, NSUB, 128), F32),
            pltpu.VMEM((INTERVALS, STATIONS, 2 * ROWS), BF16),
            pltpu.VMEM((INTERVALS, ROWS // 128, DIRS, 128), F32),
            pltpu.VMEM((INTERVALS, 2, ROWS // 128, DIRS, 128), F32),
            pltpu.VMEM((INTERVALS, 2, ROWS // 128, DIRS, DIRS, 128), F32),
            pltpu.VMEM((2, ROWS // 128, DIRS, 128), F32),
            pltpu.VMEM((INTERVALS, ROWS, 128), F32),
            pltpu.VMEM((HALVES, GROUP * PITCH, 128), F32),
            pltpu.VMEM((INTERVALS, 32, 2 * ROWS), F32),
            pltpu.VMEM((INTERVALS, 32, ROWS), F32),
            pltpu.VMEM((PLANE, 24, 128), F32),
            pltpu.VMEM((PLANE - 1, 24, 128), F32),
            pltpu.VMEM((2, COLUMN, 24, 128), F32),
            pltpu.VMEM((PLANE, 16, 128), F32),
            pltpu.SemaphoreType.DMA,
            pltpu.SemaphoreType.DMA,
            pltpu.SemaphoreType.DMA,
            pltpu.SemaphoreType.DMA((2,)),
            pltpu.SemaphoreType.DMA,
            pltpu.SemaphoreType.DMA,
            pltpu.SemaphoreType.DMA((6,)),
        ],
        compiler_params=pltpu.CompilerParams(
            collective_id=0, has_side_effects=True, vmem_limit_bytes=SOLVE_MIB * 1024 * 1024
        ),
        name="solve",
    )(*in_hbm(owner, model, visibilities, pairs, held, uv))


def image_kernel(
    owner_far,
    place_far,
    gains,
    resid,
    phase_across,
    phase_down,
    facets,
    gains_out,
    owner,
    place,
    left_even,
    left_odd,
    loaded,
):
    half = SG // 2
    whole = (
        (owner_far, owner),
        (place_far, place),
        (gains, gains_out),
    )
    loads = [
        pltpu.make_async_copy(far, near, loaded.at[k]) for k, (far, near) in enumerate(whole)
    ]
    for load in loads:
        load.start()

    def clear(index, carry):
        facets[index] = jnp.zeros((FACET, 128), F32)
        return carry

    lax.fori_loop(0, facets.shape[0], clear, 0)
    lane = lax.broadcasted_iota(jnp.int32, (1, 128), 1)
    low = lane < 64

    def where(index):
        interval = lax.div(index, NSUB // GROUP)
        return interval, pl.multiple_of(lax.rem(index, NSUB // GROUP) * GROUP, GROUP)

    def operands(index, left):
        interval, first = where(index)
        rows = pl.ds(first, GROUP)
        re = jnp.concatenate([resid[interval, 0, h, rows, :] for h in range(HALVES)], axis=1)
        im = jnp.concatenate([resid[interval, 1, h, rows, :] for h in range(HALVES)], axis=1)

        def put(part, pixel, value):
            for h in range(HALVES):
                left[h, pl.ds(part * SG + pixel, GROUP, stride=PITCH), :] = value[
                    :, h * 128 : h * 128 + 128
                ]

        put(0, half, re)
        put(1, half, im)
        for n in range(1, half + 1):
            c, s = (
                jnp.concatenate(
                    [phase_down[interval, n - 1, z, h, rows, :] for h in range(HALVES)], axis=1
                )
                for z in range(2)
            )
            rc, rs, ic, js = re * c, re * s, im * c, im * s
            if n < half:
                put(0, half + n, rc - js)
                put(1, half + n, rs + ic)
            put(0, half - n, rc + js)
            put(1, half - n, ic - rs)

    def images(index, left):
        interval, first = where(index)
        sign = jnp.where(low, -1.0, 1.0)
        inside = lax.rem(lane, 64) < SG
        for j in range(GROUP):
            span = slice(j * PITCH, j * PITCH + 2 * SG)
            lhs = jnp.concatenate([left[h, span, :] for h in range(HALVES)], axis=1)
            high = lhs.astype(BF16)
            rest = (lhs - high.astype(F32)).astype(BF16)
            both = lax.dot_general(
                jnp.concatenate([high, rest], axis=0),
                phase_across[interval, first + j],
                (((1,), (1,)), ((), ())),
                preferred_element_type=F32,
            )
            real = both[0:SG] + both[2 * SG : 3 * SG]
            imag = both[SG : 2 * SG] + both[3 * SG :]
            image = real + sign * pltpu.roll(imag, 64, axis=1)
            image = image + pltpu.roll(image, 128 - SG, axis=1)
            image = jnp.where(inside, image, 0.0)
            at = owner[interval, first + j]
            at = lax.rem(at, 2) * (facets.shape[0] // 2) + lax.div(at, 2)
            across = place[interval, 1, first + j]
            down = place[interval, 0, first + j]
            image = pltpu.roll(image, across, axis=1)
            facets[at, pl.ds(down, SG), :] += image

    operands(0, left_even)
    for load in loads:
        load.wait()
    groups = INTERVALS * NSUB // GROUP

    def two_groups(index, carry):
        operands(2 * index + 1, left_odd)
        images(2 * index, left_even)
        operands(jnp.minimum(2 * index + 2, groups - 1), left_even)
        images(2 * index + 1, left_odd)
        return carry

    lax.fori_loop(0, groups // 2, two_groups, 0)


def local_facets(gains, resid, phase_across, phase_down, owner, place):
    devices = lax.axis_size("freq") * lax.axis_size("bl")
    owner = owner[:, 0, :, 0]
    place = place[:, 0].transpose(0, 2, 1)
    vmem = pl.BlockSpec(memory_space=pltpu.VMEM)
    far = pl.BlockSpec(memory_space=pltpu.HBM)
    return pl.pallas_call(
        image_kernel,
        out_shape=(
            jax.ShapeDtypeStruct((devices, FACET, 128), F32),
            jax.ShapeDtypeStruct(gains.shape, F32),
        ),
        in_specs=[far] * 2 + [vmem] * 4,
        out_specs=(vmem, far),
        scratch_shapes=[
            pltpu.SMEM((INTERVALS, NSUB), jnp.int32),
            pltpu.SMEM((INTERVALS, 2, NSUB), jnp.int32),
            pltpu.VMEM((HALVES, GROUP * PITCH, 128), F32),
            pltpu.VMEM((HALVES, GROUP * PITCH, 128), F32),
            pltpu.SemaphoreType.DMA((3,)),
        ],
        compiler_params=pltpu.CompilerParams(vmem_limit_bytes=IMAGE_MIB * 1024 * 1024),
        name="image",
    )(*in_hbm(owner, place), gains, resid, phase_across, phase_down)


PARTS = ((0, 24, (0, 1, 2)), (24, 24, (1, 2, 0)), (48, 16, (2, 0, 1)))


def collect_kernel(facets, out, *scratch):
    sibling, one, two, three, s1, s2, s3 = (scratch[3 * n : 3 * n + 3] for n in range(7))
    core_send, core_recv, send, recv = scratch[21:]
    freq = lax.axis_index("freq")
    bl = lax.axis_index("bl")
    core = lax.rem(bl, 2)
    here = (freq, lax.div(bl, 8), lax.rem(lax.div(bl, 2), 4))

    def device(at, core):
        return (at[0], at[1] * 8 + at[2] * 2 + core)

    def peer(axis, step):
        other = lax.rem(here[axis] + step, 4)
        at = list(here)
        at[axis] = other
        return other, device(at, core)

    barrier = pltpu.get_barrier_semaphore()
    pl.semaphore_signal(barrier, inc=1, device_id=device(here, 1 - core), device_id_type=MESH)
    for axis in range(3):
        for step in range(1, 4):
            pl.semaphore_signal(barrier, inc=1, device_id=peer(axis, step)[1], device_id_type=MESH)
    pl.semaphore_wait(barrier, 10)

    def core_copy(p):
        first, rows, _ = PARTS[p]
        return pltpu.make_async_remote_copy(
            src_ref=facets.at[1 - core, :, :, :, pl.ds(first, rows), :],
            dst_ref=sibling[p],
            send_sem=core_send.at[p],
            recv_sem=core_recv.at[p],
            device_id=device(here, 1 - core),
            device_id_type=MESH,
        )

    def stage_copy(stage, p, step):
        axis = PARTS[p][2][stage]
        other, target = peer(axis, step)
        source, into = ((one, s1), (two, s2), (three, s3))[stage]
        return pltpu.make_async_remote_copy(
            src_ref=source[p].at[other],
            dst_ref=into[p].at[step - 1],
            send_sem=send.at[stage, p, step],
            recv_sem=recv.at[stage, p, step],
            device_id=target,
            device_id_type=MESH,
        )

    for p in range(3):
        core_copy(p).start()
    for p in range(3):
        first, rows, order = PARTS[p]
        core_copy(p).wait_recv()

        def add(index, carry, p=p, first=first, rows=rows, order=order):
            at = (lax.div(index, 16), lax.rem(lax.div(index, 4), 4), lax.rem(index, 4))
            i, j, k = (at[axis] for axis in order)
            one[p][i, j, k] = (
                facets[core, at[0], at[1], at[2], pl.ds(first, rows), :]
                + sibling[p][at[0], at[1], at[2]]
            )
            return carry

        lax.fori_loop(0, 64, add, 0, unroll=4)
        for step in range(1, 4):
            stage_copy(0, p, step).start()
    for stage in range(3):
        source, into = ((one, s1), (two, s2), (three, s3))[stage]
        for p in range(3):
            first, rows, order = PARTS[p]
            mine = here[order[stage]]
            for step in range(1, 4):
                stage_copy(stage, p, step).wait_recv()
            total = source[p][mine] + into[p][0] + into[p][1] + into[p][2]
            if stage < 2:
                (two, three)[stage][p][...] = total
                for step in range(1, 4):
                    stage_copy(stage + 1, p, step).start()
            else:
                out[first : first + rows, :] = total
    for p in range(3):
        core_copy(p).wait_send()
        for stage in range(3):
            for step in range(1, 4):
                stage_copy(stage, p, step).wait_send()


def collect(facets):
    vmem = pl.BlockSpec(memory_space=pltpu.VMEM)
    leads = ((4, 4, 4), (4, 4, 4), (4, 4), (4,), (3, 4, 4), (3, 4), (3,))
    return pl.pallas_call(
        collect_kernel,
        out_shape=jax.ShapeDtypeStruct((FACET, 128), F32),
        in_specs=[vmem],
        out_specs=vmem,
        scratch_shapes=[
            pltpu.VMEM(lead + (rows, 128), F32) for lead in leads for _, rows, _ in PARTS
        ]
        + [
            pltpu.SemaphoreType.DMA((3,)),
            pltpu.SemaphoreType.DMA((3,)),
            pltpu.SemaphoreType.DMA((3, 3, 4)),
            pltpu.SemaphoreType.DMA((3, 3, 4)),
        ],
        compiler_params=pltpu.CompilerParams(
            collective_id=1, has_side_effects=True, vmem_limit_bytes=32 * 1024 * 1024
        ),
        name="collect",
    )(facets.reshape(2, 4, 4, 4, FACET, 128))


def body(visibilities, model, pairs, uv, held_gains, solver_owner, facet_owner, subgrid_pos):
    gains, resid, phase_across, phase_down = solve(
        model, visibilities, pairs, held_gains[0], solver_owner, uv
    )
    facets, gains = local_facets(
        gains, resid, phase_across, phase_down, facet_owner, subgrid_pos
    )
    facet = collect(facets)
    facet = facet.reshape(FACET, 2, FACET).transpose(1, 0, 2)
    return (gains.reshape(INTERVALS, 2, DIRS, STATIONS), facet[None, None])


def solution(mesh):
    placed = (
        P(None, None, "freq", "bl"),
        P(None, None, None, "freq", "bl"),
        P(None, "bl", None),
        P(None, None, "bl"),
        P("bl", None, None, None, None),
        P(),
        P(None, "freq", "bl", None),
        P(None, "freq", "bl", None),
    )
    return jax.shard_map(
        body,
        mesh=mesh,
        in_specs=placed,
        out_specs=(P(), P("freq", "bl", None, None, None)),
        check_vma=False,
    )
```

```python
import functools
import math

import jax
import jax.numpy as jnp
from jax import lax
from jax.experimental import pallas as pl
from jax.experimental.pallas import tpu as pltpu
from jax.sharding import PartitionSpec as P

SG = 32
FACET = 64
RPS = 4
ITERS = 4
INTERVALS = 2
DIRS = 16
STATIONS = 512
ROWS = 512
CH = 64
PLANE = 16
COLUMN = 8
SBLOCKS = STATIONS // 128
MESH = pl.DeviceIdType.MESH
F32 = jnp.float32
BF16 = jnp.bfloat16

damping = 0.5


def split3(x):
    hi = x.astype(BF16)
    rest = x - hi.astype(F32)
    mid = rest.astype(BF16)
    low = (rest - mid.astype(F32)).astype(BF16)
    return hi, mid, low


GROUP = 32
SOLVE_MIB = 20
IMAGE_MIB = 12
PITCH = 2 * SG + 1
HALVES = 2
NSUB = ROWS // RPS


def sincos(x):
    y = x * x
    s = jnp.full_like(x, 1.0 / math.factorial(17))
    c = jnp.full_like(x, 1.0 / math.factorial(16))
    for n in range(7, -1, -1):
        s = s * y + (-1) ** n / math.factorial(2 * n + 1)
        c = c * y + (-1) ** n / math.factorial(2 * n)
    return c, s * x


def powers(c, s):
    table = {1: (c, s)}
    for n in range(2, SG // 2 + 1):
        (ca, sa), (cb, sb) = table[n // 2], table[n - n // 2]
        table[n] = (ca * cb - sa * sb, ca * sb + sa * cb)
    return table


def spread(sizes):
    steps = [(i, j) for i in range(sizes[0]) for j in range(sizes[1]) if i or j]
    return sorted(steps, key=lambda t: -sum(min(k, n - k) for k, n in zip(t, sizes)))


PLANE_STEPS = spread((4, 4))
COLUMN_STEPS = spread((4, 2))


def solve_kernel(
    owner_far,
    model_far,
    vis_far,
    pairs_far,
    held_far,
    uv_far,
    gains_out,
    resid,
    across,
    down,
    owner,
    model,
    vis,
    pairs,
    held,
    uv,
    turned,
    coords,
    hot,
    power,
    bterm,
    gram,
    kterm,
    flipped,
    right,
    pairgain,
    mix,
    sums,
    arrived,
    partial,
    chunk,
    rs_send,
    rs_recv,
    ex_send,
    ex_recv,
    ag_send,
    ag_recv,
    loaded,
):
    freq = lax.axis_index("freq")
    bl = lax.axis_index("bl")
    core = lax.rem(bl, 2)
    plane = lax.div(bl, 2)
    column = freq * 2 + core

    def plane_peer(steps):
        first = lax.rem(lax.div(plane, 4) + steps[0], 4)
        second = lax.rem(lax.rem(plane, 4) + steps[1], 4)
        other = first * 4 + second
        return other, (freq, other * 2 + core)

    def column_peer(steps):
        first = lax.rem(freq + steps[0], 4)
        second = lax.rem(core + steps[1], 2)
        return first * 2 + second, (first, plane * 2 + second)

    barrier = pltpu.get_barrier_semaphore()
    for steps in PLANE_STEPS:
        pl.semaphore_signal(barrier, inc=1, device_id=plane_peer(steps)[1], device_id_type=MESH)
    for steps in COLUMN_STEPS:
        pl.semaphore_signal(barrier, inc=1, device_id=column_peer(steps)[1], device_id_type=MESH)
    whole = (
        (owner_far, owner),
        (held_far, held),
        (pairs_far, pairs),
        (uv_far, uv),
        (vis_far, vis),
        (model_far, model),
    )
    loads = [
        pltpu.make_async_copy(far, near, loaded.at[k]) for k, (far, near) in enumerate(whole)
    ]
    for load in loads:
        load.start()

    def exchange(turn, update, column_steps, during_sums, during_gains):
        par = lax.rem(turn, 2)
        reach = len(column_steps)

        def remote(source, into, send, recv, device):
            return pltpu.make_async_remote_copy(
                src_ref=source,
                dst_ref=into,
                send_sem=send,
                recv_sem=recv,
                device_id=device,
                device_id_type=MESH,
            )

        near = plane_peer(PLANE_STEPS[0])[1]
        beside = column_peer(column_steps[0])[1]
        rs_all = remote(sums.at[pl.ds(0, PLANE - 1)], arrived, rs_send, rs_recv, near)
        ex_all = remote(
            partial.at[par, pl.ds(0, reach)],
            partial.at[par, pl.ds(0, reach)],
            ex_send,
            ex_recv.at[par],
            beside,
        )
        ag_all = remote(
            chunk.at[pl.ds(0, PLANE - 1)], chunk.at[pl.ds(0, PLANE - 1)], ag_send, ag_recv, near
        )
        for k, steps in enumerate(PLANE_STEPS):
            other, device = plane_peer(steps)
            remote(sums.at[other], arrived.at[k], rs_send, rs_recv, device).start()
        during_sums()
        rs_all.wait_recv()
        total = sums[plane]
        for k in range(PLANE - 1):
            total = total + arrived[k]
        partial[par, column] = total
        for steps in column_steps:
            _, device = column_peer(steps)
            mine = partial.at[par, column]
            remote(mine, mine, ex_send, ex_recv.at[par], device).start()
        rs_all.wait_send()
        ex_all.wait_recv()
        if reach == COLUMN - 1:
            total = partial[par, 0]
            for m in range(1, COLUMN):
                total = total + partial[par, m]
        else:
            total = partial[par, freq * 2] + partial[par, freq * 2 + 1]
        chunk[plane] = update(total)
        for steps in PLANE_STEPS:
            _, device = plane_peer(steps)
            mine = chunk.at[plane]
            remote(mine, mine, ag_send, ag_recv, device).start()
        during_gains()
        ex_all.wait_send()
        ag_all.wait_recv()
        ag_all.wait_send()

    def pack(interval, table):
        for sb in range(SBLOCKS):
            for dh in range(2):
                for q in range(3):
                    sums[interval * 8 + sb * 2 + dh, q * 8 : q * 8 + 8, :] = table[
                        q * 16 + dh * 8 : q * 16 + dh * 8 + 8, sb * 128 : sb * 128 + 128
                    ]

    def first_update(total):
        scale = 1.0 / total[16:24]
        return jnp.concatenate([total[0:8] * scale, total[8:16] * scale], axis=0)

    def model_at(interval, d, lanes):
        return (
            model[interval, d, 0, :, lanes].astype(F32),
            model[interval, d, 1, :, lanes].astype(F32),
        )

    def lookup_table(interval):
        stations = lax.broadcasted_iota(jnp.int32, (STATIONS, ROWS), 0)
        for end in range(2):
            found = stations == pairs[interval, end : end + 1, :]
            hot[interval, :, end * ROWS : end * ROWS + ROWS] = found.astype(F32).astype(BF16)

    def prepare(interval, first, last):
        def block(index, carry):
            lanes = pl.ds(pl.multiple_of(index * 128, 128), 128)
            vre, vim = vis[interval, 0, :, lanes], vis[interval, 1, :, lanes]

            def direction(d, carry):
                dre, dim = model_at(interval, d, lanes)
                at = pl.ds(d, 1)
                bterm[interval, 0, index, at, :] = jnp.sum(
                    vre * dre + vim * dim, axis=0, keepdims=True
                )
                bterm[interval, 1, index, at, :] = jnp.sum(
                    vim * dre - vre * dim, axis=0, keepdims=True
                )
                strength = jnp.sum(dre * dre + dim * dim, axis=0, keepdims=True)
                power[interval, index, at, :] = strength
                gram[interval, 0, index, d, at, :] = strength
                gram[interval, 1, index, d, at, :] = jnp.zeros_like(strength)
                for step in range(1, DIRS // 2 + 1):
                    e = lax.rem(d + step, DIRS)
                    ere, eim = model_at(interval, e, lanes)
                    re = jnp.sum(ere * dre + eim * dim, axis=0, keepdims=True)
                    im = jnp.sum(eim * dre - ere * dim, axis=0, keepdims=True)
                    gram[interval, 0, index, e, at, :] = re
                    gram[interval, 1, index, e, at, :] = im
                    gram[interval, 0, index, d, pl.ds(e, 1), :] = re
                    gram[interval, 1, index, d, pl.ds(e, 1), :] = -im
                return carry

            lax.fori_loop(0, DIRS, direction, 0)
            return carry

        lax.fori_loop(first, last, block, 0)

    def sample_coords(interval):
        for block in range(ROWS // 128):
            lanes = slice(block * 128, block * 128 + 128)
            padded = jnp.concatenate([uv[interval, :, lanes], jnp.zeros((126, 128), F32)], axis=0)
            turned[lanes, :] = padded.T
        for row in range(RPS):
            coords[interval, row] = turned[pl.ds(row, NSUB, stride=RPS), :]

    for load in loads[:4]:
        load.wait()
    for interval in range(INTERVALS):
        lookup_table(interval)
        sample_coords(interval)
    for interval in range(INTERVALS):
        mine = (owner[interval] == bl).astype(F32)
        pack(
            interval,
            jnp.concatenate([held[interval] * mine, jnp.full((DIRS, STATIONS), mine)], axis=0),
        )

    pl.semaphore_wait(barrier, PLANE - 1 + COLUMN - 1)

    def during_first_sums():
        for load in loads[4:]:
            load.wait()
        prepare(0, 0, 2)

    exchange(0, first_update, [(0, 1)], during_first_sums, lambda: prepare(0, 2, 4))

    def direct(interval):
        def block(index, carry):
            lanes = pl.ds(pl.multiple_of(index * 128, 128), 128)

            rre, rim = vis[interval, 0, :, lanes], vis[interval, 1, :, lanes]
            for d in range(DIRS):
                mre, mim = model_at(interval, d, lanes)
                wre = mix[interval, d : d + 1, lanes]
                wim = mix[interval, d + 16 : d + 17, lanes]
                rre = rre - (wre * mre - wim * mim)
                rim = rim - (wre * mim + wim * mre)

            def correlate(d, carry):
                mre, mim = model_at(interval, d, lanes)
                at = pl.ds(d, 1)
                kterm[0, index, at, :] = jnp.sum(rre * mre + rim * mim, axis=0, keepdims=True)
                kterm[1, index, at, :] = jnp.sum(rim * mre - rre * mim, axis=0, keepdims=True)
                power[interval, index, at, :] = jnp.sum(
                    mre * mre + mim * mim, axis=0, keepdims=True
                )
                return carry

            lax.fori_loop(0, DIRS, correlate, 0, unroll=4)
            return carry

        lax.fori_loop(0, ROWS // 128, block, 0)

    def gather(interval):
        rows = []
        for z in range(2):
            for dh in range(2):
                rows.append(
                    jnp.concatenate(
                        [
                            chunk[interval * 8 + sb * 2 + dh, z * 8 : z * 8 + 8, :]
                            for sb in range(SBLOCKS)
                        ],
                        axis=1,
                    )
                )
        table = jnp.concatenate(rows, axis=0)
        found = jnp.dot(
            jnp.concatenate(split3(table), axis=0), hot[interval], preferred_element_type=F32
        )
        found = found[0:32] + found[32:64] + found[64:96]
        pairgain[interval] = found
        pre, pim = found[0:16, 0:ROWS], found[16:32, 0:ROWS]
        qre, qim = found[0:16, ROWS:], found[16:32, ROWS:]
        mix[interval, 0:16] = pre * qre + pim * qim
        mix[interval, 16:32] = pim * qre - pre * qim
        return table

    def scatter(interval, prepared=True):
        left, right = [], []
        for block in range(ROWS // 128):
            lanes = slice(block * 128, block * 128 + 128)
            if prepared:
                kre, kim = bterm[interval, 0, block], bterm[interval, 1, block]
            else:
                kre, kim = kterm[0, block], kterm[1, block]
            for e in range(DIRS if prepared else 0):
                wre, wim = mix[interval, e : e + 1, lanes], mix[interval, e + 16 : e + 17, lanes]
                are, aim = gram[interval, 0, block, e], gram[interval, 1, block, e]
                kre = kre - (wre * are - wim * aim)
                kim = kim - (wre * aim + wim * are)
            pre, pim = pairgain[interval, 0:16, lanes], pairgain[interval, 16:32, lanes]
            lanes = slice(ROWS + block * 128, ROWS + block * 128 + 128)
            qre, qim = pairgain[interval, 0:16, lanes], pairgain[interval, 16:32, lanes]
            strength = power[interval, block]
            left.append(
                jnp.concatenate(
                    [
                        qre * kre - qim * kim,
                        qre * kim + qim * kre,
                        strength * (qre * qre + qim * qim),
                    ],
                    axis=0,
                )
            )
            right.append(
                jnp.concatenate(
                    [
                        pre * kre + pim * kim,
                        pim * kre - pre * kim,
                        strength * (pre * pre + pim * pim),
                    ],
                    axis=0,
                )
            )
        terms = jnp.concatenate(left + right, axis=1)
        table = lax.dot_general(
            jnp.concatenate(split3(terms), axis=0),
            hot[interval],
            (((1,), (1,)), ((), ())),
            preferred_element_type=F32,
        )
        pack(interval, table[0:48] + table[48:96] + table[96:144])

    def update(total):
        scale = damping / total[16:24]
        return chunk[plane] + jnp.concatenate([total[0:8] * scale, total[8:16] * scale], axis=0)

    lane = lax.broadcasted_iota(jnp.int32, (1, 128), 1)
    low = lane < CH
    channel = (freq * CH + lax.rem(lane, CH)).astype(F32)
    factor = 1.0 + 0.5 * channel / (4 * CH)

    def put(pixel, value):
        for h in range(HALVES):
            right[h, pl.ds(pixel, GROUP, stride=PITCH), :] = value[:, h * 128 : h * 128 + 128]

    def phases(index, carry):
        interval = lax.div(index, NSUB // GROUP)
        first = pl.multiple_of(lax.rem(index, NSUB // GROUP) * GROUP, GROUP)
        rows = pl.ds(first, GROUP)

        def angles(which):
            coord = []
            for h in range(HALVES):
                one = coords[interval, 2 * h, rows, which : which + 1]
                two = coords[interval, 2 * h + 1, rows, which : which + 1]
                coord.append(jnp.where(low, one, two) * factor)
            return powers(*sincos(jnp.concatenate(coord, axis=1) * (2.0 * math.pi / SG)))

        for n, pair in angles(0).items():
            for z in range(2):
                for h in range(HALVES):
                    down[interval, n - 1, z, h, rows, :] = pair[z][:, h * 128 : h * 128 + 128]
        half = SG // 2
        one = jnp.ones((GROUP, HALVES * 128), F32)
        put(half, one)
        put(SG + half, one * 0.0)
        for n, (c, s) in angles(1).items():
            if n < half:
                put(half + n, c)
                put(SG + half + n, s)
            put(half - n, c)
            put(SG + half - n, -s)
        for j in range(GROUP):
            for part in range(2):
                span = slice(j * PITCH + part * SG, j * PITCH + part * SG + SG)
                for h in range(HALVES):
                    lanes = slice(h * 128, h * 128 + 128)
                    value = right[h, span, :]
                    high = value.astype(BF16)
                    across[interval, first + j, 2 * part * SG : 2 * part * SG + SG, lanes] = high
                    across[interval, first + j, 2 * part * SG + SG : 2 * part * SG + 2 * SG, lanes] = (
                        value - high.astype(F32)
                    ).astype(BF16)
        return carry

    groups = INTERVALS * NSUB // GROUP
    slots = 2 * (ITERS - 1)

    def some_phases(slot):
        first = lax.div(slot * groups, slots)
        last = lax.div((slot + 1) * groups, slots)
        lax.fori_loop(first, last, phases, 0)

    def iterate(turn, carry):
        for interval in range(INTERVALS):
            gather(interval)
            scatter(interval)
        slot = (turn - 2) * 2
        exchange(
            turn,
            update,
            COLUMN_STEPS,
            lambda: some_phases(slot),
            lambda: some_phases(slot + 1),
        )
        return carry

    for interval in range(INTERVALS):
        gather(interval)
    scatter(0)
    direct(1)
    scatter(1, prepared=False)
    exchange(1, update, COLUMN_STEPS, lambda: prepare(1, 0, 2), lambda: prepare(1, 2, 4))
    lax.fori_loop(2, ITERS + 1, iterate, 0)
    for interval in range(INTERVALS):
        gains_out[interval] = gather(interval)

    def residual(index, carry):
        interval = lax.div(index, 4)
        start = pl.multiple_of(lax.rem(index, 4) * 128, 128)
        lanes = pl.ds(start, 128)
        rre, rim = vis[interval, 0, :, lanes], vis[interval, 1, :, lanes]
        for d in range(DIRS):
            mre, mim = model_at(interval, d, lanes)
            wre = mix[interval, d : d + 1, lanes]
            wim = mix[interval, d + 16 : d + 17, lanes]
            rre = rre - (wre * mre - wim * mim)
            rim = rim - (wre * mim + wim * mre)
        flipped[interval, lanes, :] = jnp.concatenate([rre, rim], axis=0).T
        return carry

    lax.fori_loop(0, INTERVALS * 4, residual, 0)
    scale = 2.0 / (math.sqrt(INTERVALS * NSUB) * math.sqrt(CH * RPS))
    for interval in range(INTERVALS):
        for h in range(HALVES):
            one = flipped[interval, pl.ds(2 * h, NSUB, stride=RPS), :] * scale
            two = flipped[interval, pl.ds(2 * h + 1, NSUB, stride=RPS), :] * scale
            resid[interval, 0, h] = jnp.where(low, one, pltpu.roll(two, 64, axis=1))
            resid[interval, 1, h] = jnp.where(low, pltpu.roll(one, 64, axis=1), two)


def in_hbm(*arrays):
    return [pltpu.with_memory_space_constraint(array, pltpu.HBM) for array in arrays]


def solve(model, visibilities, pairs, held, owner, uv):
    held = held.reshape(INTERVALS, 32, STATIONS)
    pairs = pairs.transpose(0, 2, 1)
    vmem = pl.BlockSpec(memory_space=pltpu.VMEM)
    far = pl.BlockSpec(memory_space=pltpu.HBM)
    return pl.pallas_call(
        solve_kernel,
        out_shape=(
            jax.ShapeDtypeStruct((INTERVALS, 32, STATIONS), F32),
            jax.ShapeDtypeStruct((INTERVALS, 2, HALVES, NSUB, 128), F32),
            jax.ShapeDtypeStruct((INTERVALS, NSUB, 4 * SG, HALVES * 128), BF16),
            jax.ShapeDtypeStruct((INTERVALS, SG // 2, 2, HALVES, NSUB, 128), F32),
        ),
        in_specs=[far] * 6,
        out_specs=(vmem, vmem, vmem, vmem),
        scratch_shapes=[
            pltpu.SMEM((INTERVALS,), jnp.int32),
            pltpu.VMEM((INTERVALS, DIRS, 2, CH, ROWS), BF16),
            pltpu.VMEM((INTERVALS, 2, CH, ROWS), F32),
            pltpu.VMEM((INTERVALS, 2, ROWS), jnp.int32),
            pltpu.VMEM((INTERVALS, 32, STATIONS), F32),
            pltpu.VMEM((INTERVALS, 2, ROWS), F32),
            pltpu.VMEM((ROWS, 128), F32),
            pltpu.VMEM((INTERVALS, RPS, NSUB, 128), F32),
            pltpu.VMEM((INTERVALS, STATIONS, 2 * ROWS), BF16),
            pltpu.VMEM((INTERVALS, ROWS // 128, DIRS, 128), F32),
            pltpu.VMEM((INTERVALS, 2, ROWS // 128, DIRS, 128), F32),
            pltpu.VMEM((INTERVALS, 2, ROWS // 128, DIRS, DIRS, 128), F32),
            pltpu.VMEM((2, ROWS // 128, DIRS, 128), F32),
            pltpu.VMEM((INTERVALS, ROWS, 128), F32),
            pltpu.VMEM((HALVES, GROUP * PITCH, 128), F32),
            pltpu.VMEM((INTERVALS, 32, 2 * ROWS), F32),
            pltpu.VMEM((INTERVALS, 32, ROWS), F32),
            pltpu.VMEM((PLANE, 24, 128), F32),
            pltpu.VMEM((PLANE - 1, 24, 128), F32),
            pltpu.VMEM((2, COLUMN, 24, 128), F32),
            pltpu.VMEM((PLANE, 16, 128), F32),
            pltpu.SemaphoreType.DMA,
            pltpu.SemaphoreType.DMA,
            pltpu.SemaphoreType.DMA,
            pltpu.SemaphoreType.DMA((2,)),
            pltpu.SemaphoreType.DMA,
            pltpu.SemaphoreType.DMA,
            pltpu.SemaphoreType.DMA((6,)),
        ],
        compiler_params=pltpu.CompilerParams(
            collective_id=0, has_side_effects=True, vmem_limit_bytes=SOLVE_MIB * 1024 * 1024
        ),
        name="solve",
    )(*in_hbm(owner, model, visibilities, pairs, held, uv))


def image_kernel(
    owner_far,
    place_far,
    gains,
    resid,
    phase_across,
    phase_down,
    facets,
    gains_out,
    owner,
    place,
    left_even,
    left_odd,
    loaded,
):
    half = SG // 2
    whole = (
        (owner_far, owner),
        (place_far, place),
        (gains, gains_out),
    )
    loads = [
        pltpu.make_async_copy(far, near, loaded.at[k]) for k, (far, near) in enumerate(whole)
    ]
    for load in loads:
        load.start()

    def clear(index, carry):
        facets[index] = jnp.zeros((FACET, 128), F32)
        return carry

    lax.fori_loop(0, facets.shape[0], clear, 0)
    lane = lax.broadcasted_iota(jnp.int32, (1, 128), 1)
    low = lane < 64

    def where(index):
        interval = lax.div(index, NSUB // GROUP)
        return interval, pl.multiple_of(lax.rem(index, NSUB // GROUP) * GROUP, GROUP)

    def operands(index, left):
        interval, first = where(index)
        rows = pl.ds(first, GROUP)
        re = jnp.concatenate([resid[interval, 0, h, rows, :] for h in range(HALVES)], axis=1)
        im = jnp.concatenate([resid[interval, 1, h, rows, :] for h in range(HALVES)], axis=1)

        def put(part, pixel, value):
            for h in range(HALVES):
                left[h, pl.ds(part * SG + pixel, GROUP, stride=PITCH), :] = value[
                    :, h * 128 : h * 128 + 128
                ]

        put(0, half, re)
        put(1, half, im)
        for n in range(1, half + 1):
            c, s = (
                jnp.concatenate(
                    [phase_down[interval, n - 1, z, h, rows, :] for h in range(HALVES)], axis=1
                )
                for z in range(2)
            )
            rc, rs, ic, js = re * c, re * s, im * c, im * s
            if n < half:
                put(0, half + n, rc - js)
                put(1, half + n, rs + ic)
            put(0, half - n, rc + js)
            put(1, half - n, ic - rs)

    def images(index, left):
        interval, first = where(index)
        sign = jnp.where(low, -1.0, 1.0)
        inside = lax.rem(lane, 64) < SG
        for j in range(GROUP):
            span = slice(j * PITCH, j * PITCH + 2 * SG)
            lhs = jnp.concatenate([left[h, span, :] for h in range(HALVES)], axis=1)
            high = lhs.astype(BF16)
            rest = (lhs - high.astype(F32)).astype(BF16)
            both = lax.dot_general(
                jnp.concatenate([high, rest], axis=0),
                phase_across[interval, first + j],
                (((1,), (1,)), ((), ())),
                preferred_element_type=F32,
            )
            real = both[0:SG] + both[2 * SG : 3 * SG]
            imag = both[SG : 2 * SG] + both[3 * SG :]
            image = real + sign * pltpu.roll(imag, 64, axis=1)
            image = image + pltpu.roll(image, 128 - SG, axis=1)
            image = jnp.where(inside, image, 0.0)
            at = owner[interval, first + j]
            at = lax.rem(at, 2) * (facets.shape[0] // 2) + lax.div(at, 2)
            across = place[interval, 1, first + j]
            down = place[interval, 0, first + j]
            image = pltpu.roll(image, across, axis=1)
            facets[at, pl.ds(down, SG), :] += image

    operands(0, left_even)
    for load in loads:
        load.wait()
    groups = INTERVALS * NSUB // GROUP

    def two_groups(index, carry):
        operands(2 * index + 1, left_odd)
        images(2 * index, left_even)
        operands(jnp.minimum(2 * index + 2, groups - 1), left_even)
        images(2 * index + 1, left_odd)
        return carry

    lax.fori_loop(0, groups // 2, two_groups, 0)


def local_facets(gains, resid, phase_across, phase_down, owner, place):
    devices = lax.axis_size("freq") * lax.axis_size("bl")
    owner = owner[:, 0, :, 0]
    place = place[:, 0].transpose(0, 2, 1)
    vmem = pl.BlockSpec(memory_space=pltpu.VMEM)
    far = pl.BlockSpec(memory_space=pltpu.HBM)
    return pl.pallas_call(
        image_kernel,
        out_shape=(
            jax.ShapeDtypeStruct((devices, FACET, 128), F32),
            jax.ShapeDtypeStruct(gains.shape, F32),
        ),
        in_specs=[far] * 2 + [vmem] * 4,
        out_specs=(vmem, far),
        scratch_shapes=[
            pltpu.SMEM((INTERVALS, NSUB), jnp.int32),
            pltpu.SMEM((INTERVALS, 2, NSUB), jnp.int32),
            pltpu.VMEM((HALVES, GROUP * PITCH, 128), F32),
            pltpu.VMEM((HALVES, GROUP * PITCH, 128), F32),
            pltpu.SemaphoreType.DMA((3,)),
        ],
        compiler_params=pltpu.CompilerParams(vmem_limit_bytes=IMAGE_MIB * 1024 * 1024),
        name="image",
    )(*in_hbm(owner, place), gains, resid, phase_across, phase_down)


PARTS = ((0, 24, (0, 1, 2)), (24, 24, (1, 2, 0)), (48, 16, (2, 0, 1)))


def collect_kernel(facets, out, *scratch):
    sibling, one, two, three, s1, s2, s3 = (scratch[3 * n : 3 * n + 3] for n in range(7))
    core_send, core_recv, send, recv = scratch[21:]
    freq = lax.axis_index("freq")
    bl = lax.axis_index("bl")
    core = lax.rem(bl, 2)
    here = (freq, lax.div(bl, 8), lax.rem(lax.div(bl, 2), 4))

    def device(at, core):
        return (at[0], at[1] * 8 + at[2] * 2 + core)

    def peer(axis, step):
        other = lax.rem(here[axis] + step, 4)
        at = list(here)
        at[axis] = other
        return other, device(at, core)

    barrier = pltpu.get_barrier_semaphore()
    pl.semaphore_signal(barrier, inc=1, device_id=device(here, 1 - core), device_id_type=MESH)
    for axis in range(3):
        for step in range(1, 4):
            pl.semaphore_signal(barrier, inc=1, device_id=peer(axis, step)[1], device_id_type=MESH)
    pl.semaphore_wait(barrier, 10)

    def core_copy(p):
        first, rows, _ = PARTS[p]
        return pltpu.make_async_remote_copy(
            src_ref=facets.at[1 - core, :, :, :, pl.ds(first, rows), :],
            dst_ref=sibling[p],
            send_sem=core_send.at[p],
            recv_sem=core_recv.at[p],
            device_id=device(here, 1 - core),
            device_id_type=MESH,
        )

    def stage_copy(stage, p, step):
        axis = PARTS[p][2][stage]
        other, target = peer(axis, step)
        source, into = ((one, s1), (two, s2), (three, s3))[stage]
        return pltpu.make_async_remote_copy(
            src_ref=source[p].at[other],
            dst_ref=into[p].at[step - 1],
            send_sem=send.at[stage, p, step],
            recv_sem=recv.at[stage, p, step],
            device_id=target,
            device_id_type=MESH,
        )

    for p in range(3):
        core_copy(p).start()
    for p in range(3):
        first, rows, order = PARTS[p]
        core_copy(p).wait_recv()

        rows = pl.ds(first, rows)
        for x in range(4):
            if order == (0, 1, 2):
                one[p][x] = facets[core, x, :, :, rows, :] + sibling[p][x]
            elif order == (1, 2, 0):
                one[p][:, :, x] = facets[core, x, :, :, rows, :] + sibling[p][x]
            else:
                for z in range(4):
                    one[p][:, x, z] = facets[core, x, z, :, rows, :] + sibling[p][x, z]
        for step in (2, 1, 3):
            stage_copy(0, p, step).start()
    for stage in range(3):
        source, into = ((one, s1), (two, s2), (three, s3))[stage]
        for p in range(3):
            first, rows, order = PARTS[p]
            mine = here[order[stage]]
            for step in range(1, 4):
                stage_copy(stage, p, step).wait_recv()
            total = source[p][mine] + into[p][0] + into[p][1] + into[p][2]
            if stage < 2:
                (two, three)[stage][p][...] = total
                for step in (2, 1, 3):
                    stage_copy(stage + 1, p, step).start()
            else:
                out[first : first + rows, :] = total
    for p in range(3):
        core_copy(p).wait_send()
        for stage in range(3):
            for step in range(1, 4):
                stage_copy(stage, p, step).wait_send()


def collect(facets):
    vmem = pl.BlockSpec(memory_space=pltpu.VMEM)
    leads = ((4, 4, 4), (4, 4, 4), (4, 4), (4,), (3, 4, 4), (3, 4), (3,))
    return pl.pallas_call(
        collect_kernel,
        out_shape=jax.ShapeDtypeStruct((FACET, 128), F32),
        in_specs=[vmem],
        out_specs=vmem,
        scratch_shapes=[
            pltpu.VMEM(lead + (rows, 128), F32) for lead in leads for _, rows, _ in PARTS
        ]
        + [
            pltpu.SemaphoreType.DMA((3,)),
            pltpu.SemaphoreType.DMA((3,)),
            pltpu.SemaphoreType.DMA((3, 3, 4)),
            pltpu.SemaphoreType.DMA((3, 3, 4)),
        ],
        compiler_params=pltpu.CompilerParams(
            collective_id=1, has_side_effects=True, vmem_limit_bytes=32 * 1024 * 1024
        ),
        name="collect",
    )(facets.reshape(2, 4, 4, 4, FACET, 128))


def body(visibilities, model, pairs, uv, held_gains, solver_owner, facet_owner, subgrid_pos):
    gains, resid, phase_across, phase_down = solve(
        model, visibilities, pairs, held_gains[0], solver_owner, uv
    )
    facets, gains = local_facets(
        gains, resid, phase_across, phase_down, facet_owner, subgrid_pos
    )
    facet = collect(facets)
    facet = facet.reshape(FACET, 2, FACET).transpose(1, 0, 2)
    return (gains.reshape(INTERVALS, 2, DIRS, STATIONS), facet[None, None])


def solution(mesh):
    placed = (
        P(None, None, "freq", "bl"),
        P(None, None, None, "freq", "bl"),
        P(None, "bl", None),
        P(None, None, "bl"),
        P("bl", None, None, None, None),
        P(),
        P(None, "freq", "bl", None),
        P(None, "freq", "bl", None),
    )
    return jax.shard_map(
        body,
        mesh=mesh,
        in_specs=placed,
        out_specs=(P(), P("freq", "bl", None, None, None)),
        check_vma=False,
    )
```

```python
import functools
import math

import jax
import jax.numpy as jnp
from jax import lax
from jax.experimental import pallas as pl
from jax.experimental.pallas import tpu as pltpu
from jax.sharding import PartitionSpec as P

SG = 32
FACET = 64
RPS = 4
ITERS = 4
INTERVALS = 2
DIRS = 16
STATIONS = 512
ROWS = 512
CH = 64
PLANE = 16
COLUMN = 8
SBLOCKS = STATIONS // 128
MESH = pl.DeviceIdType.MESH
F32 = jnp.float32
BF16 = jnp.bfloat16

damping = 0.5


def split3(x):
    hi = x.astype(BF16)
    rest = x - hi.astype(F32)
    mid = rest.astype(BF16)
    low = (rest - mid.astype(F32)).astype(BF16)
    return hi, mid, low


GROUP = 32
SOLVE_MIB = 20
IMAGE_MIB = 12
PITCH = 2 * SG + 1
HALVES = 2
NSUB = ROWS // RPS


def sincos(x):
    y = x * x
    s = jnp.full_like(x, 1.0 / math.factorial(17))
    c = jnp.full_like(x, 1.0 / math.factorial(16))
    for n in range(7, -1, -1):
        s = s * y + (-1) ** n / math.factorial(2 * n + 1)
        c = c * y + (-1) ** n / math.factorial(2 * n)
    return c, s * x


def powers(c, s):
    table = {1: (c, s)}
    for n in range(2, SG // 2 + 1):
        (ca, sa), (cb, sb) = table[n // 2], table[n - n // 2]
        table[n] = (ca * cb - sa * sb, ca * sb + sa * cb)
    return table


def spread(sizes):
    steps = [(i, j) for i in range(sizes[0]) for j in range(sizes[1]) if i or j]
    return sorted(steps, key=lambda t: -sum(min(k, n - k) for k, n in zip(t, sizes)))


PLANE_STEPS = spread((4, 4))
COLUMN_STEPS = spread((4, 2))


def solve_kernel(
    owner_far,
    model_far,
    vis_far,
    pairs_far,
    held_far,
    uv_far,
    gains_out,
    resid,
    across,
    down,
    owner,
    model,
    vis,
    pairs,
    held,
    uv,
    turned,
    coords,
    hot,
    power,
    bterm,
    gram,
    kterm,
    flipped,
    right,
    pairgain,
    mix,
    sums,
    arrived,
    partial,
    chunk,
    rs_send,
    rs_recv,
    ex_send,
    ex_recv,
    ag_send,
    ag_recv,
    loaded,
):
    freq = lax.axis_index("freq")
    bl = lax.axis_index("bl")
    core = lax.rem(bl, 2)
    plane = lax.div(bl, 2)
    column = freq * 2 + core

    def plane_peer(steps):
        first = lax.rem(lax.div(plane, 4) + steps[0], 4)
        second = lax.rem(lax.rem(plane, 4) + steps[1], 4)
        other = first * 4 + second
        return other, (freq, other * 2 + core)

    def column_peer(steps):
        first = lax.rem(freq + steps[0], 4)
        second = lax.rem(core + steps[1], 2)
        return first * 2 + second, (first, plane * 2 + second)

    barrier = pltpu.get_barrier_semaphore()
    for steps in PLANE_STEPS:
        pl.semaphore_signal(barrier, inc=1, device_id=plane_peer(steps)[1], device_id_type=MESH)
    for steps in COLUMN_STEPS:
        pl.semaphore_signal(barrier, inc=1, device_id=column_peer(steps)[1], device_id_type=MESH)
    whole = (
        (owner_far, owner),
        (held_far, held),
        (pairs_far, pairs),
        (uv_far, uv),
        (vis_far, vis),
        (model_far, model),
    )
    loads = [
        pltpu.make_async_copy(far, near, loaded.at[k]) for k, (far, near) in enumerate(whole)
    ]
    for load in loads:
        load.start()

    def exchange(turn, update, column_steps, during_sums, during_gains):
        par = lax.rem(turn, 2)
        reach = len(column_steps)

        def remote(source, into, send, recv, device):
            return pltpu.make_async_remote_copy(
                src_ref=source,
                dst_ref=into,
                send_sem=send,
                recv_sem=recv,
                device_id=device,
                device_id_type=MESH,
            )

        near = plane_peer(PLANE_STEPS[0])[1]
        beside = column_peer(column_steps[0])[1]
        rs_all = remote(sums.at[pl.ds(0, PLANE - 1)], arrived, rs_send, rs_recv, near)
        ex_all = remote(
            partial.at[par, pl.ds(0, reach)],
            partial.at[par, pl.ds(0, reach)],
            ex_send,
            ex_recv.at[par],
            beside,
        )
        ag_all = remote(
            chunk.at[pl.ds(0, PLANE - 1)], chunk.at[pl.ds(0, PLANE - 1)], ag_send, ag_recv, near
        )
        for k, steps in enumerate(PLANE_STEPS):
            other, device = plane_peer(steps)
            remote(sums.at[other], arrived.at[k], rs_send, rs_recv, device).start()
        during_sums()
        rs_all.wait_recv()
        total = sums[plane]
        for k in range(PLANE - 1):
            total = total + arrived[k]
        partial[par, column] = total
        for steps in column_steps:
            _, device = column_peer(steps)
            mine = partial.at[par, column]
            remote(mine, mine, ex_send, ex_recv.at[par], device).start()
        rs_all.wait_send()
        ex_all.wait_recv()
        if reach == COLUMN - 1:
            total = partial[par, 0]
            for m in range(1, COLUMN):
                total = total + partial[par, m]
        else:
            total = partial[par, freq * 2] + partial[par, freq * 2 + 1]
        chunk[plane] = update(total)
        for steps in PLANE_STEPS:
            _, device = plane_peer(steps)
            mine = chunk.at[plane]
            remote(mine, mine, ag_send, ag_recv, device).start()
        during_gains()
        ex_all.wait_send()
        ag_all.wait_recv()
        ag_all.wait_send()

    def pack(interval, table):
        for sb in range(SBLOCKS):
            for dh in range(2):
                for q in range(3):
                    sums[interval * 8 + sb * 2 + dh, q * 8 : q * 8 + 8, :] = table[
                        q * 16 + dh * 8 : q * 16 + dh * 8 + 8, sb * 128 : sb * 128 + 128
                    ]

    def first_update(total):
        scale = 1.0 / total[16:24]
        return jnp.concatenate([total[0:8] * scale, total[8:16] * scale], axis=0)

    def model_at(interval, d, lanes):
        return (
            model[interval, d, 0, :, lanes].astype(F32),
            model[interval, d, 1, :, lanes].astype(F32),
        )

    def lookup_table(interval):
        stations = lax.broadcasted_iota(jnp.int32, (STATIONS, ROWS), 0)
        for end in range(2):
            found = stations == pairs[interval, end : end + 1, :]
            hot[interval, :, end * ROWS : end * ROWS + ROWS] = found.astype(F32).astype(BF16)

    def prepare(interval, first, last):
        def block(index, carry):
            lanes = pl.ds(pl.multiple_of(index * 128, 128), 128)
            vre, vim = vis[interval, 0, :, lanes], vis[interval, 1, :, lanes]

            def direction(d, carry):
                dre, dim = model_at(interval, d, lanes)
                at = pl.ds(d, 1)
                bterm[interval, 0, index, at, :] = jnp.sum(
                    vre * dre + vim * dim, axis=0, keepdims=True
                )
                bterm[interval, 1, index, at, :] = jnp.sum(
                    vim * dre - vre * dim, axis=0, keepdims=True
                )
                strength = jnp.sum(dre * dre + dim * dim, axis=0, keepdims=True)
                power[interval, index, at, :] = strength
                gram[interval, 0, index, d, at, :] = strength
                gram[interval, 1, index, d, at, :] = jnp.zeros_like(strength)
                for step in range(1, DIRS // 2 + 1):
                    e = lax.rem(d + step, DIRS)
                    ere, eim = model_at(interval, e, lanes)
                    re = jnp.sum(ere * dre + eim * dim, axis=0, keepdims=True)
                    im = jnp.sum(eim * dre - ere * dim, axis=0, keepdims=True)
                    gram[interval, 0, index, e, at, :] = re
                    gram[interval, 1, index, e, at, :] = im
                    gram[interval, 0, index, d, pl.ds(e, 1), :] = re
                    gram[interval, 1, index, d, pl.ds(e, 1), :] = -im
                return carry

            lax.fori_loop(0, DIRS, direction, 0)
            return carry

        lax.fori_loop(first, last, block, 0)

    def sample_coords(interval):
        for block in range(ROWS // 128):
            lanes = slice(block * 128, block * 128 + 128)
            padded = jnp.concatenate([uv[interval, :, lanes], jnp.zeros((126, 128), F32)], axis=0)
            turned[lanes, :] = padded.T
        for row in range(RPS):
            coords[interval, row] = turned[pl.ds(row, NSUB, stride=RPS), :]

    for load in loads[:4]:
        load.wait()
    for interval in range(INTERVALS):
        lookup_table(interval)
        sample_coords(interval)
    for interval in range(INTERVALS):
        mine = (owner[interval] == bl).astype(F32)
        pack(
            interval,
            jnp.concatenate([held[interval] * mine, jnp.full((DIRS, STATIONS), mine)], axis=0),
        )

    pl.semaphore_wait(barrier, PLANE - 1 + COLUMN - 1)

    def during_first_sums():
        for load in loads[4:]:
            load.wait()
        prepare(0, 0, 2)

    exchange(0, first_update, [(0, 1)], during_first_sums, lambda: prepare(0, 2, 4))

    def direct(interval):
        def block(index, carry):
            lanes = pl.ds(pl.multiple_of(index * 128, 128), 128)

            rre, rim = vis[interval, 0, :, lanes], vis[interval, 1, :, lanes]
            for d in range(DIRS):
                mre, mim = model_at(interval, d, lanes)
                wre = mix[interval, d : d + 1, lanes]
                wim = mix[interval, d + 16 : d + 17, lanes]
                rre = rre - (wre * mre - wim * mim)
                rim = rim - (wre * mim + wim * mre)

            def correlate(d, carry):
                mre, mim = model_at(interval, d, lanes)
                at = pl.ds(d, 1)
                kterm[0, index, at, :] = jnp.sum(rre * mre + rim * mim, axis=0, keepdims=True)
                kterm[1, index, at, :] = jnp.sum(rim * mre - rre * mim, axis=0, keepdims=True)
                power[interval, index, at, :] = jnp.sum(
                    mre * mre + mim * mim, axis=0, keepdims=True
                )
                return carry

            lax.fori_loop(0, DIRS, correlate, 0, unroll=4)
            return carry

        lax.fori_loop(0, ROWS // 128, block, 0)

    def gather(interval):
        rows = []
        for z in range(2):
            for dh in range(2):
                rows.append(
                    jnp.concatenate(
                        [
                            chunk[interval * 8 + sb * 2 + dh, z * 8 : z * 8 + 8, :]
                            for sb in range(SBLOCKS)
                        ],
                        axis=1,
                    )
                )
        table = jnp.concatenate(rows, axis=0)
        found = jnp.dot(
            jnp.concatenate(split3(table), axis=0), hot[interval], preferred_element_type=F32
        )
        found = found[0:32] + found[32:64] + found[64:96]
        pairgain[interval] = found
        pre, pim = found[0:16, 0:ROWS], found[16:32, 0:ROWS]
        qre, qim = found[0:16, ROWS:], found[16:32, ROWS:]
        mix[interval, 0:16] = pre * qre + pim * qim
        mix[interval, 16:32] = pim * qre - pre * qim
        return table

    def scatter(interval, prepared=True):
        left, right = [], []
        for block in range(ROWS // 128):
            lanes = slice(block * 128, block * 128 + 128)
            if prepared:
                kre, kim = bterm[interval, 0, block], bterm[interval, 1, block]
            else:
                kre, kim = kterm[0, block], kterm[1, block]
            for e in range(DIRS if prepared else 0):
                wre, wim = mix[interval, e : e + 1, lanes], mix[interval, e + 16 : e + 17, lanes]
                are, aim = gram[interval, 0, block, e], gram[interval, 1, block, e]
                kre = kre - (wre * are - wim * aim)
                kim = kim - (wre * aim + wim * are)
            pre, pim = pairgain[interval, 0:16, lanes], pairgain[interval, 16:32, lanes]
            lanes = slice(ROWS + block * 128, ROWS + block * 128 + 128)
            qre, qim = pairgain[interval, 0:16, lanes], pairgain[interval, 16:32, lanes]
            strength = power[interval, block]
            left.append(
                jnp.concatenate(
                    [
                        qre * kre - qim * kim,
                        qre * kim + qim * kre,
                        strength * (qre * qre + qim * qim),
                    ],
                    axis=0,
                )
            )
            right.append(
                jnp.concatenate(
                    [
                        pre * kre + pim * kim,
                        pim * kre - pre * kim,
                        strength * (pre * pre + pim * pim),
                    ],
                    axis=0,
                )
            )
        terms = jnp.concatenate(left + right, axis=1)
        table = lax.dot_general(
            jnp.concatenate(split3(terms), axis=0),
            hot[interval],
            (((1,), (1,)), ((), ())),
            preferred_element_type=F32,
        )
        pack(interval, table[0:48] + table[48:96] + table[96:144])

    def update(total):
        scale = damping / total[16:24]
        return chunk[plane] + jnp.concatenate([total[0:8] * scale, total[8:16] * scale], axis=0)

    lane = lax.broadcasted_iota(jnp.int32, (1, 128), 1)
    low = lane < CH
    channel = (freq * CH + lax.rem(lane, CH)).astype(F32)
    factor = 1.0 + 0.5 * channel / (4 * CH)

    def put(pixel, value):
        for h in range(HALVES):
            right[h, pl.ds(pixel, GROUP, stride=PITCH), :] = value[:, h * 128 : h * 128 + 128]

    def phases(index, carry):
        interval = lax.div(index, NSUB // GROUP)
        first = pl.multiple_of(lax.rem(index, NSUB // GROUP) * GROUP, GROUP)
        rows = pl.ds(first, GROUP)

        def angles(which):
            coord = []
            for h in range(HALVES):
                one = coords[interval, 2 * h, rows, which : which + 1]
                two = coords[interval, 2 * h + 1, rows, which : which + 1]
                coord.append(jnp.where(low, one, two) * factor)
            return powers(*sincos(jnp.concatenate(coord, axis=1) * (2.0 * math.pi / SG)))

        for n, pair in angles(0).items():
            for z in range(2):
                for h in range(HALVES):
                    down[interval, n - 1, z, h, rows, :] = pair[z][:, h * 128 : h * 128 + 128]
        half = SG // 2
        one = jnp.ones((GROUP, HALVES * 128), F32)
        put(half, one)
        put(SG + half, one * 0.0)
        for n, (c, s) in angles(1).items():
            if n < half:
                put(half + n, c)
                put(SG + half + n, s)
            put(half - n, c)
            put(SG + half - n, -s)
        for j in range(GROUP):
            for part in range(2):
                span = slice(j * PITCH + part * SG, j * PITCH + part * SG + SG)
                for h in range(HALVES):
                    lanes = slice(h * 128, h * 128 + 128)
                    value = right[h, span, :]
                    high = value.astype(BF16)
                    across[interval, first + j, 2 * part * SG : 2 * part * SG + SG, lanes] = high
                    across[interval, first + j, 2 * part * SG + SG : 2 * part * SG + 2 * SG, lanes] = (
                        value - high.astype(F32)
                    ).astype(BF16)
        return carry

    groups = INTERVALS * NSUB // GROUP
    slots = 2 * (ITERS - 1)

    def some_phases(slot):
        first = lax.div(slot * groups, slots)
        last = lax.div((slot + 1) * groups, slots)
        lax.fori_loop(first, last, phases, 0)

    def iterate(turn, carry):
        for interval in range(INTERVALS):
            gather(interval)
            scatter(interval)
        slot = (turn - 2) * 2
        exchange(
            turn,
            update,
            COLUMN_STEPS,
            lambda: some_phases(slot),
            lambda: some_phases(slot + 1),
        )
        return carry

    for interval in range(INTERVALS):
        gather(interval)
    scatter(0)
    direct(1)
    scatter(1, prepared=False)
    exchange(1, update, COLUMN_STEPS, lambda: prepare(1, 0, 2), lambda: prepare(1, 2, 4))
    lax.fori_loop(2, ITERS + 1, iterate, 0)
    for interval in range(INTERVALS):
        gains_out[interval] = gather(interval)

    def residual(index, carry):
        interval = lax.div(index, 4)
        start = pl.multiple_of(lax.rem(index, 4) * 128, 128)
        lanes = pl.ds(start, 128)
        rre, rim = vis[interval, 0, :, lanes], vis[interval, 1, :, lanes]
        for d in range(DIRS):
            mre, mim = model_at(interval, d, lanes)
            wre = mix[interval, d : d + 1, lanes]
            wim = mix[interval, d + 16 : d + 17, lanes]
            rre = rre - (wre * mre - wim * mim)
            rim = rim - (wre * mim + wim * mre)
        flipped[interval, lanes, :] = jnp.concatenate([rre, rim], axis=0).T
        return carry

    lax.fori_loop(0, INTERVALS * 4, residual, 0)
    scale = 2.0 / (math.sqrt(INTERVALS * NSUB) * math.sqrt(CH * RPS))
    for interval in range(INTERVALS):
        for h in range(HALVES):
            one = flipped[interval, pl.ds(2 * h, NSUB, stride=RPS), :] * scale
            two = flipped[interval, pl.ds(2 * h + 1, NSUB, stride=RPS), :] * scale
            resid[interval, 0, h] = jnp.where(low, one, pltpu.roll(two, 64, axis=1))
            resid[interval, 1, h] = jnp.where(low, pltpu.roll(one, 64, axis=1), two)


def in_hbm(*arrays):
    return [pltpu.with_memory_space_constraint(array, pltpu.HBM) for array in arrays]


def solve(model, visibilities, pairs, held, owner, uv):
    held = held.reshape(INTERVALS, 32, STATIONS)
    pairs = pairs.transpose(0, 2, 1)
    vmem = pl.BlockSpec(memory_space=pltpu.VMEM)
    far = pl.BlockSpec(memory_space=pltpu.HBM)
    return pl.pallas_call(
        solve_kernel,
        out_shape=(
            jax.ShapeDtypeStruct((INTERVALS, 32, STATIONS), F32),
            jax.ShapeDtypeStruct((INTERVALS, 2, HALVES, NSUB, 128), F32),
            jax.ShapeDtypeStruct((INTERVALS, NSUB, 4 * SG, HALVES * 128), BF16),
            jax.ShapeDtypeStruct((INTERVALS, SG // 2, 2, HALVES, NSUB, 128), F32),
        ),
        in_specs=[far] * 6,
        out_specs=(vmem, vmem, vmem, vmem),
        scratch_shapes=[
            pltpu.SMEM((INTERVALS,), jnp.int32),
            pltpu.VMEM((INTERVALS, DIRS, 2, CH, ROWS), BF16),
            pltpu.VMEM((INTERVALS, 2, CH, ROWS), F32),
            pltpu.VMEM((INTERVALS, 2, ROWS), jnp.int32),
            pltpu.VMEM((INTERVALS, 32, STATIONS), F32),
            pltpu.VMEM((INTERVALS, 2, ROWS), F32),
            pltpu.VMEM((ROWS + 8, 128), F32),
            pltpu.VMEM((INTERVALS, RPS, NSUB, 128), F32),
            pltpu.VMEM((INTERVALS, STATIONS, 2 * ROWS), BF16),
            pltpu.VMEM((INTERVALS, ROWS // 128, DIRS, 128), F32),
            pltpu.VMEM((INTERVALS, 2, ROWS // 128, DIRS, 128), F32),
            pltpu.VMEM((INTERVALS, 2, ROWS // 128, DIRS, DIRS, 128), F32),
            pltpu.VMEM((2, ROWS // 128, DIRS, 128), F32),
            pltpu.VMEM((INTERVALS, ROWS + 8, 128), F32),
            pltpu.VMEM((HALVES, GROUP * PITCH + 72, 128), F32),
            pltpu.VMEM((INTERVALS, 32, 2 * ROWS), F32),
            pltpu.VMEM((INTERVALS, 32, ROWS), F32),
            pltpu.VMEM((PLANE, 24, 128), F32),
            pltpu.VMEM((PLANE - 1, 24, 128), F32),
            pltpu.VMEM((2, COLUMN, 24, 128), F32),
            pltpu.VMEM((PLANE, 16, 128), F32),
            pltpu.SemaphoreType.DMA,
            pltpu.SemaphoreType.DMA,
            pltpu.SemaphoreType.DMA,
            pltpu.SemaphoreType.DMA((2,)),
            pltpu.SemaphoreType.DMA,
            pltpu.SemaphoreType.DMA,
            pltpu.SemaphoreType.DMA((6,)),
        ],
        compiler_params=pltpu.CompilerParams(
            collective_id=0, has_side_effects=True, vmem_limit_bytes=SOLVE_MIB * 1024 * 1024
        ),
        name="solve",
    )(*in_hbm(owner, model, visibilities, pairs, held, uv))


def image_kernel(
    owner_far,
    place_far,
    gains,
    resid,
    phase_across,
    phase_down,
    facets,
    gains_out,
    owner,
    place,
    left_even,
    left_odd,
    loaded,
):
    half = SG // 2
    whole = (
        (owner_far, owner),
        (place_far, place),
        (gains, gains_out),
    )
    loads = [
        pltpu.make_async_copy(far, near, loaded.at[k]) for k, (far, near) in enumerate(whole)
    ]
    for load in loads:
        load.start()

    def clear(index, carry):
        facets[index] = jnp.zeros((FACET, 128), F32)
        return carry

    lax.fori_loop(0, facets.shape[0], clear, 0)
    lane = lax.broadcasted_iota(jnp.int32, (1, 128), 1)
    low = lane < 64

    def where(index):
        interval = lax.div(index, NSUB // GROUP)
        return interval, pl.multiple_of(lax.rem(index, NSUB // GROUP) * GROUP, GROUP)

    def operands(index, left):
        interval, first = where(index)
        rows = pl.ds(first, GROUP)
        re = jnp.concatenate([resid[interval, 0, h, rows, :] for h in range(HALVES)], axis=1)
        im = jnp.concatenate([resid[interval, 1, h, rows, :] for h in range(HALVES)], axis=1)

        def put(part, pixel, value):
            for h in range(HALVES):
                left[h, pl.ds(part * SG + pixel, GROUP, stride=PITCH), :] = value[
                    :, h * 128 : h * 128 + 128
                ]

        put(0, half, re)
        put(1, half, im)
        for n in range(1, half + 1):
            c, s = (
                jnp.concatenate(
                    [phase_down[interval, n - 1, z, h, rows, :] for h in range(HALVES)], axis=1
                )
                for z in range(2)
            )
            rc, rs, ic, js = re * c, re * s, im * c, im * s
            if n < half:
                put(0, half + n, rc - js)
                put(1, half + n, rs + ic)
            put(0, half - n, rc + js)
            put(1, half - n, ic - rs)

    def images(index, left):
        interval, first = where(index)
        sign = jnp.where(low, -1.0, 1.0)
        inside = lax.rem(lane, 64) < SG
        for j in range(GROUP):
            span = slice(j * PITCH, j * PITCH + 2 * SG)
            lhs = jnp.concatenate([left[h, span, :] for h in range(HALVES)], axis=1)
            high = lhs.astype(BF16)
            rest = (lhs - high.astype(F32)).astype(BF16)
            both = lax.dot_general(
                jnp.concatenate([high, rest], axis=0),
                phase_across[interval, first + j],
                (((1,), (1,)), ((), ())),
                preferred_element_type=F32,
            )
            real = both[0:SG] + both[2 * SG : 3 * SG]
            imag = both[SG : 2 * SG] + both[3 * SG :]
            image = real + sign * pltpu.roll(imag, 64, axis=1)
            image = image + pltpu.roll(image, 128 - SG, axis=1)
            image = jnp.where(inside, image, 0.0)
            at = owner[interval, first + j]
            at = lax.rem(at, 2) * (facets.shape[0] // 2) + lax.div(at, 2)
            across = place[interval, 1, first + j]
            down = place[interval, 0, first + j]
            image = pltpu.roll(image, across, axis=1)
            facets[at, pl.ds(down, SG), :] += image

    operands(0, left_even)
    for load in loads:
        load.wait()
    groups = INTERVALS * NSUB // GROUP

    def two_groups(index, carry):
        operands(2 * index + 1, left_odd)
        images(2 * index, left_even)
        operands(jnp.minimum(2 * index + 2, groups - 1), left_even)
        images(2 * index + 1, left_odd)
        return carry

    lax.fori_loop(0, groups // 2, two_groups, 0)


def local_facets(gains, resid, phase_across, phase_down, owner, place):
    devices = lax.axis_size("freq") * lax.axis_size("bl")
    owner = owner[:, 0, :, 0]
    place = place[:, 0].transpose(0, 2, 1)
    vmem = pl.BlockSpec(memory_space=pltpu.VMEM)
    far = pl.BlockSpec(memory_space=pltpu.HBM)
    return pl.pallas_call(
        image_kernel,
        out_shape=(
            jax.ShapeDtypeStruct((devices, FACET, 128), F32),
            jax.ShapeDtypeStruct(gains.shape, F32),
        ),
        in_specs=[far] * 2 + [vmem] * 4,
        out_specs=(vmem, far),
        scratch_shapes=[
            pltpu.SMEM((INTERVALS, NSUB), jnp.int32),
            pltpu.SMEM((INTERVALS, 2, NSUB), jnp.int32),
            pltpu.VMEM((HALVES, GROUP * PITCH + 72, 128), F32),
            pltpu.VMEM((HALVES, GROUP * PITCH + 72, 128), F32),
            pltpu.SemaphoreType.DMA((3,)),
        ],
        compiler_params=pltpu.CompilerParams(vmem_limit_bytes=IMAGE_MIB * 1024 * 1024),
        name="image",
    )(*in_hbm(owner, place), gains, resid, phase_across, phase_down)


PARTS = ((0, 24, (0, 1, 2)), (24, 24, (1, 2, 0)), (48, 16, (2, 0, 1)))


def collect_kernel(facets, out, *scratch):
    sibling, one, two, three, s1, s2, s3 = (scratch[3 * n : 3 * n + 3] for n in range(7))
    core_send, core_recv, send, recv = scratch[21:]
    freq = lax.axis_index("freq")
    bl = lax.axis_index("bl")
    core = lax.rem(bl, 2)
    here = (freq, lax.div(bl, 8), lax.rem(lax.div(bl, 2), 4))

    def device(at, core):
        return (at[0], at[1] * 8 + at[2] * 2 + core)

    def peer(axis, step):
        other = lax.rem(here[axis] + step, 4)
        at = list(here)
        at[axis] = other
        return other, device(at, core)

    barrier = pltpu.get_barrier_semaphore()
    pl.semaphore_signal(barrier, inc=1, device_id=device(here, 1 - core), device_id_type=MESH)
    for axis in range(3):
        for step in range(1, 4):
            pl.semaphore_signal(barrier, inc=1, device_id=peer(axis, step)[1], device_id_type=MESH)
    pl.semaphore_wait(barrier, 10)

    def core_copy(p):
        first, rows, _ = PARTS[p]
        return pltpu.make_async_remote_copy(
            src_ref=facets.at[1 - core, :, :, :, pl.ds(first, rows), :],
            dst_ref=sibling[p],
            send_sem=core_send.at[p],
            recv_sem=core_recv.at[p],
            device_id=device(here, 1 - core),
            device_id_type=MESH,
        )

    def stage_copy(stage, p, step):
        axis = PARTS[p][2][stage]
        other, target = peer(axis, step)
        source, into = ((one, s1), (two, s2), (three, s3))[stage]
        return pltpu.make_async_remote_copy(
            src_ref=source[p].at[other],
            dst_ref=into[p].at[step - 1],
            send_sem=send.at[stage, p, step],
            recv_sem=recv.at[stage, p, step],
            device_id=target,
            device_id_type=MESH,
        )

    for p in range(3):
        core_copy(p).start()
    for p in range(3):
        first, rows, order = PARTS[p]
        core_copy(p).wait_recv()

        rows = pl.ds(first, rows)
        for x in range(4):
            if order == (0, 1, 2):
                one[p][x] = facets[core, x, :, :, rows, :] + sibling[p][x]
            elif order == (1, 2, 0):
                one[p][:, :, x] = facets[core, x, :, :, rows, :] + sibling[p][x]
            else:
                for z in range(4):
                    one[p][:, x, z] = facets[core, x, z, :, rows, :] + sibling[p][x, z]
        for step in (2, 1, 3):
            stage_copy(0, p, step).start()
    for stage in range(3):
        source, into = ((one, s1), (two, s2), (three, s3))[stage]
        for p in range(3):
            first, rows, order = PARTS[p]
            mine = here[order[stage]]
            for step in range(1, 4):
                stage_copy(stage, p, step).wait_recv()
            total = source[p][mine] + into[p][0] + into[p][1] + into[p][2]
            if stage < 2:
                (two, three)[stage][p][...] = total
                for step in (2, 1, 3):
                    stage_copy(stage + 1, p, step).start()
            else:
                out[first : first + rows, :] = total
    for p in range(3):
        core_copy(p).wait_send()
        for stage in range(3):
            for step in range(1, 4):
                stage_copy(stage, p, step).wait_send()


def collect(facets):
    vmem = pl.BlockSpec(memory_space=pltpu.VMEM)
    leads = ((4, 4, 4), (4, 4, 4), (4, 4), (4,), (3, 4, 4), (3, 4), (3,))
    return pl.pallas_call(
        collect_kernel,
        out_shape=jax.ShapeDtypeStruct((FACET, 128), F32),
        in_specs=[vmem],
        out_specs=vmem,
        scratch_shapes=[
            pltpu.VMEM(lead + (rows, 128), F32) for lead in leads for _, rows, _ in PARTS
        ]
        + [
            pltpu.SemaphoreType.DMA((3,)),
            pltpu.SemaphoreType.DMA((3,)),
            pltpu.SemaphoreType.DMA((3, 3, 4)),
            pltpu.SemaphoreType.DMA((3, 3, 4)),
        ],
        compiler_params=pltpu.CompilerParams(
            collective_id=1, has_side_effects=True, vmem_limit_bytes=32 * 1024 * 1024
        ),
        name="collect",
    )(facets.reshape(2, 4, 4, 4, FACET, 128))


def body(visibilities, model, pairs, uv, held_gains, solver_owner, facet_owner, subgrid_pos):
    gains, resid, phase_across, phase_down = solve(
        model, visibilities, pairs, held_gains[0], solver_owner, uv
    )
    facets, gains = local_facets(
        gains, resid, phase_across, phase_down, facet_owner, subgrid_pos
    )
    facet = collect(facets)
    facet = facet.reshape(FACET, 2, FACET).transpose(1, 0, 2)
    return (gains.reshape(INTERVALS, 2, DIRS, STATIONS), facet[None, None])


def solution(mesh):
    placed = (
        P(None, None, "freq", "bl"),
        P(None, None, None, "freq", "bl"),
        P(None, "bl", None),
        P(None, None, "bl"),
        P("bl", None, None, None, None),
        P(),
        P(None, "freq", "bl", None),
        P(None, "freq", "bl", None),
    )
    return jax.shard_map(
        body,
        mesh=mesh,
        in_specs=placed,
        out_specs=(P(), P("freq", "bl", None, None, None)),
        check_vma=False,
    )
```

```python
import functools
import math

import jax
import jax.numpy as jnp
from jax import lax
from jax.experimental import pallas as pl
from jax.experimental.pallas import tpu as pltpu
from jax.sharding import PartitionSpec as P

SG = 32
FACET = 64
RPS = 4
ITERS = 4
INTERVALS = 2
DIRS = 16
STATIONS = 512
ROWS = 512
CH = 64
PLANE = 16
COLUMN = 8
SBLOCKS = STATIONS // 128
MESH = pl.DeviceIdType.MESH
F32 = jnp.float32
BF16 = jnp.bfloat16

damping = 0.5


def split3(x):
    hi = x.astype(BF16)
    rest = x - hi.astype(F32)
    mid = rest.astype(BF16)
    low = (rest - mid.astype(F32)).astype(BF16)
    return hi, mid, low


GROUP = 32
SOLVE_MIB = 20
IMAGE_MIB = 12
PITCH = 2 * SG + 1
HALVES = 2
NSUB = ROWS // RPS


def sincos(x):
    y = x * x
    s = jnp.full_like(x, 1.0 / math.factorial(17))
    c = jnp.full_like(x, 1.0 / math.factorial(16))
    for n in range(7, -1, -1):
        s = s * y + (-1) ** n / math.factorial(2 * n + 1)
        c = c * y + (-1) ** n / math.factorial(2 * n)
    return c, s * x


def powers(c, s):
    table = {1: (c, s)}
    for n in range(2, SG // 2 + 1):
        (ca, sa), (cb, sb) = table[n // 2], table[n - n // 2]
        table[n] = (ca * cb - sa * sb, ca * sb + sa * cb)
    return table


def spread(sizes):
    steps = [(i, j) for i in range(sizes[0]) for j in range(sizes[1]) if i or j]
    return sorted(steps, key=lambda t: -sum(min(k, n - k) for k, n in zip(t, sizes)))


PLANE_STEPS = spread((4, 4))
COLUMN_STEPS = spread((4, 2))


def solve_kernel(
    owner_far,
    model_far,
    vis_far,
    pairs_far,
    held_far,
    uv_far,
    gains_out,
    resid,
    across,
    down,
    owner,
    model,
    vis,
    pairs,
    held,
    uv,
    turned,
    coords,
    hot,
    power,
    bterm,
    gram,
    kterm,
    flipped,
    right,
    pairgain,
    mix,
    sums,
    arrived,
    partial,
    chunk,
    rs_send,
    rs_recv,
    ex_send,
    ex_recv,
    ag_send,
    ag_recv,
    loaded,
):
    freq = lax.axis_index("freq")
    bl = lax.axis_index("bl")
    core = lax.rem(bl, 2)
    plane = lax.div(bl, 2)
    column = freq * 2 + core

    def plane_peer(steps):
        first = lax.rem(lax.div(plane, 4) + steps[0], 4)
        second = lax.rem(lax.rem(plane, 4) + steps[1], 4)
        other = first * 4 + second
        return other, (freq, other * 2 + core)

    def column_peer(steps):
        first = lax.rem(freq + steps[0], 4)
        second = lax.rem(core + steps[1], 2)
        return first * 2 + second, (first, plane * 2 + second)

    barrier = pltpu.get_barrier_semaphore()
    for steps in PLANE_STEPS:
        pl.semaphore_signal(barrier, inc=1, device_id=plane_peer(steps)[1], device_id_type=MESH)
    for steps in COLUMN_STEPS:
        pl.semaphore_signal(barrier, inc=1, device_id=column_peer(steps)[1], device_id_type=MESH)
    whole = (
        (owner_far, owner),
        (held_far, held),
        (pairs_far, pairs),
        (uv_far, uv),
        (vis_far, vis),
        (model_far, model),
    )
    loads = [
        pltpu.make_async_copy(far, near, loaded.at[k]) for k, (far, near) in enumerate(whole)
    ]
    for load in loads:
        load.start()

    def exchange(turn, update, column_steps, during_sums, during_gains):
        par = lax.rem(turn, 2)
        reach = len(column_steps)

        def remote(source, into, send, recv, device):
            return pltpu.make_async_remote_copy(
                src_ref=source,
                dst_ref=into,
                send_sem=send,
                recv_sem=recv,
                device_id=device,
                device_id_type=MESH,
            )

        near = plane_peer(PLANE_STEPS[0])[1]
        beside = column_peer(column_steps[0])[1]
        rs_all = remote(sums.at[pl.ds(0, PLANE - 1)], arrived, rs_send, rs_recv, near)
        ex_all = remote(
            partial.at[par, pl.ds(0, reach)],
            partial.at[par, pl.ds(0, reach)],
            ex_send,
            ex_recv.at[par],
            beside,
        )
        ag_all = remote(
            chunk.at[pl.ds(0, PLANE - 1)], chunk.at[pl.ds(0, PLANE - 1)], ag_send, ag_recv, near
        )
        for k, steps in enumerate(PLANE_STEPS):
            other, device = plane_peer(steps)
            remote(sums.at[other], arrived.at[k], rs_send, rs_recv, device).start()
        during_sums()
        rs_all.wait_recv()
        total = sums[plane]
        for k in range(PLANE - 1):
            total = total + arrived[k]
        partial[par, column] = total
        for steps in column_steps:
            _, device = column_peer(steps)
            mine = partial.at[par, column]
            remote(mine, mine, ex_send, ex_recv.at[par], device).start()
        rs_all.wait_send()
        ex_all.wait_recv()
        if reach == COLUMN - 1:
            total = partial[par, 0]
            for m in range(1, COLUMN):
                total = total + partial[par, m]
        else:
            total = partial[par, freq * 2] + partial[par, freq * 2 + 1]
        chunk[plane] = update(total)
        for steps in PLANE_STEPS:
            _, device = plane_peer(steps)
            mine = chunk.at[plane]
            remote(mine, mine, ag_send, ag_recv, device).start()
        during_gains()
        ex_all.wait_send()
        ag_all.wait_recv()
        ag_all.wait_send()

    def pack(interval, table):
        for sb in range(SBLOCKS):
            for dh in range(2):
                for q in range(3):
                    sums[interval * 8 + sb * 2 + dh, q * 8 : q * 8 + 8, :] = table[
                        q * 16 + dh * 8 : q * 16 + dh * 8 + 8, sb * 128 : sb * 128 + 128
                    ]

    def first_update(total):
        scale = 1.0 / total[16:24]
        return jnp.concatenate([total[0:8] * scale, total[8:16] * scale], axis=0)

    def model_at(interval, d, lanes):
        return (
            model[interval, d, 0, :, lanes].astype(F32),
            model[interval, d, 1, :, lanes].astype(F32),
        )

    def lookup_table(interval):
        stations = lax.broadcasted_iota(jnp.int32, (STATIONS, ROWS), 0)
        for end in range(2):
            found = stations == pairs[interval, end : end + 1, :]
            hot[interval, :, end * ROWS : end * ROWS + ROWS] = found.astype(F32).astype(BF16)

    def prepare(interval, first, last):
        def block(index, carry):
            lanes = pl.ds(pl.multiple_of(index * 128, 128), 128)
            vre, vim = vis[interval, 0, :, lanes], vis[interval, 1, :, lanes]

            def direction(d, carry):
                dre, dim = model_at(interval, d, lanes)
                at = pl.ds(d, 1)
                bterm[interval, 0, index, at, :] = jnp.sum(
                    vre * dre + vim * dim, axis=0, keepdims=True
                )
                bterm[interval, 1, index, at, :] = jnp.sum(
                    vim * dre - vre * dim, axis=0, keepdims=True
                )
                strength = jnp.sum(dre * dre + dim * dim, axis=0, keepdims=True)
                power[interval, index, at, :] = strength
                gram[interval, 0, index, d, at, :] = strength
                gram[interval, 1, index, d, at, :] = jnp.zeros_like(strength)
                for step in range(1, DIRS // 2 + 1):
                    e = lax.rem(d + step, DIRS)
                    ere, eim = model_at(interval, e, lanes)
                    re = jnp.sum(ere * dre + eim * dim, axis=0, keepdims=True)
                    im = jnp.sum(eim * dre - ere * dim, axis=0, keepdims=True)
                    gram[interval, 0, index, e, at, :] = re
                    gram[interval, 1, index, e, at, :] = im
                    gram[interval, 0, index, d, pl.ds(e, 1), :] = re
                    gram[interval, 1, index, d, pl.ds(e, 1), :] = -im
                return carry

            lax.fori_loop(0, DIRS, direction, 0)
            return carry

        lax.fori_loop(first, last, block, 0)

    def sample_coords(interval):
        for block in range(ROWS // 128):
            lanes = slice(block * 128, block * 128 + 128)
            padded = jnp.concatenate([uv[interval, :, lanes], jnp.zeros((126, 128), F32)], axis=0)
            turned[lanes, :] = padded.T
        for row in range(RPS):
            coords[interval, row] = turned[pl.ds(row, NSUB, stride=RPS), :]

    for load in loads[:4]:
        load.wait()
    for interval in range(INTERVALS):
        lookup_table(interval)
        sample_coords(interval)
    for interval in range(INTERVALS):
        mine = (owner[interval] == bl).astype(F32)
        pack(
            interval,
            jnp.concatenate([held[interval] * mine, jnp.full((DIRS, STATIONS), mine)], axis=0),
        )

    pl.semaphore_wait(barrier, PLANE - 1 + COLUMN - 1)

    def during_first_sums():
        for load in loads[4:]:
            load.wait()
        prepare(0, 0, 2)

    exchange(0, first_update, [(0, 1)], during_first_sums, lambda: prepare(0, 2, 4))

    def direct(interval):
        def block(index, carry):
            lanes = pl.ds(pl.multiple_of(index * 128, 128), 128)

            rre, rim = vis[interval, 0, :, lanes], vis[interval, 1, :, lanes]
            for d in range(DIRS):
                mre, mim = model_at(interval, d, lanes)
                wre = mix[interval, d : d + 1, lanes]
                wim = mix[interval, d + 16 : d + 17, lanes]
                rre = rre - (wre * mre - wim * mim)
                rim = rim - (wre * mim + wim * mre)

            def correlate(d, carry):
                mre, mim = model_at(interval, d, lanes)
                at = pl.ds(d, 1)
                kterm[0, index, at, :] = jnp.sum(rre * mre + rim * mim, axis=0, keepdims=True)
                kterm[1, index, at, :] = jnp.sum(rim * mre - rre * mim, axis=0, keepdims=True)
                power[interval, index, at, :] = jnp.sum(
                    mre * mre + mim * mim, axis=0, keepdims=True
                )
                return carry

            lax.fori_loop(0, DIRS, correlate, 0, unroll=DIRS)
            return carry

        lax.fori_loop(0, ROWS // 128, block, 0)

    def gather(interval):
        rows = []
        for z in range(2):
            for dh in range(2):
                rows.append(
                    jnp.concatenate(
                        [
                            chunk[interval * 8 + sb * 2 + dh, z * 8 : z * 8 + 8, :]
                            for sb in range(SBLOCKS)
                        ],
                        axis=1,
                    )
                )
        table = jnp.concatenate(rows, axis=0)
        found = jnp.dot(
            jnp.concatenate(split3(table), axis=0), hot[interval], preferred_element_type=F32
        )
        found = found[0:32] + found[32:64] + found[64:96]
        pairgain[interval] = found
        pre, pim = found[0:16, 0:ROWS], found[16:32, 0:ROWS]
        qre, qim = found[0:16, ROWS:], found[16:32, ROWS:]
        mix[interval, 0:16] = pre * qre + pim * qim
        mix[interval, 16:32] = pim * qre - pre * qim
        return table

    def scatter(interval, prepared=True):
        left, right = [], []
        for block in range(ROWS // 128):
            lanes = slice(block * 128, block * 128 + 128)
            if prepared:
                kre, kim = bterm[interval, 0, block], bterm[interval, 1, block]
            else:
                kre, kim = kterm[0, block], kterm[1, block]
            for e in range(DIRS if prepared else 0):
                wre, wim = mix[interval, e : e + 1, lanes], mix[interval, e + 16 : e + 17, lanes]
                are, aim = gram[interval, 0, block, e], gram[interval, 1, block, e]
                kre = kre - (wre * are - wim * aim)
                kim = kim - (wre * aim + wim * are)
            pre, pim = pairgain[interval, 0:16, lanes], pairgain[interval, 16:32, lanes]
            lanes = slice(ROWS + block * 128, ROWS + block * 128 + 128)
            qre, qim = pairgain[interval, 0:16, lanes], pairgain[interval, 16:32, lanes]
            strength = power[interval, block]
            left.append(
                jnp.concatenate(
                    [
                        qre * kre - qim * kim,
                        qre * kim + qim * kre,
                        strength * (qre * qre + qim * qim),
                    ],
                    axis=0,
                )
            )
            right.append(
                jnp.concatenate(
                    [
                        pre * kre + pim * kim,
                        pim * kre - pre * kim,
                        strength * (pre * pre + pim * pim),
                    ],
                    axis=0,
                )
            )
        terms = jnp.concatenate(left + right, axis=1)
        table = lax.dot_general(
            jnp.concatenate(split3(terms), axis=0),
            hot[interval],
            (((1,), (1,)), ((), ())),
            preferred_element_type=F32,
        )
        pack(interval, table[0:48] + table[48:96] + table[96:144])

    def update(total):
        scale = damping / total[16:24]
        return chunk[plane] + jnp.concatenate([total[0:8] * scale, total[8:16] * scale], axis=0)

    lane = lax.broadcasted_iota(jnp.int32, (1, 128), 1)
    low = lane < CH
    channel = (freq * CH + lax.rem(lane, CH)).astype(F32)
    factor = 1.0 + 0.5 * channel / (4 * CH)

    def put(pixel, value):
        for h in range(HALVES):
            right[h, pl.ds(pixel, GROUP, stride=PITCH), :] = value[:, h * 128 : h * 128 + 128]

    def phases(index, carry):
        interval = lax.div(index, NSUB // GROUP)
        first = pl.multiple_of(lax.rem(index, NSUB // GROUP) * GROUP, GROUP)
        rows = pl.ds(first, GROUP)

        def angles(which):
            coord = []
            for h in range(HALVES):
                one = coords[interval, 2 * h, rows, which : which + 1]
                two = coords[interval, 2 * h + 1, rows, which : which + 1]
                coord.append(jnp.where(low, one, two) * factor)
            return powers(*sincos(jnp.concatenate(coord, axis=1) * (2.0 * math.pi / SG)))

        for n, pair in angles(0).items():
            for z in range(2):
                for h in range(HALVES):
                    down[interval, n - 1, z, h, rows, :] = pair[z][:, h * 128 : h * 128 + 128]
        half = SG // 2
        one = jnp.ones((GROUP, HALVES * 128), F32)
        put(half, one)
        put(SG + half, one * 0.0)
        for n, (c, s) in angles(1).items():
            if n < half:
                put(half + n, c)
                put(SG + half + n, s)
            put(half - n, c)
            put(SG + half - n, -s)
        for j in range(GROUP):
            for part in range(2):
                span = slice(j * PITCH + part * SG, j * PITCH + part * SG + SG)
                for h in range(HALVES):
                    lanes = slice(h * 128, h * 128 + 128)
                    value = right[h, span, :]
                    high = value.astype(BF16)
                    across[interval, first + j, 2 * part * SG : 2 * part * SG + SG, lanes] = high
                    across[interval, first + j, 2 * part * SG + SG : 2 * part * SG + 2 * SG, lanes] = (
                        value - high.astype(F32)
                    ).astype(BF16)
        return carry

    groups = INTERVALS * NSUB // GROUP
    slots = 2 * (ITERS - 1)

    def some_phases(slot):
        first = lax.div(slot * groups, slots)
        last = lax.div((slot + 1) * groups, slots)
        lax.fori_loop(first, last, phases, 0)

    def iterate(turn, carry):
        for interval in range(INTERVALS):
            gather(interval)
            scatter(interval)
        slot = (turn - 2) * 2
        exchange(
            turn,
            update,
            COLUMN_STEPS,
            lambda: some_phases(slot),
            lambda: some_phases(slot + 1),
        )
        return carry

    for interval in range(INTERVALS):
        gather(interval)
    scatter(0)
    direct(1)
    scatter(1, prepared=False)
    exchange(1, update, COLUMN_STEPS, lambda: prepare(1, 0, 2), lambda: prepare(1, 2, 4))
    lax.fori_loop(2, ITERS + 1, iterate, 0)
    for interval in range(INTERVALS):
        gains_out[interval] = gather(interval)

    def residual(index, carry):
        interval = lax.div(index, 4)
        start = pl.multiple_of(lax.rem(index, 4) * 128, 128)
        lanes = pl.ds(start, 128)
        rre, rim = vis[interval, 0, :, lanes], vis[interval, 1, :, lanes]
        for d in range(DIRS):
            mre, mim = model_at(interval, d, lanes)
            wre = mix[interval, d : d + 1, lanes]
            wim = mix[interval, d + 16 : d + 17, lanes]
            rre = rre - (wre * mre - wim * mim)
            rim = rim - (wre * mim + wim * mre)
        flipped[interval, lanes, :] = jnp.concatenate([rre, rim], axis=0).T
        return carry

    lax.fori_loop(0, INTERVALS * 4, residual, 0, unroll=4)
    scale = 2.0 / (math.sqrt(INTERVALS * NSUB) * math.sqrt(CH * RPS))
    for interval in range(INTERVALS):
        for h in range(HALVES):
            one = flipped[interval, pl.ds(2 * h, NSUB, stride=RPS), :] * scale
            two = flipped[interval, pl.ds(2 * h + 1, NSUB, stride=RPS), :] * scale
            resid[interval, 0, h] = jnp.where(low, one, pltpu.roll(two, 64, axis=1))
            resid[interval, 1, h] = jnp.where(low, pltpu.roll(one, 64, axis=1), two)


def in_hbm(*arrays):
    return [pltpu.with_memory_space_constraint(array, pltpu.HBM) for array in arrays]


def solve(model, visibilities, pairs, held, owner, uv):
    held = held.reshape(INTERVALS, 32, STATIONS)
    pairs = pairs.transpose(0, 2, 1)
    vmem = pl.BlockSpec(memory_space=pltpu.VMEM)
    far = pl.BlockSpec(memory_space=pltpu.HBM)
    return pl.pallas_call(
        solve_kernel,
        out_shape=(
            jax.ShapeDtypeStruct((INTERVALS, 32, STATIONS), F32),
            jax.ShapeDtypeStruct((INTERVALS, 2, HALVES, NSUB, 128), F32),
            jax.ShapeDtypeStruct((INTERVALS, NSUB, 4 * SG, HALVES * 128), BF16),
            jax.ShapeDtypeStruct((INTERVALS, SG // 2, 2, HALVES, NSUB, 128), F32),
        ),
        in_specs=[far] * 6,
        out_specs=(vmem, vmem, vmem, vmem),
        scratch_shapes=[
            pltpu.SMEM((INTERVALS,), jnp.int32),
            pltpu.VMEM((INTERVALS, DIRS, 2, CH, ROWS), BF16),
            pltpu.VMEM((INTERVALS, 2, CH, ROWS), F32),
            pltpu.VMEM((INTERVALS, 2, ROWS), jnp.int32),
            pltpu.VMEM((INTERVALS, 32, STATIONS), F32),
            pltpu.VMEM((INTERVALS, 2, ROWS), F32),
            pltpu.VMEM((ROWS + 8, 128), F32),
            pltpu.VMEM((INTERVALS, RPS, NSUB, 128), F32),
            pltpu.VMEM((INTERVALS, STATIONS, 2 * ROWS), BF16),
            pltpu.VMEM((INTERVALS, ROWS // 128, DIRS, 128), F32),
            pltpu.VMEM((INTERVALS, 2, ROWS // 128, DIRS, 128), F32),
            pltpu.VMEM((INTERVALS, 2, ROWS // 128, DIRS, DIRS, 128), F32),
            pltpu.VMEM((2, ROWS // 128, DIRS, 128), F32),
            pltpu.VMEM((INTERVALS, ROWS + 8, 128), F32),
            pltpu.VMEM((HALVES, GROUP * PITCH + 72, 128), F32),
            pltpu.VMEM((INTERVALS, 32, 2 * ROWS), F32),
            pltpu.VMEM((INTERVALS, 32, ROWS), F32),
            pltpu.VMEM((PLANE, 24, 128), F32),
            pltpu.VMEM((PLANE - 1, 24, 128), F32),
            pltpu.VMEM((2, COLUMN, 24, 128), F32),
            pltpu.VMEM((PLANE, 16, 128), F32),
            pltpu.SemaphoreType.DMA,
            pltpu.SemaphoreType.DMA,
            pltpu.SemaphoreType.DMA,
            pltpu.SemaphoreType.DMA((2,)),
            pltpu.SemaphoreType.DMA,
            pltpu.SemaphoreType.DMA,
            pltpu.SemaphoreType.DMA((6,)),
        ],
        compiler_params=pltpu.CompilerParams(
            collective_id=0, has_side_effects=True, vmem_limit_bytes=SOLVE_MIB * 1024 * 1024
        ),
        name="solve",
    )(*in_hbm(owner, model, visibilities, pairs, held, uv))


def image_kernel(
    owner_far,
    place_far,
    gains,
    resid,
    phase_across,
    phase_down,
    facets,
    gains_out,
    owner,
    place,
    left_even,
    left_odd,
    loaded,
):
    half = SG // 2
    whole = (
        (owner_far, owner),
        (place_far, place),
        (gains, gains_out),
    )
    loads = [
        pltpu.make_async_copy(far, near, loaded.at[k]) for k, (far, near) in enumerate(whole)
    ]
    for load in loads:
        load.start()

    def clear(index, carry):
        facets[index] = jnp.zeros((FACET, 128), F32)
        return carry

    lax.fori_loop(0, facets.shape[0], clear, 0)
    lane = lax.broadcasted_iota(jnp.int32, (1, 128), 1)
    low = lane < 64

    def where(index):
        interval = lax.div(index, NSUB // GROUP)
        return interval, pl.multiple_of(lax.rem(index, NSUB // GROUP) * GROUP, GROUP)

    def operands(index, left):
        interval, first = where(index)
        rows = pl.ds(first, GROUP)
        re = jnp.concatenate([resid[interval, 0, h, rows, :] for h in range(HALVES)], axis=1)
        im = jnp.concatenate([resid[interval, 1, h, rows, :] for h in range(HALVES)], axis=1)

        def put(part, pixel, value):
            for h in range(HALVES):
                left[h, pl.ds(part * SG + pixel, GROUP, stride=PITCH), :] = value[
                    :, h * 128 : h * 128 + 128
                ]

        put(0, half, re)
        put(1, half, im)
        for n in range(1, half + 1):
            c, s = (
                jnp.concatenate(
                    [phase_down[interval, n - 1, z, h, rows, :] for h in range(HALVES)], axis=1
                )
                for z in range(2)
            )
            rc, rs, ic, js = re * c, re * s, im * c, im * s
            if n < half:
                put(0, half + n, rc - js)
                put(1, half + n, rs + ic)
            put(0, half - n, rc + js)
            put(1, half - n, ic - rs)

    def images(index, left):
        interval, first = where(index)
        sign = jnp.where(low, -1.0, 1.0)
        inside = lax.rem(lane, 64) < SG
        for j in range(GROUP):
            span = slice(j * PITCH, j * PITCH + 2 * SG)
            lhs = jnp.concatenate([left[h, span, :] for h in range(HALVES)], axis=1)
            high = lhs.astype(BF16)
            rest = (lhs - high.astype(F32)).astype(BF16)
            both = lax.dot_general(
                jnp.concatenate([high, rest], axis=0),
                phase_across[interval, first + j],
                (((1,), (1,)), ((), ())),
                preferred_element_type=F32,
            )
            real = both[0:SG] + both[2 * SG : 3 * SG]
            imag = both[SG : 2 * SG] + both[3 * SG :]
            image = real + sign * pltpu.roll(imag, 64, axis=1)
            image = image + pltpu.roll(image, 128 - SG, axis=1)
            image = jnp.where(inside, image, 0.0)
            at = owner[interval, first + j]
            at = lax.rem(at, 2) * (facets.shape[0] // 2) + lax.div(at, 2)
            across = place[interval, 1, first + j]
            down = place[interval, 0, first + j]
            image = pltpu.roll(image, across, axis=1)
            facets[at, pl.ds(down, SG), :] += image

    operands(0, left_even)
    for load in loads:
        load.wait()
    groups = INTERVALS * NSUB // GROUP

    def two_groups(index, carry):
        operands(2 * index + 1, left_odd)
        images(2 * index, left_even)
        operands(jnp.minimum(2 * index + 2, groups - 1), left_even)
        images(2 * index + 1, left_odd)
        return carry

    lax.fori_loop(0, groups // 2, two_groups, 0)


def local_facets(gains, resid, phase_across, phase_down, owner, place):
    devices = lax.axis_size("freq") * lax.axis_size("bl")
    owner = owner[:, 0, :, 0]
    place = place[:, 0].transpose(0, 2, 1)
    vmem = pl.BlockSpec(memory_space=pltpu.VMEM)
    far = pl.BlockSpec(memory_space=pltpu.HBM)
    return pl.pallas_call(
        image_kernel,
        out_shape=(
            jax.ShapeDtypeStruct((devices, FACET, 128), F32),
            jax.ShapeDtypeStruct(gains.shape, F32),
        ),
        in_specs=[far] * 2 + [vmem] * 4,
        out_specs=(vmem, far),
        scratch_shapes=[
            pltpu.SMEM((INTERVALS, NSUB), jnp.int32),
            pltpu.SMEM((INTERVALS, 2, NSUB), jnp.int32),
            pltpu.VMEM((HALVES, GROUP * PITCH + 72, 128), F32),
            pltpu.VMEM((HALVES, GROUP * PITCH + 72, 128), F32),
            pltpu.SemaphoreType.DMA((3,)),
        ],
        compiler_params=pltpu.CompilerParams(vmem_limit_bytes=IMAGE_MIB * 1024 * 1024),
        name="image",
    )(*in_hbm(owner, place), gains, resid, phase_across, phase_down)


PARTS = ((0, 24, (0, 1, 2)), (24, 24, (1, 2, 0)), (48, 16, (2, 0, 1)))


def collect_kernel(facets, out, *scratch):
    sibling, one, two, three, s1, s2, s3 = (scratch[3 * n : 3 * n + 3] for n in range(7))
    core_send, core_recv, send, recv = scratch[21:]
    freq = lax.axis_index("freq")
    bl = lax.axis_index("bl")
    core = lax.rem(bl, 2)
    here = (freq, lax.div(bl, 8), lax.rem(lax.div(bl, 2), 4))

    def device(at, core):
        return (at[0], at[1] * 8 + at[2] * 2 + core)

    def peer(axis, step):
        other = lax.rem(here[axis] + step, 4)
        at = list(here)
        at[axis] = other
        return other, device(at, core)

    barrier = pltpu.get_barrier_semaphore()
    pl.semaphore_signal(barrier, inc=1, device_id=device(here, 1 - core), device_id_type=MESH)
    for axis in range(3):
        for step in range(1, 4):
            pl.semaphore_signal(barrier, inc=1, device_id=peer(axis, step)[1], device_id_type=MESH)
    pl.semaphore_wait(barrier, 10)

    def core_copy(p):
        first, rows, _ = PARTS[p]
        return pltpu.make_async_remote_copy(
            src_ref=facets.at[1 - core, :, :, :, pl.ds(first, rows), :],
            dst_ref=sibling[p],
            send_sem=core_send.at[p],
            recv_sem=core_recv.at[p],
            device_id=device(here, 1 - core),
            device_id_type=MESH,
        )

    def stage_copy(stage, p, step):
        axis = PARTS[p][2][stage]
        other, target = peer(axis, step)
        source, into = ((one, s1), (two, s2), (three, s3))[stage]
        return pltpu.make_async_remote_copy(
            src_ref=source[p].at[other],
            dst_ref=into[p].at[step - 1],
            send_sem=send.at[stage, p, step],
            recv_sem=recv.at[stage, p, step],
            device_id=target,
            device_id_type=MESH,
        )

    for p in range(3):
        core_copy(p).start()
    for p in range(3):
        first, rows, order = PARTS[p]
        core_copy(p).wait_recv()

        rows = pl.ds(first, rows)
        for x in range(4):
            if order == (0, 1, 2):
                one[p][x] = facets[core, x, :, :, rows, :] + sibling[p][x]
            elif order == (1, 2, 0):
                one[p][:, :, x] = facets[core, x, :, :, rows, :] + sibling[p][x]
            else:
                for z in range(4):
                    one[p][:, x, z] = facets[core, x, z, :, rows, :] + sibling[p][x, z]
        for step in (2, 1, 3):
            stage_copy(0, p, step).start()
    for stage in range(3):
        source, into = ((one, s1), (two, s2), (three, s3))[stage]
        for p in range(3):
            first, rows, order = PARTS[p]
            mine = here[order[stage]]
            for step in range(1, 4):
                stage_copy(stage, p, step).wait_recv()
            total = source[p][mine] + into[p][0] + into[p][1] + into[p][2]
            if stage < 2:
                (two, three)[stage][p][...] = total
                for step in (2, 1, 3):
                    stage_copy(stage + 1, p, step).start()
            else:
                out[first : first + rows, :] = total
    for p in range(3):
        core_copy(p).wait_send()
        for stage in range(3):
            for step in range(1, 4):
                stage_copy(stage, p, step).wait_send()


def collect(facets):
    vmem = pl.BlockSpec(memory_space=pltpu.VMEM)
    leads = ((4, 4, 4), (4, 4, 4), (4, 4), (4,), (3, 4, 4), (3, 4), (3,))
    return pl.pallas_call(
        collect_kernel,
        out_shape=jax.ShapeDtypeStruct((FACET, 128), F32),
        in_specs=[vmem],
        out_specs=vmem,
        scratch_shapes=[
            pltpu.VMEM(lead + (rows, 128), F32) for lead in leads for _, rows, _ in PARTS
        ]
        + [
            pltpu.SemaphoreType.DMA((3,)),
            pltpu.SemaphoreType.DMA((3,)),
            pltpu.SemaphoreType.DMA((3, 3, 4)),
            pltpu.SemaphoreType.DMA((3, 3, 4)),
        ],
        compiler_params=pltpu.CompilerParams(
            collective_id=1, has_side_effects=True, vmem_limit_bytes=32 * 1024 * 1024
        ),
        name="collect",
    )(facets.reshape(2, 4, 4, 4, FACET, 128))


def body(visibilities, model, pairs, uv, held_gains, solver_owner, facet_owner, subgrid_pos):
    gains, resid, phase_across, phase_down = solve(
        model, visibilities, pairs, held_gains[0], solver_owner, uv
    )
    facets, gains = local_facets(
        gains, resid, phase_across, phase_down, facet_owner, subgrid_pos
    )
    facet = collect(facets)
    facet = facet.reshape(FACET, 2, FACET).transpose(1, 0, 2)
    return (gains.reshape(INTERVALS, 2, DIRS, STATIONS), facet[None, None])


def solution(mesh):
    placed = (
        P(None, None, "freq", "bl"),
        P(None, None, None, "freq", "bl"),
        P(None, "bl", None),
        P(None, None, "bl"),
        P("bl", None, None, None, None),
        P(),
        P(None, "freq", "bl", None),
        P(None, "freq", "bl", None),
    )
    return jax.shard_map(
        body,
        mesh=mesh,
        in_specs=placed,
        out_specs=(P(), P("freq", "bl", None, None, None)),
        check_vma=False,
    )
```
